128 devices in a mesh: row: 8 (over y, core), col: 16 (over x, z).
Axes of the slice: x: 4, y: 4, z: 4, core: 2. Of those that a mesh axis runs over, the one named last changes fastest.
Arguments:
- object_field: float32 [2, 4096, 8192], P(None, 'row', 'col'), may hold values from -6 to 6
- probe: float32 [4, 2, 256, 256], replicated, may hold values from -4 to 4
- amplitudes: bfloat16 [512, 256, 256], P(('row', 'col')), may hold values from 0 to 2
- owner: int32 [512], P(('row', 'col')), may hold values from 0 to 15, as said below
- offsets: int32 [512, 2], P(('row', 'col')), may hold values from 0 to 511
Outputs:
- object_out: float32 [2, 4096, 8192], P(None, 'row', 'col')
- probe_gradient: float32 [4, 2, 256, 256], replicated
The draws below stay inside these ranges and needn't reach their ends.
Inputs may be any that keep to these rules, and one draw needn't show every extreme that they name: owner[p] is a tile column of the same tile row as the device holding p. The patterns of one device that share an owner number at most 1, and on every device some owner receives exactly 1 of them. Every tile comes to own either exactly 12 patterns or one or two.
All inputs are finite; a program needn't handle non-finite values.
Results may differ from the reference program's by a relative error of at most 0.0024.
Values may be sent and summed in bfloat16 or wider, within the bound.
A program may use at most 128 MiB of HBM per device.

```python
import math
import jax
import jax.numpy as jnp
from jax import lax

PAT = 256
MODES = 4
TILE = 512
P_DEV = 4
TILE_ROWS = 8
TILE_COLS = 16
HEIGHT = 4096
WIDTH = 8192
TOTAL = 512


def draw_owner(key, part):
    key = jax.random.fold_in(key, 7)
    across_count = TILE_COLS
    quarter = across_count // 4

    def one_row(row_key):
        key_one, key_two, key_three, key_four = jax.random.split(row_key, 4)
        order_all = jax.random.permutation(key_one, across_count)
        group_of = jax.random.permutation(key_two, across_count) // 4
        spread_of = jax.random.permutation(key_three, across_count) % (across_count - quarter)
        shift_steps = jnp.arange(1, P_DEV)
        heavy = order_all[(group_of[:, None] + shift_steps[None, :]) % quarter]
        light = order_all[quarter + spread_of]
        table = jnp.concatenate([light[:, None], heavy], axis=1)
        slot_keys = jax.random.split(key_four, across_count)
        slot_order = jax.vmap(lambda slot_key: jax.random.permutation(slot_key, P_DEV))(slot_keys)
        return jnp.take_along_axis(table, slot_order, axis=1)
    tables = jax.vmap(one_row)(jax.random.split(key, TILE_ROWS))
    return tables.reshape(-1).astype(jnp.int32)


def touch_ends(array, key, low, largest):
    longest = array.shape.index(max(array.shape))
    spots = []
    for shift in (0, 1):
        where = [jax.random.randint(jax.random.fold_in(key, axis), (), 0, length) for axis, length in enumerate(array.shape)]
        where[longest] = (where[longest] + shift) % array.shape[longest]
        spots.append(tuple(where))
    return array.at[spots[0]].set(low).at[spots[1]].set(largest)


def steps_of(rng, dims, pieces, least, top_value):
    factor_of, own = 1.0, jax.random.fold_in(rng, 6)
    for axis_at, blocks in pieces:
        heights = jnp.exp(jax.random.uniform(jax.random.fold_in(own, axis_at), (blocks,), jnp.float32, least / len(pieces), top_value / len(pieces)))
        factor_of = factor_of * jnp.repeat(heights, dims[axis_at] // blocks).reshape([-1 if axis == axis_at else 1 for axis in range(len(dims))])
    return factor_of


def normal_values(key, dims, deviation, bound, cuts=(), held_as=jnp.bfloat16):
    entries = deviation * jax.random.normal(key, dims, jnp.float32)
    if cuts:
        entries = entries * steps_of(key, dims, cuts, -0.22, 0.18)
    return jnp.clip(entries, -bound, bound).astype(held_as)


def setup_inputs(seed: int = 0) -> dict:
    key_of = jax.random.split(jax.random.key(seed), 6)
    object_field = normal_values(key_of[0], (2, HEIGHT, WIDTH), 0.7, 6.0, ((1, 8), (2, 16)), jnp.float32)
    probe = normal_values(key_of[1], (MODES, 2, PAT, PAT), 0.5, 4.0, (), jnp.float32)
    amplitudes = jnp.clip(2.0 * jax.random.uniform(key_of[2], (TOTAL, PAT, PAT), jnp.float32) ** steps_of(key_of[2], (TOTAL, PAT, PAT), ((0, 128),), -0.2, 0.2), 0.0, 2.0).astype(jnp.bfloat16)
    owner = draw_owner(jax.random.fold_in(key_of[5], 71), 0)
    offsets = touch_ends(jax.random.randint(key_of[4], (TOTAL, 2), 0, TILE), jax.random.fold_in(key_of[4], 1), 0, TILE - 1).astype(jnp.int32)
    return dict(object_field=object_field, probe=probe, amplitudes=amplitudes, owner=owner, offsets=offsets)


def dft_tables(side_length):
    series = jnp.arange(side_length, dtype=jnp.int32)
    product = series[:, None] * series[None, :] % side_length
    angles = product.astype(jnp.float32) * (2.0 * math.pi / side_length)
    factor = 1.0 / math.sqrt(side_length)
    table_re = (jnp.cos(angles) * factor).astype(jnp.bfloat16)
    table_im = (-jnp.sin(angles) * factor).astype(jnp.bfloat16)
    return (table_re, table_im)

def left_pass(table_re, table_im, field_re, field_im):

    def multiply(table, field):
        return jnp.einsum('jk,mkl->mjl', table.astype(jnp.float32), field.astype(jnp.float32))
    real_part = multiply(table_re, field_re) - multiply(table_im, field_im)
    imag_part = multiply(table_re, field_im) + multiply(table_im, field_re)
    return (real_part, imag_part)

def right_pass(field_re, field_im, table_re, table_im):

    def multiply(field, table):
        return jnp.einsum('mjk,kl->mjl', field.astype(jnp.float32), table.astype(jnp.float32))
    real_part = multiply(field_re, table_re) - multiply(field_im, table_im)
    imag_part = multiply(field_im, table_re) + multiply(field_re, table_im)
    return (real_part, imag_part)

def pattern_terms(patch, probe, amp_one, table_re, table_im):
    probe_re = probe[:, 0]
    probe_im = probe[:, 1]
    patch_re = patch[0]
    patch_im = patch[1]
    exit_re = probe_re * patch_re - probe_im * patch_im
    exit_im = probe_re * patch_im + probe_im * patch_re
    half_re, half_im = left_pass(table_re, table_im, exit_re.astype(jnp.bfloat16), exit_im.astype(jnp.bfloat16))
    far_re, far_im = right_pass(half_re.astype(jnp.bfloat16), half_im.astype(jnp.bfloat16), table_re, table_im)
    model = jnp.sqrt(lax.optimization_barrier(jnp.sum(far_re * far_re + far_im * far_im, axis=0)))
    ratio = amp_one.astype(jnp.float32) / jnp.maximum(model, 0.5)
    repl_re = (far_re * ratio).astype(jnp.bfloat16)
    repl_im = (far_im * ratio).astype(jnp.bfloat16)
    conj_im = -table_im
    back_re, back_im = left_pass(table_re, conj_im, repl_re, repl_im)
    ret_re, ret_im = right_pass(back_re.astype(jnp.bfloat16), back_im.astype(jnp.bfloat16), table_re, conj_im)
    change_re = ret_re - exit_re
    change_im = ret_im - exit_im
    numer_one = jnp.stack([lax.optimization_barrier(jnp.sum(probe_re * change_re + probe_im * change_im, axis=0)), lax.optimization_barrier(jnp.sum(probe_re * change_im - probe_im * change_re, axis=0))])
    grad_one = jnp.stack([patch_re * change_re + patch_im * change_im, patch_re * change_im - patch_im * change_re], axis=1)
    return (numer_one, grad_one)

def reference(object_field, probe, amplitudes, owner, offsets):
    half_width = PAT // 2
    table_re, table_im = dft_tables(PAT)
    padded = jnp.pad(object_field, ((0, 0), (half_width, half_width), (half_width, half_width)))
    source_row = jnp.arange(TOTAL, dtype=jnp.int32) // P_DEV // TILE_COLS
    start_row = (source_row * TILE + offsets[:, 0]).astype(jnp.int32)
    start_col = (owner * TILE + offsets[:, 1]).astype(jnp.int32)
    power = lax.optimization_barrier(jnp.sum(probe[:, 0] * probe[:, 0] + probe[:, 1] * probe[:, 1], axis=0))
    zero_index = jnp.zeros((), jnp.int32)

    def visit(carry, item):
        numer, weight, gradient = carry
        amp_one, row_at, col_at = item
        corner = (zero_index, row_at, col_at)
        patch = lax.dynamic_slice(padded, corner, (2, PAT, PAT))
        numer_one, grad_one = pattern_terms(patch, probe, amp_one, table_re, table_im)
        current = lax.dynamic_slice(numer, corner, (2, PAT, PAT))
        numer = lax.dynamic_update_slice(numer, current + numer_one, corner)
        weight_now = lax.dynamic_slice(weight, (row_at, col_at), (PAT, PAT))
        weight = lax.dynamic_update_slice(weight, weight_now + power, (row_at, col_at))
        return ((numer, weight, gradient + grad_one), None)
    start = (jnp.zeros(padded.shape, jnp.float32), jnp.zeros(padded.shape[1:], jnp.float32), jnp.zeros(probe.shape, jnp.float32))
    (numer, weight, gradient), skipped = lax.scan(visit, start, (amplitudes, start_row, start_col))
    numer_core = numer[:, half_width:half_width + HEIGHT, half_width:half_width + WIDTH]
    weight_core = weight[half_width:half_width + HEIGHT, half_width:half_width + WIDTH]
    object_out = object_field + numer_core / (weight_core + 1.0)
    probe_gradient = gradient * (1.0 / math.sqrt(TOTAL))
    return (object_out, probe_gradient)
```

```python
import functools
import math

import jax
import jax.numpy as jnp
import numpy as np
from jax import lax
from jax.experimental import pallas as pl
from jax.experimental.pallas import tpu as pltpu
from jax.sharding import PartitionSpec as P

F32, BF16 = jnp.float32, jnp.bfloat16

def tables(side):
    series = np.arange(side, dtype=np.int32)
    angles = (series[:, None] * series[None, :] % side).astype(np.float32) * np.float32(2.0 * math.pi / side)
    factor = np.float32(1.0 / math.sqrt(side))
    re = jnp.asarray(np.cos(angles) * factor).astype(BF16)
    im = jnp.asarray(-np.sin(angles) * factor).astype(BF16)
    return re, im

def dot(a, b):
    return jnp.dot(a, b, preferred_element_type=F32)

def kernel(slots, modes, side, det_ref, ext_ref, probe_ref, amp_ref, tab_ref,
           num_ref, wgt_ref, grad_ref,
           patch, ebuf, hbuf, far, pow_ref, ssum, nbuf):
    wide, tall = side + 128, side + 8
    num_ref[...] = jnp.zeros_like(num_ref)
    wgt_ref[...] = jnp.zeros_like(wgt_ref)
    grad_ref[...] = jnp.zeros_like(grad_ref)
    ssum[...] = jnp.zeros_like(ssum)
    power = jnp.zeros((side, side), F32)
    for m in range(modes):
        power += probe_ref[m, 0] * probe_ref[m, 0] + probe_ref[m, 1] * probe_ref[m, 1]
    pow_ref[...] = jnp.zeros_like(pow_ref)
    pow_ref[:side, :side] = power
    nbuf[...] = jnp.zeros_like(nbuf)

    def visit(s, carry):
        @pl.when(det_ref[s, 0] == 1)
        def _():
            r = det_ref[s, 1]
            c = det_ref[s, 2]
            c0 = pl.multiple_of((c // 128) * 128, 128)
            cc = c - c0
            r0 = pl.multiple_of((r // 8) * 8, 8)
            rr0 = r - r0
            for q in range(2):
                w = ext_ref[q, pl.ds(r0, tall), pl.ds(c0, wide)]
                w = pltpu.roll(w, wide - cc, 1)[:, :side]
                patch[q] = pltpu.roll(w, tall - rr0, 0)[:side]
            ssum[...] += patch[0] * patch[0] + patch[1] * patch[1]
            for m in range(modes):
                pr, pi = probe_ref[m, 0], probe_ref[m, 1]
                xr, xi = patch[0], patch[1]
                ebuf[m, :side] = (pr * xr - pi * xi).astype(BF16)
                ebuf[m, side:] = (pr * xi + pi * xr).astype(BF16)
                half = dot(tab_ref[0], ebuf[m])
                hbuf[m, :, :side] = half[:side].astype(BF16)
                hbuf[m, :, side:] = half[side:].astype(BF16)
                far[m] = dot(hbuf[m], tab_ref[1])
            tot = jnp.zeros((side, side), F32)
            for m in range(modes):
                fr, fi = far[m, :, :side], far[m, :, side:]
                tot += fr * fr + fi * fi
            ratio = amp_ref[s].astype(F32) * lax.rsqrt(jnp.maximum(tot, 0.25))
            xr, xi = patch[0], patch[1]
            nbuf[:, :side, :side] = jnp.zeros((2, side, side), F32)
            for m in range(modes):
                ebuf[m, :side] = (far[m, :, :side] * ratio).astype(BF16)
                ebuf[m, side:] = (far[m, :, side:] * ratio).astype(BF16)
                half = dot(tab_ref[2], ebuf[m])
                hbuf[m, :, :side] = half[:side].astype(BF16)
                hbuf[m, :, side:] = half[side:].astype(BF16)
                ret = dot(hbuf[m], tab_ref[3])
                rr, ri = ret[:, :side], ret[:, side:]
                pr, pi = probe_ref[m, 0], probe_ref[m, 1]
                nbuf[0, :side, :side] += pr * rr + pi * ri
                nbuf[1, :side, :side] += pr * ri - pi * rr
                grad_ref[m, 0] += xr * rr + xi * ri
                grad_ref[m, 1] += xr * ri - xi * rr
            for q in range(2):
                num_ref[q, pl.ds(r0, tall), pl.ds(c0, wide)] += pltpu.roll(pltpu.roll(nbuf[q], rr0, 0), cc, 1)
            wgt_ref[pl.ds(r0, tall), pl.ds(c0, wide)] += pltpu.roll(pltpu.roll(pow_ref[...], rr0, 0), cc, 1)
        return carry
    lax.fori_loop(0, slots, visit, 0)
    for m in range(modes):
        for q in range(2):
            grad_ref[m, q] -= probe_ref[m, q] * ssum[...]

def pattern_call(det, ext, probe, amp):
    slots, side = amp.shape[0], amp.shape[1]
    modes = probe.shape[0]
    tr, ti = tables(side)
    def left(a, b):
        return jnp.concatenate([jnp.concatenate([a, -b], 1), jnp.concatenate([b, a], 1)], 0)
    def right(a, b):
        return jnp.concatenate([jnp.concatenate([a, b], 1), jnp.concatenate([-b, a], 1)], 0)
    tab = jnp.stack([left(tr, ti), right(tr, ti), left(tr, -ti), right(tr, -ti)])
    V = pl.BlockSpec(memory_space=pltpu.VMEM)
    S = pl.BlockSpec(memory_space=pltpu.SMEM)
    big = ext.shape[1]
    return pl.pallas_call(
        functools.partial(kernel, slots, modes, side),
        out_shape=[jax.ShapeDtypeStruct(ext.shape, F32), jax.ShapeDtypeStruct(ext.shape[1:], F32), jax.ShapeDtypeStruct(probe.shape, F32)],
        in_specs=[S, V, V, V, V], out_specs=[V, V, V],
        scratch_shapes=[
            pltpu.VMEM((2, side, side), F32),
            pltpu.VMEM((modes, 2 * side, side), BF16),
            pltpu.VMEM((modes, side, 2 * side), BF16),
            pltpu.VMEM((modes, side, 2 * side), F32),
            pltpu.VMEM((side + 8, side + 128), F32),
            pltpu.VMEM((side, side), F32),
            pltpu.VMEM((2, side + 8, side + 128), F32),
        ],
        compiler_params=pltpu.CompilerParams(vmem_limit_bytes=56 * 2**20),
        name="patterns",
    )(det, ext, probe, amp, tab)


def shifted(value, axis, by):
    size = lax.axis_size(axis)
    pairs = [(i, i + by) for i in range(size) if 0 <= i + by < size]
    return lax.ppermute(value, axis, pairs)


def padded(cells, sides, width):
    for axis, dim in sides:
        count = lax.axis_size(axis)
        ends = count - 1
        head = lax.slice_in_dim(cells, 0, width, axis=dim)
        tail = lax.slice_in_dim(cells, cells.shape[dim] - width, cells.shape[dim], axis=dim)
        cells = jnp.concatenate(
            [
                lax.ppermute(tail, axis, [(i, (i + 1) % count) for i in range(ends)]),
                cells,
                lax.ppermute(head, axis, [((i + 1) % count, i) for i in range(ends)]),
            ],
            axis=dim,
        )
    return cells


def pass_rows(numer_rim, weight_rim, offset_by):
    return shifted((numer_rim, weight_rim), "row", offset_by)


def pass_cols(numer_rim, weight_rim, offset_by):
    return shifted((numer_rim, weight_rim), "col", offset_by)


def settle(numer, weight, tile_side, half_width):
    pattern_side = 2 * half_width
    from_below = pass_rows(numer[:, :half_width], weight[:half_width], -1)
    from_above = pass_rows(numer[:, tile_side + half_width :], weight[tile_side + half_width :], 1)
    numer = numer.at[:, tile_side : tile_side + half_width].add(from_below[0])
    numer = numer.at[:, half_width:pattern_side].add(from_above[0])
    weight = weight.at[tile_side : tile_side + half_width].add(from_below[1])
    weight = weight.at[half_width:pattern_side].add(from_above[1])
    numer = numer[:, half_width : half_width + tile_side]
    weight = weight[half_width : half_width + tile_side]
    from_right = pass_cols(numer[:, :, :half_width], weight[:, :half_width], -1)
    from_left = pass_cols(
        numer[:, :, tile_side + half_width :], weight[:, tile_side + half_width :], 1
    )
    numer = numer.at[:, :, tile_side : tile_side + half_width].add(from_right[0])
    numer = numer.at[:, :, half_width:pattern_side].add(from_left[0])
    weight = weight.at[:, tile_side : tile_side + half_width].add(from_right[1])
    weight = weight.at[:, half_width:pattern_side].add(from_left[1])
    return (
        numer[:, :, half_width : half_width + tile_side],
        weight[:, half_width : half_width + tile_side],
    )


def on_device(object_field, probe, amplitudes, owner, offsets):
    tile_across = lax.axis_size("col")
    held_count = amplitudes.shape[0]
    total_count = lax.axis_size("row") * tile_across * held_count
    tile_side = object_field.shape[1]
    pattern_side = probe.shape[-1]
    half_width = pattern_side // 2
    quarter = tile_across // 4
    capacity = (held_count - 2) // quarter + 1
    slots_all = tile_across * capacity
    extended = padded(object_field, (("row", 1), ("col", 2)), half_width)
    series_held = jnp.arange(held_count, dtype=jnp.int32)
    same_owner = owner[:, None] == owner[None, :]
    earlier = series_held[None, :] < series_held[:, None]
    rank_held = jnp.sum((same_owner & earlier).astype(jnp.int32), axis=1)
    target_slot = owner * capacity + rank_held
    select = target_slot[None, :] == jnp.arange(slots_all, dtype=jnp.int32)[:, None]
    details = jnp.stack([jnp.ones((held_count,), jnp.int32), offsets[:, 0], offsets[:, 1]], axis=1)
    send_details = jnp.sum(select[:, :, None].astype(jnp.int32) * details[None], axis=1)
    flat_amp = amplitudes.reshape(held_count, pattern_side * pattern_side)
    send_amp = jnp.dot(
        select.astype(jnp.bfloat16), flat_amp, preferred_element_type=jnp.float32
    ).astype(jnp.bfloat16)
    got_amp, got_details = (
        lax.all_to_all(send_amp, "col", split_axis=0, concat_axis=0, tiled=True),
        lax.all_to_all(send_details, "col", split_axis=0, concat_axis=0, tiled=True),
    )
    got_amp = got_amp.reshape(slots_all, pattern_side, pattern_side)
    numer, weight, gradient = pattern_call(got_details, extended, probe, got_amp)
    numer_core, weight_core = settle(numer, weight, tile_side, half_width)
    object_out = (object_field + numer_core) / (weight_core + 1.0)
    gradient_total = lax.psum(gradient, ("row", "col"))
    probe_gradient = gradient_total * (1.0 / math.sqrt(total_count))
    return (object_out, probe_gradient)


def solution(mesh):
    return jax.shard_map(
        on_device,
        mesh=mesh,
        in_specs=(
            P(None, "row", "col"),
            P(),
            P(("row", "col"), None, None),
            P(("row", "col")),
            P(("row", "col"), None),
        ),
        out_specs=(P(None, "row", "col"), P()),
        check_vma=False,
    )
```

```python
import functools
import math

import jax
import jax.numpy as jnp
import numpy as np
from jax import lax
from jax.experimental import pallas as pl
from jax.experimental.pallas import tpu as pltpu
from jax.sharding import PartitionSpec as P

F32, BF16 = jnp.float32, jnp.bfloat16
MESH = pl.DeviceIdType.MESH

def tables(side):
    series = np.arange(side, dtype=np.int32)
    angles = (series[:, None] * series[None, :] % side).astype(np.float32) * np.float32(2.0 * math.pi / side)
    factor = np.float32(1.0 / math.sqrt(side))
    re = jnp.asarray(np.cos(angles) * factor).astype(BF16)
    im = jnp.asarray(-np.sin(angles) * factor).astype(BF16)
    return re, im

def dot(a, b):
    return jnp.dot(a, b, preferred_element_type=F32)

def kernel(slots, modes, side, rows, cols, held, meta_ref, ext_hbm, probe_ref, amp_ref, tab_ref,
           rim_ref, core_ref, grad_ref,
           ext_ref, num_ref, esem, patch, ebuf, hbuf, far, pow_ref, ssum, nbuf):
    wide, tall = side + 128, side + 8
    row, col = lax.axis_index("row"), lax.axis_index("col")
    fetch = pltpu.make_async_copy(ext_hbm, ext_ref, esem)
    fetch.start()
    num_ref[...] = jnp.zeros_like(num_ref)
    grad_ref[...] = jnp.zeros_like(grad_ref)
    ssum[...] = jnp.zeros_like(ssum)
    power = jnp.zeros((side, side), F32)
    for m in range(modes):
        power += probe_ref[m, 0] * probe_ref[m, 0] + probe_ref[m, 1] * probe_ref[m, 1]
    pow_ref[...] = jnp.zeros_like(pow_ref)
    pow_ref[:side, :side] = power
    nbuf[...] = jnp.zeros_like(nbuf)

    fetch.wait()
    big, half = ext_ref.shape[1], side // 2

    @pl.when(row == 0)
    def _():
        ext_ref[:, :half, :] = jnp.zeros((2, half, big), F32)

    @pl.when(row == rows - 1)
    def _():
        ext_ref[:, big - half:, :] = jnp.zeros((2, half, big), F32)

    @pl.when(col == 0)
    def _():
        ext_ref[:, :, :half] = jnp.zeros((2, big, half), F32)

    @pl.when(col == cols - 1)
    def _():
        ext_ref[:, :, big - half:] = jnp.zeros((2, big, half), F32)

    def visit(s, carry):
        live, r, c = jnp.int32(0), jnp.int32(0), jnp.int32(0)
        for h in range(held):
            hit = meta_ref[s, 0, h] == col
            live = jnp.where(hit, 1, live)
            r = jnp.where(hit, meta_ref[s, 0, held + 2 * h], r)
            c = jnp.where(hit, meta_ref[s, 0, held + 2 * h + 1], c)

        @pl.when(live == 1)
        def _():
            c0 = pl.multiple_of((c // 128) * 128, 128)
            cc = c - c0
            r0 = pl.multiple_of((r // 8) * 8, 8)
            rr0 = r - r0
            for q in range(2):
                w = ext_ref[q, pl.ds(r0, tall), pl.ds(c0, wide)]
                w = pltpu.roll(w, wide - cc, 1)[:, :side]
                patch[q] = pltpu.roll(w, tall - rr0, 0)[:side]
            ssum[...] += patch[0] * patch[0] + patch[1] * patch[1]
            for m in range(modes):
                pr, pi = probe_ref[m, 0], probe_ref[m, 1]
                xr, xi = patch[0], patch[1]
                ebuf[m, :side] = (pr * xr - pi * xi).astype(BF16)
                ebuf[m, side:] = (pr * xi + pi * xr).astype(BF16)
                half = dot(tab_ref[0], ebuf[m])
                hbuf[m, :, :side] = half[:side].astype(BF16)
                hbuf[m, :, side:] = half[side:].astype(BF16)
                far[m] = dot(hbuf[m], tab_ref[1])
            tot = jnp.zeros((side, side), F32)
            for m in range(modes):
                fr, fi = far[m, :, :side], far[m, :, side:]
                tot += fr * fr + fi * fi
            ratio = amp_ref[s].astype(F32) * lax.rsqrt(jnp.maximum(tot, 0.25))
            xr, xi = patch[0], patch[1]
            nbuf[:, :side, :side] = jnp.zeros((2, side, side), F32)
            for m in range(modes):
                ebuf[m, :side] = (far[m, :, :side] * ratio).astype(BF16)
                ebuf[m, side:] = (far[m, :, side:] * ratio).astype(BF16)
                half = dot(tab_ref[2], ebuf[m])
                hbuf[m, :, :side] = half[:side].astype(BF16)
                hbuf[m, :, side:] = half[side:].astype(BF16)
                ret = dot(hbuf[m], tab_ref[3])
                rr, ri = ret[:, :side], ret[:, side:]
                pr, pi = probe_ref[m, 0], probe_ref[m, 1]
                nbuf[0, :side, :side] += pr * rr + pi * ri
                nbuf[1, :side, :side] += pr * ri - pi * rr
                grad_ref[pl.ds(2 * m * side, side)] += xr * rr + xi * ri
                grad_ref[pl.ds((2 * m + 1) * side, side)] += xr * ri - xi * rr
            for q in range(2):
                num_ref[q, pl.ds(r0, tall), pl.ds(c0, wide)] += pltpu.roll(pltpu.roll(nbuf[q], rr0, 0), cc, 1)
            num_ref[2, pl.ds(r0, tall), pl.ds(c0, wide)] += pltpu.roll(pltpu.roll(pow_ref[...], rr0, 0), cc, 1)
        return carry
    lax.fori_loop(0, slots, visit, 0)
    for m in range(modes):
        for q in range(2):
            grad_ref[pl.ds((2 * m + q) * side, side)] -= probe_ref[m, q] * ssum[...]
    wgt = num_ref[2]
    for q in range(2):
        num_ref[q] -= ext_ref[q] * wgt
    for q in range(3):
        rim_ref[q] = num_ref[q].astype(BF16)
        core_ref[q] = num_ref[q, half:big - half, half:big - half]

def pattern_call(meta, ext, probe, amp, rows, cols, held):
    slots, side = amp.shape[0], amp.shape[1]
    modes = probe.shape[0]
    tr, ti = tables(side)

    def left(a, b):
        return jnp.concatenate([jnp.concatenate([a, -b], 1), jnp.concatenate([b, a], 1)], 0)

    def right(a, b):
        return jnp.concatenate([jnp.concatenate([a, b], 1), jnp.concatenate([-b, a], 1)], 0)

    tab = jnp.stack([left(tr, ti), right(tr, ti), left(tr, -ti), right(tr, -ti)])
    V = pl.BlockSpec(memory_space=pltpu.VMEM)
    S = pl.BlockSpec(memory_space=pltpu.SMEM)
    A = pl.BlockSpec(memory_space=pl.ANY)
    big = ext.shape[1]
    core = big - side
    return pl.pallas_call(
        functools.partial(kernel, slots, modes, side, rows, cols, held),
        out_shape=[
            jax.ShapeDtypeStruct((3, big, big), BF16),
            jax.ShapeDtypeStruct((3, core, core), F32),
            jax.ShapeDtypeStruct((modes * 2 * side, side), F32),
        ],
        in_specs=[S, A, V, V, V],
        out_specs=[V, V, V],
        scratch_shapes=[
            pltpu.VMEM((2, big, big), F32),
            pltpu.VMEM((3, big, big), F32),
            pltpu.SemaphoreType.DMA,
            pltpu.VMEM((2, side, side), F32),
            pltpu.VMEM((modes, 2 * side, side), BF16),
            pltpu.VMEM((modes, side, 2 * side), BF16),
            pltpu.VMEM((modes, side, 2 * side), F32),
            pltpu.VMEM((side + 8, side + 128), F32),
            pltpu.VMEM((side, side), F32),
            pltpu.VMEM((2, side + 8, side + 128), F32),
        ],
        compiler_params=pltpu.CompilerParams(vmem_limit_bytes=56 * 2**20),
        name="patterns",
    )(meta, ext, probe, amp, tab)


def around(row, col, dr, dc, rows, cols):
    return lax.rem(row + dr + rows, rows), lax.rem(col + dc + cols, cols)


NEAR = [(dr, dc) for dr in (-1, 0, 1) for dc in (-1, 0, 1) if (dr, dc) != (0, 0)]


def span(step, tile, half):
    return {-1: (0, half), 0: (half, tile), 1: (half + tile, half)}[step]


def landing(step, tile, half):
    return {-1: (tile - half, half), 0: (0, tile), 1: (0, half)}[step]


class Sends:
    def __init__(self, send_sem, recv_sem):
        self.send_sem, self.recv_sem, self.at, self.all = send_sem, recv_sem, 0, []

    def __call__(self, src, dst, device):
        n = self.at
        self.at += 1
        copy = pltpu.make_async_remote_copy(
            src_ref=src, dst_ref=dst, send_sem=self.send_sem.at[n], recv_sem=self.recv_sem.at[n],
            device_id=device, device_id_type=MESH)
        copy.start()
        self.all.append(copy)
        return copy

    def finish(self):
        for copy in self.all:
            copy.wait_send()


def greet(devices):
    barrier = pltpu.get_barrier_semaphore()
    for device in devices:
        pl.semaphore_signal(barrier, inc=1, device_id=device, device_id_type=MESH)
    pl.semaphore_wait(barrier, len(devices))


def post_kernel(rows, cols, tile, half, scale, rim_ref, core_ref, obj_ref, grad_ref, out_ref, pg_ref,
                wsum, rims, mate, sum_a, sum_b, got_a, got_b, part_a, part_b, got_a2, got_b2, all16, gsend, grecv):
    row, col = lax.axis_index("row"), lax.axis_index("col")
    core, y = lax.rem(row, 2), row // 2
    ys = rows // 2
    other = (row + 1 - 2 * core, col)
    y_peers = [(lax.rem(y + s, ys) * 2 + core, col) for s in range(1, ys)]
    c_peers = [(row, lax.rem(col + s, cols)) for s in range(1, cols)]
    near = [around(row, col, dr, dc, rows, cols) for dr, dc in NEAR]
    greet([other] + y_peers + c_peers + near)
    send = Sends(gsend, grecv)
    n = grad_ref.shape[0] // 2
    na, nb = n // ys, n // cols
    fin = n // (ys * cols)
    theirs = pl.ds(pl.multiple_of((1 - core) * n, n), n)
    mine = pl.ds(pl.multiple_of(core * n, n), n)
    pair = send(grad_ref.at[theirs], mate, other)
    rim_copies = []
    for i, (dr, dc) in enumerate(NEAR):
        r0, rl = span(dr, tile, half)
        c0, cl = span(dc, tile, half)
        rim_copies.append(send(rim_ref.at[:, r0:r0 + rl, c0:c0 + cl], rims.at[i, :, 0:rl, 0:cl], near[i]))
    pair.wait_recv()
    h = grad_ref[mine, :] + mate[...]
    sum_a[...] = h[:, :128]
    sum_b[...] = h[:, 128:]
    y_at = [lax.rem(y + s, ys) for s in range(1, ys)]
    c_at = [lax.rem(col + s, cols) for s in range(1, cols)]

    def piece(k, size):
        return pl.ds(pl.multiple_of(k * size, size), size)

    a1 = [send(sum_a.at[piece(y_at[s], na)], got_a.at[s], y_peers[s]) for s in range(ys - 1)]
    b1 = [send(sum_b.at[piece(c_at[s], nb)], got_b.at[s], c_peers[s]) for s in range(cols - 1)]
    for c in a1:
        c.wait_recv()
    tot = sum_a[piece(y, na), :]
    for s in range(ys - 1):
        tot += got_a[s]
    part_a[...] = tot
    a2 = [send(part_a.at[piece(c_at[s], fin)], got_a2.at[s], c_peers[s]) for s in range(cols - 1)]
    for c in b1:
        c.wait_recv()
    tot = sum_b[piece(col, nb), :]
    for s in range(cols - 1):
        tot += got_b[s]
    part_b[...] = tot
    b2 = [send(part_b.at[piece(y_at[s], fin)], got_b2.at[s], y_peers[s]) for s in range(ys - 1)]
    for c in a2:
        c.wait_recv()
    tot = part_a[piece(col, fin), :]
    for s in range(cols - 1):
        tot += got_a2[s]
    at_a = piece(y * cols + col, fin)
    all16[core, 0, at_a, :] = (tot * scale).astype(all16.dtype)
    a3 = [send(all16.at[core, 0, at_a], all16.at[core, 0, at_a], p) for p in c_peers]
    for c in b2:
        c.wait_recv()
    tot = part_b[piece(y, fin), :]
    for s in range(ys - 1):
        tot += got_b2[s]
    at_b = piece(col * ys + y, fin)
    all16[core, 1, at_b, :] = (tot * scale).astype(all16.dtype)
    b3 = [send(all16.at[core, 1, at_b], all16.at[core, 1, at_b], p) for p in y_peers]
    for c in a3:
        c.wait_recv()
    big_a = piece(y, na)
    a4 = [send(all16.at[core, 0, big_a], all16.at[core, 0, big_a], p) for p in y_peers]
    for c in b3:
        c.wait_recv()
    big_b = piece(col, nb)
    b4 = [send(all16.at[core, 1, big_b], all16.at[core, 1, big_b], p) for p in c_peers]
    for c in rim_copies:
        c.wait_recv()
    out_ref[...] = core_ref[0:2]
    wsum[...] = core_ref[2]
    for i, (dr, dc) in enumerate(NEAR):
        r0, rl = landing(dr, tile, half)
        c0, cl = landing(dc, tile, half)
        keep = (row != -1) & (col != -1)
        if dr:
            keep = keep & (row != (0 if dr == 1 else rows - 1))
        if dc:
            keep = keep & (col != (0 if dc == 1 else cols - 1))

        @pl.when(keep)
        def _(i=i, r0=r0, rl=rl, c0=c0, cl=cl):
            for q in range(2):
                out_ref[q, r0:r0 + rl, c0:c0 + cl] += rims[i, q, 0:rl, 0:cl].astype(F32)
            wsum[r0:r0 + rl, c0:c0 + cl] += rims[i, 2, 0:rl, 0:cl].astype(F32)

    for q in range(2):
        out_ref[q] = obj_ref[q] + out_ref[q] / (wsum[...] + 1.0)
    for c in a4 + b4:
        c.wait_recv()
    last = send(all16.at[core], all16.at[core], other)
    for k in range(2):
        pg_ref[mine, 128 * k:128 * (k + 1)] = all16[core, k].astype(F32)
    last.wait_recv()
    for k in range(2):
        pg_ref[theirs, 128 * k:128 * (k + 1)] = all16[1 - core, k].astype(F32)
    send.finish()


def post_call(rim, core, obj, grad, rows, cols, scale):
    tile, wide = obj.shape[1], rim.shape[1]
    half = (wide - tile) // 2
    total = grad.shape[0]
    ys, n = rows // 2, total // 2
    na, nb, fin = n // ys, n // cols, n // (ys * cols)
    copies = 1 + 8 + 2 * (ys - 1) + 2 * (cols - 1) + 2 * (ys - 1) + 2 * (cols - 1) + 1
    V = pl.BlockSpec(memory_space=pltpu.VMEM)
    A = pl.BlockSpec(memory_space=pl.ANY)
    return pl.pallas_call(
        functools.partial(post_kernel, rows, cols, tile, half, scale),
        out_shape=[jax.ShapeDtypeStruct(obj.shape, F32), jax.ShapeDtypeStruct(grad.shape, F32)],
        in_specs=[A, V, V, V],
        out_specs=[V, V],
        scratch_shapes=[
            pltpu.VMEM((tile, tile), F32),
            pltpu.VMEM((8, 3, tile, tile), BF16),
            pltpu.VMEM((n, 256), F32),
            pltpu.VMEM((n, 128), F32),
            pltpu.VMEM((n, 128), F32),
            pltpu.VMEM((ys - 1, na, 128), F32),
            pltpu.VMEM((cols - 1, nb, 128), F32),
            pltpu.VMEM((na, 128), F32),
            pltpu.VMEM((nb, 128), F32),
            pltpu.VMEM((cols - 1, fin, 128), F32),
            pltpu.VMEM((ys - 1, fin, 128), F32),
            pltpu.VMEM((2, 2, n, 128), BF16),
            pltpu.SemaphoreType.DMA((copies,)),
            pltpu.SemaphoreType.DMA((copies,)),
        ],
        compiler_params=pltpu.CompilerParams(collective_id=1, has_side_effects=True, vmem_limit_bytes=56 * 2**20),
        name="post",
    )(rim, core, obj, grad)


def pre_kernel(rows, cols, tile, half, owner_ref, mine_ref, amp_ref, obj_ref, ext_ref, meta_ref, amps_ref,
               slots, gsend, grecv, lsem):
    row, col = lax.axis_index("row"), lax.axis_index("col")
    near = [around(row, col, dr, dc, rows, cols) for dr, dc in NEAR]
    c_peers = [(row, lax.rem(col + s, cols)) for s in range(1, cols)]
    held = amp_ref.shape[0]
    greet(c_peers + near)
    send = Sends(gsend, grecv)
    got = []
    for s in range(cols - 1):
        got.append(send(mine_ref, meta_ref.at[col], c_peers[s]))
    for i, (dr, dc) in enumerate(NEAR):
        r0, rl = {-1: (0, half), 0: (0, tile), 1: (tile - half, half)}[dr]
        c0, cl = {-1: (0, half), 0: (0, tile), 1: (tile - half, half)}[dc]
        tr, _ = span(-dr, tile, half)
        tc, _ = span(-dc, tile, half)
        got.append(send(obj_ref.at[:, r0:r0 + rl, c0:c0 + cl], ext_ref.at[:, tr:tr + rl, tc:tc + cl], near[i]))
    local = [
        pltpu.make_async_copy(obj_ref, ext_ref.at[:, half:half + tile, half:half + tile], lsem.at[0]),
        pltpu.make_async_copy(mine_ref, meta_ref.at[col], lsem.at[1]),
        pltpu.make_async_copy(slots.at[0], amps_ref.at[col], lsem.at[2]),
    ]
    local[0].start()
    local[1].start()
    for s in range(cols):
        to = lax.rem(col + s, cols)
        which = jnp.int32(0)
        for h in range(1, held):
            which = jnp.where(owner_ref[h] == to, h, which)
        slots[s] = amp_ref[which]
        if s == 0:
            local[2].start()
        else:
            got.append(send(slots.at[s], amps_ref.at[col], c_peers[s - 1]))
    for c in got:
        c.wait_recv()
    for c in local:
        c.wait()
    send.finish()


def pre_call(owner, mine, amp, obj, rows, cols):
    tile = obj.shape[1]
    half = amp.shape[1] // 2
    wide = tile + 2 * half
    copies = 8 + 2 * (cols - 1)
    V = pl.BlockSpec(memory_space=pltpu.VMEM)
    A = pl.BlockSpec(memory_space=pl.ANY)
    S = pl.BlockSpec(memory_space=pltpu.SMEM)
    return pl.pallas_call(
        functools.partial(pre_kernel, rows, cols, tile, half),
        out_shape=[
            jax.ShapeDtypeStruct((2, wide, wide), F32),
            jax.ShapeDtypeStruct((cols, 1, 128), jnp.int32),
            jax.ShapeDtypeStruct((cols,) + amp.shape[1:], BF16),
        ],
        in_specs=[S, V, V, A],
        out_specs=[A, A, A],
        scratch_shapes=[
            pltpu.VMEM((cols,) + amp.shape[1:], BF16),
            pltpu.SemaphoreType.DMA((copies,)),
            pltpu.SemaphoreType.DMA((copies,)),
            pltpu.SemaphoreType.DMA((3,)),
        ],
        compiler_params=pltpu.CompilerParams(collective_id=0, has_side_effects=True, vmem_limit_bytes=32 * 2**20),
        name="pre",
    )(owner, mine, amp, obj)


def on_device(object_field, probe, amplitudes, owner, offsets):
    rows, cols = lax.axis_size("row"), lax.axis_size("col")
    held = amplitudes.shape[0]
    mine = jnp.concatenate([owner, offsets.reshape(-1), jnp.zeros((128 - 3 * held,), jnp.int32)])[None]
    ext, meta, amps = pre_call(owner, mine, amplitudes, object_field, rows, cols)
    rim, core, grad = pattern_call(meta, ext, probe, amps, rows, cols, held)
    scale = 1.0 / math.sqrt(rows * cols * held)
    object_out, gradient = post_call(rim, core, object_field, grad, rows, cols, scale)
    return (object_out, gradient.reshape(probe.shape))


def solution(mesh):
    return jax.shard_map(
        on_device,
        mesh=mesh,
        in_specs=(
            P(None, "row", "col"),
            P(),
            P(("row", "col"), None, None),
            P(("row", "col")),
            P(("row", "col"), None),
        ),
        out_specs=(P(None, "row", "col"), P()),
        check_vma=False,
    )
```

```python
import functools
import math

import jax
import jax.numpy as jnp
import numpy as np
from jax import lax
from jax.experimental import pallas as pl
from jax.experimental.pallas import tpu as pltpu
from jax.sharding import PartitionSpec as P

F32, BF16 = jnp.float32, jnp.bfloat16
MESH = pl.DeviceIdType.MESH

def tables(side):
    series = np.arange(side, dtype=np.int32)
    angles = (series[:, None] * series[None, :] % side).astype(np.float32) * np.float32(2.0 * math.pi / side)
    factor = np.float32(1.0 / math.sqrt(side))
    re = jnp.asarray(np.cos(angles) * factor).astype(BF16)
    im = jnp.asarray(-np.sin(angles) * factor).astype(BF16)
    return re, im

def dot(a, b):
    return jnp.dot(a, b, preferred_element_type=F32)

def around(row, col, dr, dc, rows, cols):
    return lax.rem(row + dr + rows, rows), lax.rem(col + dc + cols, cols)


NEAR = [(dr, dc) for dr in (-1, 0, 1) for dc in (-1, 0, 1) if (dr, dc) != (0, 0)]


def span(step, tile, half):
    return {-1: (0, half), 0: (half, tile), 1: (half + tile, half)}[step]


def landing(step, tile, half):
    return {-1: (tile - half, half), 0: (0, tile), 1: (0, half)}[step]


class Sends:
    def __init__(self, send_sem, recv_sem):
        self.send_sem, self.recv_sem, self.at, self.all = send_sem, recv_sem, 0, []

    def __call__(self, src, dst, device):
        n = self.at
        self.at += 1
        copy = pltpu.make_async_remote_copy(
            src_ref=src, dst_ref=dst, send_sem=self.send_sem.at[n], recv_sem=self.recv_sem.at[n],
            device_id=device, device_id_type=MESH)
        copy.start()
        self.all.append(copy)
        return copy

    def finish(self):
        for copy in self.all:
            copy.wait_send()


def greet(devices):
    barrier = pltpu.get_barrier_semaphore()
    for device in devices:
        pl.semaphore_signal(barrier, inc=1, device_id=device, device_id_type=MESH)
    pl.semaphore_wait(barrier, len(devices))


def post_kernel(rows, cols, tile, half, scale, rim_ref, core_ref, obj_ref, grad_ref, out_ref, all16,
                wsum, rims, mate, sum_a, sum_b, got_a, got_b, part_a, part_b, got_a2, got_b2, gsend, grecv):
    row, col = lax.axis_index("row"), lax.axis_index("col")
    core, y = lax.rem(row, 2), row // 2
    ys = rows // 2
    other = (row + 1 - 2 * core, col)
    y_peers = [(lax.rem(y + s, ys) * 2 + core, col) for s in range(1, ys)]
    c_peers = [(row, lax.rem(col + s, cols)) for s in range(1, cols)]
    near = [around(row, col, dr, dc, rows, cols) for dr, dc in NEAR]
    greet([other] + y_peers + c_peers + near)
    send = Sends(gsend, grecv)
    n = grad_ref.shape[0] // 2
    na, nb = n // ys, n // cols
    fin = n // (ys * cols)
    theirs = pl.ds(pl.multiple_of((1 - core) * n, n), n)
    mine = pl.ds(pl.multiple_of(core * n, n), n)
    pair = send(grad_ref.at[theirs], mate, other)
    rim_copies = []
    for i, (dr, dc) in enumerate(NEAR):
        r0, rl = span(dr, tile, half)
        c0, cl = span(dc, tile, half)
        rim_copies.append(send(rim_ref.at[:, r0:r0 + rl, c0:c0 + cl], rims.at[i, :, 0:rl, 0:cl], near[i]))
    pair.wait_recv()
    h = grad_ref[mine, :] + mate[...]
    sum_a[...] = h[:, :128]
    sum_b[...] = h[:, 128:]
    y_at = [lax.rem(y + s, ys) for s in range(1, ys)]
    c_at = [lax.rem(col + s, cols) for s in range(1, cols)]

    def piece(k, size):
        return pl.ds(pl.multiple_of(k * size, size), size)

    a1 = [send(sum_a.at[piece(y_at[s], na)], got_a.at[s], y_peers[s]) for s in range(ys - 1)]
    b1 = [send(sum_b.at[piece(c_at[s], nb)], got_b.at[s], c_peers[s]) for s in range(cols - 1)]
    for c in a1:
        c.wait_recv()
    tot = sum_a[piece(y, na), :]
    for s in range(ys - 1):
        tot += got_a[s]
    part_a[...] = tot
    a2 = [send(part_a.at[piece(c_at[s], fin)], got_a2.at[s], c_peers[s]) for s in range(cols - 1)]
    for c in b1:
        c.wait_recv()
    tot = sum_b[piece(col, nb), :]
    for s in range(cols - 1):
        tot += got_b[s]
    part_b[...] = tot
    b2 = [send(part_b.at[piece(y_at[s], fin)], got_b2.at[s], y_peers[s]) for s in range(ys - 1)]
    for c in a2:
        c.wait_recv()
    tot = part_a[piece(col, fin), :]
    for s in range(cols - 1):
        tot += got_a2[s]
    at_a = piece(y * cols + col, fin)
    all16[core, 0, at_a, :] = (tot * scale).astype(all16.dtype)
    a3 = [send(all16.at[core, 0, at_a], all16.at[core, 0, at_a], p) for p in c_peers]
    for c in b2:
        c.wait_recv()
    tot = part_b[piece(y, fin), :]
    for s in range(ys - 1):
        tot += got_b2[s]
    at_b = piece(col * ys + y, fin)
    all16[core, 1, at_b, :] = (tot * scale).astype(all16.dtype)
    b3 = [send(all16.at[core, 1, at_b], all16.at[core, 1, at_b], p) for p in y_peers]
    for c in a3:
        c.wait_recv()
    big_a = piece(y, na)
    a4 = [send(all16.at[core, 0, big_a], all16.at[core, 0, big_a], p) for p in y_peers]
    for c in b3:
        c.wait_recv()
    big_b = piece(col, nb)
    b4 = [send(all16.at[core, 1, big_b], all16.at[core, 1, big_b], p) for p in c_peers]
    for c in rim_copies:
        c.wait_recv()
    out_ref[...] = core_ref[0:2]
    wsum[...] = core_ref[2]
    for i, (dr, dc) in enumerate(NEAR):
        r0, rl = landing(dr, tile, half)
        c0, cl = landing(dc, tile, half)
        keep = (row != -1) & (col != -1)
        if dr:
            keep = keep & (row != (0 if dr == 1 else rows - 1))
        if dc:
            keep = keep & (col != (0 if dc == 1 else cols - 1))

        @pl.when(keep)
        def _(i=i, r0=r0, rl=rl, c0=c0, cl=cl):
            for q in range(2):
                out_ref[q, r0:r0 + rl, c0:c0 + cl] += rims[i, q, 0:rl, 0:cl].astype(F32)
            wsum[r0:r0 + rl, c0:c0 + cl] += rims[i, 2, 0:rl, 0:cl].astype(F32)

    for q in range(2):
        out_ref[q] = obj_ref[q] + out_ref[q] / (wsum[...] + 1.0)
    for c in a4 + b4:
        c.wait_recv()
    last = send(all16.at[core], all16.at[core], other)
    last.wait_recv()
    send.finish()


def post_call(rim, core, obj, grad, rows, cols, scale):
    tile, wide = obj.shape[1], rim.shape[1]
    half = (wide - tile) // 2
    total = grad.shape[0]
    ys, n = rows // 2, total // 2
    na, nb, fin = n // ys, n // cols, n // (ys * cols)
    copies = 1 + 8 + 2 * (ys - 1) + 2 * (cols - 1) + 2 * (ys - 1) + 2 * (cols - 1) + 1
    V = pl.BlockSpec(memory_space=pltpu.VMEM)
    A = pl.BlockSpec(memory_space=pl.ANY)
    return pl.pallas_call(
        functools.partial(post_kernel, rows, cols, tile, half, scale),
        out_shape=[jax.ShapeDtypeStruct(obj.shape, F32), jax.ShapeDtypeStruct((2, 2, n, 128), BF16)],
        in_specs=[A, V, V, V],
        out_specs=[V, V],
        scratch_shapes=[
            pltpu.VMEM((tile, tile), F32),
            pltpu.VMEM((8, 3, tile, tile), BF16),
            pltpu.VMEM((n, 256), F32),
            pltpu.VMEM((n, 128), F32),
            pltpu.VMEM((n, 128), F32),
            pltpu.VMEM((ys - 1, na, 128), F32),
            pltpu.VMEM((cols - 1, nb, 128), F32),
            pltpu.VMEM((na, 128), F32),
            pltpu.VMEM((nb, 128), F32),
            pltpu.VMEM((cols - 1, fin, 128), F32),
            pltpu.VMEM((ys - 1, fin, 128), F32),
            pltpu.SemaphoreType.DMA((copies,)),
            pltpu.SemaphoreType.DMA((copies,)),
        ],
        compiler_params=pltpu.CompilerParams(collective_id=1, has_side_effects=True, vmem_limit_bytes=56 * 2**20),
        name="post",
    )(rim, core, obj, grad)


def pre_kernel(rows, cols, tile, half, owner_ref, offsets_ref, obj_ref, ext_ref, meta_ref, mine, gsend, grecv, lsem):
    row, col = lax.axis_index("row"), lax.axis_index("col")
    near = [around(row, col, dr, dc, rows, cols) for dr, dc in NEAR]
    c_peers = [(row, lax.rem(col + s, cols)) for s in range(1, cols)]
    held = owner_ref.shape[0]
    core = pltpu.make_async_copy(obj_ref, ext_ref.at[:, half:half + tile, half:half + tile], lsem.at[0])
    core.start()
    lane = lax.broadcasted_iota(jnp.int32, (1, 128), 1)
    note = jnp.zeros((1, 128), jnp.int32)
    for h in range(held):
        note = jnp.where(lane == h, owner_ref[h], note)
        for k in range(2):
            note = jnp.where(lane == held + 2 * h + k, offsets_ref[h, k], note)
    mine[...] = note
    greet(c_peers + near)
    send = Sends(gsend, grecv)
    got = []
    for i, (dr, dc) in enumerate(NEAR):
        r0, rl = {-1: (0, half), 0: (0, tile), 1: (tile - half, half)}[dr]
        c0, cl = {-1: (0, half), 0: (0, tile), 1: (tile - half, half)}[dc]
        tr, _ = span(-dr, tile, half)
        tc, _ = span(-dc, tile, half)
        got.append(send(obj_ref.at[:, r0:r0 + rl, c0:c0 + cl], ext_ref.at[:, tr:tr + rl, tc:tc + cl], near[i]))
    for s in range(cols - 1):
        got.append(send(mine, meta_ref.at[col], c_peers[s]))
    own = pltpu.make_async_copy(mine, meta_ref.at[col], lsem.at[1])
    own.start()
    for c in got:
        c.wait_recv()
    core.wait()
    own.wait()
    send.finish()


def pre_call(owner, offsets, obj, side, rows, cols):
    tile, half = obj.shape[1], side // 2
    big = tile + side
    copies = 8 + cols - 1
    A = pl.BlockSpec(memory_space=pl.ANY)
    S = pl.BlockSpec(memory_space=pltpu.SMEM)
    return pl.pallas_call(
        functools.partial(pre_kernel, rows, cols, tile, half),
        out_shape=[jax.ShapeDtypeStruct((2, big, big), F32), jax.ShapeDtypeStruct((cols, 1, 128), jnp.int32)],
        in_specs=[S, S, A],
        out_specs=[A, A],
        scratch_shapes=[
            pltpu.VMEM((1, 128), jnp.int32),
            pltpu.SemaphoreType.DMA((copies,)),
            pltpu.SemaphoreType.DMA((copies,)),
            pltpu.SemaphoreType.DMA((2,)),
        ],
        compiler_params=pltpu.CompilerParams(collective_id=0, has_side_effects=True),
        name="pre",
    )(owner, offsets, obj)


def cut_kernel(rows, cols, tile, half, held, meta_ref, ext_hbm, patch_hbm, list_ref, ext, patch, esem, osem):
    row, col = lax.axis_index("row"), lax.axis_index("col")
    side = 2 * half
    big, tall, wide, most = tile + side, side + 8, side + 128, list_ref.shape[0]
    fetch = pltpu.make_async_copy(ext_hbm, ext, esem)
    fetch.start()

    def clear(p, carry):
        for k in range(4):
            list_ref[p, k] = 0
        return carry

    lax.fori_loop(0, most, clear, 0)

    def scan(s, count):
        live, r, c = jnp.int32(0), jnp.int32(0), jnp.int32(0)
        for h in range(held):
            hit = meta_ref[s, 0, h] == col
            live = jnp.where(hit, 1, live)
            r = jnp.where(hit, meta_ref[s, 0, held + 2 * h], r)
            c = jnp.where(hit, meta_ref[s, 0, held + 2 * h + 1], c)

        @pl.when((live == 1) & (count < most))
        def _():
            list_ref[count, 0] = 1
            list_ref[count, 1] = s
            list_ref[count, 2] = r
            list_ref[count, 3] = c
        return count + live

    lax.fori_loop(0, cols, scan, 0)
    fetch.wait()

    @pl.when(row == 0)
    def _():
        ext[:, :half, :] = jnp.zeros((2, half, big), F32)

    @pl.when(row == rows - 1)
    def _():
        ext[:, big - half:, :] = jnp.zeros((2, half, big), F32)

    @pl.when(col == 0)
    def _():
        ext[:, :, :half] = jnp.zeros((2, big, half), F32)

    @pl.when(col == cols - 1)
    def _():
        ext[:, :, big - half:] = jnp.zeros((2, big, half), F32)

    def out(p):
        return pltpu.make_async_copy(patch.at[p], patch_hbm.at[p], osem.at[p])

    def visit(p, carry):
        @pl.when(list_ref[p, 0] == 1)
        def _():
            r, c = list_ref[p, 2], list_ref[p, 3]
            c0 = pl.multiple_of((c // 128) * 128, 128)
            r0 = pl.multiple_of((r // 8) * 8, 8)
            for q in range(2):
                w = ext[q, pl.ds(r0, tall), pl.ds(c0, wide)]
                w = pltpu.roll(w, wide - (c - c0), 1)[:, :side]
                patch[p, q] = pltpu.roll(w, tall - (r - r0), 0)[:side]

        @pl.when(list_ref[p, 0] == 0)
        def _():
            patch[p] = jnp.zeros((2, side, side), F32)

        out(p).start()
        return carry

    lax.fori_loop(0, most, visit, 0)

    def drain(p, carry):
        out(p).wait()
        return carry

    lax.fori_loop(0, most, drain, 0)


def cut_call(meta, ext, tile, rows, cols, held, most):
    big = ext.shape[1]
    side = big - tile
    A = pl.BlockSpec(memory_space=pl.ANY)
    S = pl.BlockSpec(memory_space=pltpu.SMEM)
    return pl.pallas_call(
        functools.partial(cut_kernel, rows, cols, tile, side // 2, held),
        out_shape=[jax.ShapeDtypeStruct((most, 2, side, side), F32), jax.ShapeDtypeStruct((most, 4), jnp.int32)],
        in_specs=[S, A],
        out_specs=[A, S],
        scratch_shapes=[
            pltpu.VMEM((2, big, big), F32),
            pltpu.VMEM((most, 2, side, side), F32),
            pltpu.SemaphoreType.DMA,
            pltpu.SemaphoreType.DMA((most,)),
        ],
        compiler_params=pltpu.CompilerParams(vmem_limit_bytes=32 * 2**20),
        name="cut",
    )(meta, ext)


def main_kernel(rows, cols, list_ref, owner_ref, amp_hbm, patch_hbm, probe_hbm, tab_hbm,
                placed_ref, grad_ref, pow_ref,
                slots, amps, amp, probe, tab, patch, far, total, ebuf, hbuf, ssum,
                gsend, grecv, lsem):
    row, col = lax.axis_index("row"), lax.axis_index("col")
    c_peers = [(row, lax.rem(col + s, cols)) for s in range(1, cols)]
    held, side, modes, most = amp.shape[0], amp.shape[1], probe.shape[0], patch.shape[0]
    local = [
        pltpu.make_async_copy(amp_hbm, amp, lsem.at[0]),
        pltpu.make_async_copy(probe_hbm, probe, lsem.at[1]),
        pltpu.make_async_copy(tab_hbm, tab, lsem.at[2]),
        pltpu.make_async_copy(patch_hbm, patch, lsem.at[3]),
    ]
    for copy in local:
        copy.start()
    greet(c_peers)
    send = Sends(gsend, grecv)
    local[0].wait()
    amp_copies = []
    for s in range(cols):
        to = lax.rem(col + s, cols)
        which = jnp.int32(0)
        for h in range(1, held):
            which = jnp.where(owner_ref[h] == to, h, which)
        if s == 0:
            amps[col] = amp[which]
        else:
            slots[s] = amp[which]
            amp_copies.append(send(slots.at[s], amps.at[col], c_peers[s - 1]))
    local[1].wait()
    power = jnp.zeros((side, side), F32)
    for m in range(modes):
        power += probe[m, 0] * probe[m, 0] + probe[m, 1] * probe[m, 1]
    pow_ref[...] = power
    grad_ref[...] = jnp.zeros_like(grad_ref)
    ssum[...] = jnp.zeros_like(ssum)
    local[2].wait()
    local[3].wait()

    def there(p, carry):
        ssum[...] += patch[p, 0] * patch[p, 0] + patch[p, 1] * patch[p, 1]
        for m in range(modes):
            pr, pi = probe[m, 0], probe[m, 1]
            xr, xi = patch[p, 0], patch[p, 1]
            ebuf[m, :side] = (pr * xr - pi * xi).astype(BF16)
            ebuf[m, side:] = (pr * xi + pi * xr).astype(BF16)
            part = dot(tab[0], ebuf[m])
            hbuf[m, :, :side] = part[:side].astype(BF16)
            hbuf[m, :, side:] = part[side:].astype(BF16)
            far[p, m] = dot(hbuf[m], tab[1])
        return carry

    lax.fori_loop(0, most, there, 0)
    for copy in amp_copies:
        copy.wait_recv()

    def back(p, carry):
        slot = list_ref[p, 1]
        tot = jnp.zeros((side, side), F32)
        for m in range(modes):
            fr, fi = far[p, m, :, :side], far[p, m, :, side:]
            tot += fr * fr + fi * fi
        total[...] = amps[slot].astype(F32) * lax.rsqrt(jnp.maximum(tot, 0.25))
        for m in range(modes):
            ratio = total[...]
            ebuf[m, :side] = (far[p, m, :, :side] * ratio).astype(BF16)
            ebuf[m, side:] = (far[p, m, :, side:] * ratio).astype(BF16)
            part = dot(tab[2], ebuf[m])
            hbuf[m, :, :side] = part[:side].astype(BF16)
            hbuf[m, :, side:] = part[side:].astype(BF16)
            ret = dot(hbuf[m], tab[3])
            rr, ri = ret[:, :side], ret[:, side:]
            pr, pi = probe[m, 0], probe[m, 1]
            xr, xi = patch[p, 0], patch[p, 1]
            if m == 0:
                placed_ref[p, 0] = pr * rr + pi * ri - xr * pow_ref[...]
                placed_ref[p, 1] = pr * ri - pi * rr - xi * pow_ref[...]
            else:
                placed_ref[p, 0] += pr * rr + pi * ri
                placed_ref[p, 1] += pr * ri - pi * rr
            grad_ref[2 * m * side:(2 * m + 1) * side] += xr * rr + xi * ri
            grad_ref[(2 * m + 1) * side:(2 * m + 2) * side] += xr * ri - xi * rr
        return carry

    lax.fori_loop(0, most, back, 0)
    for m in range(modes):
        for q in range(2):
            grad_ref[(2 * m + q) * side:(2 * m + q + 1) * side] -= probe[m, q] * ssum[...]
    send.finish()


def main_call(items, owner, amp, patch, probe, rows, cols):
    side, modes, most = amp.shape[1], probe.shape[0], patch.shape[0]
    copies = cols - 1
    tr, ti = tables(side)

    def left(a, b):
        return jnp.concatenate([jnp.concatenate([a, -b], 1), jnp.concatenate([b, a], 1)], 0)

    def right(a, b):
        return jnp.concatenate([jnp.concatenate([a, b], 1), jnp.concatenate([-b, a], 1)], 0)

    tab = jnp.stack([left(tr, ti), right(tr, ti), left(tr, -ti), right(tr, -ti)])
    V = pl.BlockSpec(memory_space=pltpu.VMEM)
    A = pl.BlockSpec(memory_space=pl.ANY)
    S = pl.BlockSpec(memory_space=pltpu.SMEM)
    return pl.pallas_call(
        functools.partial(main_kernel, rows, cols),
        out_shape=[
            jax.ShapeDtypeStruct((most, 2, side, side), F32),
            jax.ShapeDtypeStruct((modes * 2 * side, side), F32),
            jax.ShapeDtypeStruct((side, side), F32),
        ],
        in_specs=[S, S, A, A, A, A],
        out_specs=[V, V, V],
        scratch_shapes=[
            pltpu.VMEM((cols, side, side), BF16),
            pltpu.VMEM((cols, side, side), BF16),
            pltpu.VMEM(amp.shape, BF16),
            pltpu.VMEM(probe.shape, F32),
            pltpu.VMEM(tab.shape, BF16),
            pltpu.VMEM((most, 2, side, side), F32),
            pltpu.VMEM((most, modes, side, 2 * side), F32),
            pltpu.VMEM((side, side), F32),
            pltpu.VMEM((modes, 2 * side, side), BF16),
            pltpu.VMEM((modes, side, 2 * side), BF16),
            pltpu.VMEM((side, side), F32),
            pltpu.SemaphoreType.DMA((copies,)),
            pltpu.SemaphoreType.DMA((copies,)),
            pltpu.SemaphoreType.DMA((4,)),
        ],
        compiler_params=pltpu.CompilerParams(collective_id=2, has_side_effects=True, vmem_limit_bytes=62 * 2**20),
        name="main",
    )(items, owner, amp, patch, probe, tab)


def place_kernel(tile, half, list_ref, placed_ref, pow_ref, rim_ref, core_ref, num, shift):
    side = 2 * half
    big, tall, wide = tile + side, side + 8, side + 128
    num[...] = jnp.zeros_like(num)
    shift[...] = jnp.zeros_like(shift)
    shift[2, :side, :side] = pow_ref[...]

    def visit(p, carry):
        @pl.when(list_ref[p, 0] == 1)
        def _():
            r, c = list_ref[p, 2], list_ref[p, 3]
            c0 = pl.multiple_of((c // 128) * 128, 128)
            r0 = pl.multiple_of((r // 8) * 8, 8)
            for q in range(3):
                if q < 2:
                    shift[q, :side, :side] = placed_ref[p, q]
                w = pltpu.roll(pltpu.roll(shift[q], r - r0, 0), c - c0, 1)
                num[q, pl.ds(r0, tall), pl.ds(c0, wide)] += w
        return carry

    lax.fori_loop(0, list_ref.shape[0], visit, 0)
    for q in range(3):
        rim_ref[q] = num[q].astype(BF16)
        core_ref[q] = num[q, half:big - half, half:big - half]


def place_call(items, placed, power, tile):
    side = power.shape[0]
    half = side // 2
    big = tile + side
    V = pl.BlockSpec(memory_space=pltpu.VMEM)
    S = pl.BlockSpec(memory_space=pltpu.SMEM)
    return pl.pallas_call(
        functools.partial(place_kernel, tile, half),
        out_shape=[jax.ShapeDtypeStruct((3, big, big), BF16), jax.ShapeDtypeStruct((3, tile, tile), F32)],
        in_specs=[S, V, V],
        out_specs=[V, V],
        scratch_shapes=[pltpu.VMEM((3, big, big), F32), pltpu.VMEM((3, side + 8, side + 128), F32)],
        compiler_params=pltpu.CompilerParams(vmem_limit_bytes=56 * 2**20),
        name="place",
    )(items, placed, power)


def widen_kernel(got_ref, out_ref):
    n = got_ref.shape[2]
    for c in range(2):
        for k in range(2):
            out_ref[c * n:(c + 1) * n, 128 * k:128 * (k + 1)] = got_ref[c, k].astype(F32)


def widen_call(got):
    n = got.shape[2]
    return pl.pallas_call(widen_kernel, out_shape=jax.ShapeDtypeStruct((2 * n, 256), F32), name="widen")(got)


def on_device(object_field, probe, amplitudes, owner, offsets):
    rows, cols = lax.axis_size("row"), lax.axis_size("col")
    held = amplitudes.shape[0]
    most = 4 * (held - 1)
    side, tile = probe.shape[-1], object_field.shape[1]
    ext, meta = pre_call(owner, offsets, object_field, side, rows, cols)
    patch, items = cut_call(meta, ext, tile, rows, cols, held, most)
    placed, grad, power = main_call(items, owner, amplitudes, patch, probe, rows, cols)
    rim, core = place_call(items, placed, power, tile)
    scale = 1.0 / math.sqrt(rows * cols * held)
    object_out, gradient = post_call(rim, core, object_field, grad, rows, cols, scale)
    return (object_out, widen_call(gradient).reshape(probe.shape))


def solution(mesh):
    return jax.shard_map(
        on_device,
        mesh=mesh,
        in_specs=(
            P(None, "row", "col"),
            P(),
            P(("row", "col"), None, None),
            P(("row", "col")),
            P(("row", "col"), None),
        ),
        out_specs=(P(None, "row", "col"), P()),
        check_vma=False,
    )
```

```python
import functools
import math

import jax
import jax.numpy as jnp
import numpy as np
from jax import lax
from jax.experimental import pallas as pl
from jax.experimental.pallas import tpu as pltpu
from jax.sharding import PartitionSpec as P

F32, BF16 = jnp.float32, jnp.bfloat16
MESH = pl.DeviceIdType.MESH

def tables(side):
    series = np.arange(side, dtype=np.int32)
    angles = (series[:, None] * series[None, :] % side).astype(np.float32) * np.float32(2.0 * math.pi / side)
    factor = np.float32(1.0 / math.sqrt(side))
    re = jnp.asarray(np.cos(angles) * factor).astype(BF16)
    im = jnp.asarray(-np.sin(angles) * factor).astype(BF16)
    return re, im

def dot(a, b):
    return jnp.dot(a, b, preferred_element_type=F32)

def around(row, col, dr, dc, rows, cols):
    return lax.rem(row + dr + rows, rows), lax.rem(col + dc + cols, cols)


NEAR = [(dr, dc) for dr in (-1, 0, 1) for dc in (-1, 0, 1) if (dr, dc) != (0, 0)]


def span(step, tile, half):
    return {-1: (0, half), 0: (half, tile), 1: (half + tile, half)}[step]


def landing(step, tile, half):
    return {-1: (tile - half, half), 0: (0, tile), 1: (0, half)}[step]


def column_peers(row, col, cols):
    depth = 4
    steps = [(0, 1), (1, 0), (0, 3), (3, 0), (1, 1), (3, 3), (1, 3), (3, 1), (2, 0), (0, 2), (2, 2), (1, 2), (3, 2), (2, 1), (2, 3)]
    x, z = col // depth, lax.rem(col, depth)
    return [(row, lax.rem(x + dx, cols // depth) * depth + lax.rem(z + dz, depth)) for dx, dz in steps]


class Sends:
    def __init__(self, send_sem, recv_sem):
        self.send_sem, self.recv_sem, self.at, self.all = send_sem, recv_sem, 0, []

    def __call__(self, src, dst, device):
        n = self.at
        self.at += 1
        copy = pltpu.make_async_remote_copy(
            src_ref=src, dst_ref=dst, send_sem=self.send_sem.at[n], recv_sem=self.recv_sem.at[n],
            device_id=device, device_id_type=MESH)
        copy.start()
        self.all.append(copy)
        return copy

    def finish(self):
        for copy in self.all:
            copy.wait_send()


def greet(devices):
    barrier = pltpu.get_barrier_semaphore()
    for device in devices:
        pl.semaphore_signal(barrier, inc=1, device_id=device, device_id_type=MESH)
    pl.semaphore_wait(barrier, len(devices))


def post_kernel(rows, cols, tile, half, scale, rim_ref, core_ref, obj_ref, grad_ref, out_ref, all16,
                wsum, rim_rows, rim_cols, rim_corners, mate, sum_a, sum_b, got_a, got_b, part_a, part_b, got_a2, got_b2, gsend, grecv):
    row, col = lax.axis_index("row"), lax.axis_index("col")
    core, y = lax.rem(row, 2), row // 2
    ys = rows // 2
    other = (row + 1 - 2 * core, col)
    y_peers = [(lax.rem(y + s, ys) * 2 + core, col) for s in range(1, ys)]
    c_peers = column_peers(row, col, cols)
    near = [around(row, col, dr, dc, rows, cols) for dr, dc in NEAR]
    greet([other] + y_peers + c_peers + near)
    send = Sends(gsend, grecv)
    n = grad_ref.shape[0] // 2
    na, nb = n // ys, n // cols
    fin = n // (ys * cols)
    theirs = pl.ds(pl.multiple_of((1 - core) * n, n), n)
    mine = pl.ds(pl.multiple_of(core * n, n), n)
    pair = send(grad_ref.at[theirs], mate, other)
    rim_copies = []

    def landed(i):
        dr, dc = NEAR[i]
        if dc == 0:
            return rim_rows.at[(dr + 1) // 2]
        if dr == 0:
            return rim_cols.at[(dc + 1) // 2]
        return rim_corners.at[dr + 1 + (dc + 1) // 2]

    def send_rims(which):
        for i in which:
            r0, rl = span(NEAR[i][0], tile, half)
            c0, cl = span(NEAR[i][1], tile, half)
            rim_copies.append(send(rim_ref.at[:, r0:r0 + rl, c0:c0 + cl], landed(i), near[i]))

    send_rims([1, 6])
    pair.wait_recv()
    h = grad_ref[mine, :] + mate[...]
    sum_a[...] = h[:, :128]
    sum_b[...] = h[:, 128:]
    y_at = [lax.rem(y + s, ys) for s in range(1, ys)]
    c_at = [peer[1] for peer in c_peers]

    def piece(k, size):
        return pl.ds(pl.multiple_of(k * size, size), size)

    a1 = [send(sum_a.at[piece(y_at[s], na)], got_a.at[s], y_peers[s]) for s in range(ys - 1)]
    b1 = [send(sum_b.at[piece(c_at[s], nb)], got_b.at[s], c_peers[s]) for s in range(cols - 1)]
    for c in a1:
        c.wait_recv()
    tot = sum_a[piece(y, na), :]
    for s in range(ys - 1):
        tot += got_a[s]
    part_a[...] = tot
    a2 = [send(part_a.at[piece(c_at[s], fin)], got_a2.at[s], c_peers[s]) for s in range(cols - 1)]
    for c in b1:
        c.wait_recv()
    tot = sum_b[piece(col, nb), :]
    for s in range(cols - 1):
        tot += got_b[s]
    part_b[...] = tot
    b2 = [send(part_b.at[piece(y_at[s], fin)], got_b2.at[s], y_peers[s]) for s in range(ys - 1)]
    send_rims([3, 4])
    for c in a2:
        c.wait_recv()
    tot = part_a[piece(col, fin), :]
    for s in range(cols - 1):
        tot += got_a2[s]
    at_a = piece(y * cols + col, fin)
    all16[core, 0, at_a, :] = (tot * scale).astype(all16.dtype)
    a3 = [send(all16.at[core, 0, at_a], all16.at[core, 0, at_a], p) for p in c_peers]
    for c in b2:
        c.wait_recv()
    tot = part_b[piece(y, fin), :]
    for s in range(ys - 1):
        tot += got_b2[s]
    at_b = piece(col * ys + y, fin)
    all16[core, 1, at_b, :] = (tot * scale).astype(all16.dtype)
    b3 = [send(all16.at[core, 1, at_b], all16.at[core, 1, at_b], p) for p in y_peers]
    send_rims([0, 2, 5, 7])
    for c in a3:
        c.wait_recv()
    big_a = piece(y, na)
    a4 = [send(all16.at[core, 0, big_a], all16.at[core, 0, big_a], p) for p in y_peers]
    for c in b3:
        c.wait_recv()
    big_b = piece(col, nb)
    b4 = [send(all16.at[core, 1, big_b], all16.at[core, 1, big_b], p) for p in c_peers]
    for c in rim_copies:
        c.wait_recv()
    out_ref[...] = core_ref[0:2]
    wsum[...] = core_ref[2]
    for i, (dr, dc) in enumerate(NEAR):
        r0, rl = landing(dr, tile, half)
        c0, cl = landing(dc, tile, half)
        keep = (row != -1) & (col != -1)
        if dr:
            keep = keep & (row != (0 if dr == 1 else rows - 1))
        if dc:
            keep = keep & (col != (0 if dc == 1 else cols - 1))

        @pl.when(keep)
        def _(i=i, r0=r0, rl=rl, c0=c0, cl=cl):
            for q in range(2):
                out_ref[q, r0:r0 + rl, c0:c0 + cl] += landed(i)[q].astype(F32)
            wsum[r0:r0 + rl, c0:c0 + cl] += landed(i)[2].astype(F32)

    for q in range(2):
        out_ref[q] = obj_ref[q] + out_ref[q] / (wsum[...] + 1.0)
    for c in a4 + b4:
        c.wait_recv()
    last = send(all16.at[core], all16.at[core], other)
    last.wait_recv()
    send.finish()


def post_call(rim, core, obj, grad, rows, cols, scale):
    tile, wide = obj.shape[1], rim.shape[1]
    half = (wide - tile) // 2
    total = grad.shape[0]
    ys, n = rows // 2, total // 2
    na, nb, fin = n // ys, n // cols, n // (ys * cols)
    copies = 1 + 8 + 2 * (ys - 1) + 2 * (cols - 1) + 2 * (ys - 1) + 2 * (cols - 1) + 1
    V = pl.BlockSpec(memory_space=pltpu.VMEM)
    return pl.pallas_call(
        functools.partial(post_kernel, rows, cols, tile, half, scale),
        out_shape=[jax.ShapeDtypeStruct(obj.shape, F32), jax.ShapeDtypeStruct((2, 2, n, 128), BF16)],
        in_specs=[V, V, V, V],
        out_specs=[V, V],
        scratch_shapes=[
            pltpu.VMEM((tile, tile), F32),
            pltpu.VMEM((2, 3, half, tile), BF16),
            pltpu.VMEM((2, 3, tile, half), BF16),
            pltpu.VMEM((4, 3, half, half), BF16),
            pltpu.VMEM((n, 256), F32),
            pltpu.VMEM((n, 128), F32),
            pltpu.VMEM((n, 128), F32),
            pltpu.VMEM((ys - 1, na, 128), F32),
            pltpu.VMEM((cols - 1, nb, 128), F32),
            pltpu.VMEM((na, 128), F32),
            pltpu.VMEM((nb, 128), F32),
            pltpu.VMEM((cols - 1, fin, 128), F32),
            pltpu.VMEM((ys - 1, fin, 128), F32),
            pltpu.SemaphoreType.DMA((copies,)),
            pltpu.SemaphoreType.DMA((copies,)),
        ],
        compiler_params=pltpu.CompilerParams(collective_id=1, has_side_effects=True, vmem_limit_bytes=40 * 2**20),
        name="post",
    )(rim, core, obj, grad)


def pre_kernel(rows, cols, tile, half, owner_ref, offsets_ref, obj_ref, ext_ref, meta_ref, mine, gsend, grecv, lsem):
    row, col = lax.axis_index("row"), lax.axis_index("col")
    near = [around(row, col, dr, dc, rows, cols) for dr, dc in NEAR]
    c_peers = column_peers(row, col, cols)
    held = owner_ref.shape[0]
    core = pltpu.make_async_copy(obj_ref, ext_ref.at[:, half:half + tile, half:half + tile], lsem.at[0])
    core.start()
    lane = lax.broadcasted_iota(jnp.int32, (1, 128), 1)
    note = jnp.zeros((1, 128), jnp.int32)
    for h in range(held):
        note = jnp.where(lane == h, owner_ref[h], note)
        for k in range(2):
            note = jnp.where(lane == held + 2 * h + k, offsets_ref[h, k], note)
    mine[...] = note
    greet(c_peers + near)
    core.wait()
    send = Sends(gsend, grecv)
    got = []
    for i, (dr, dc) in enumerate(NEAR):
        r0, rl = {-1: (0, half), 0: (0, tile), 1: (tile - half, half)}[dr]
        c0, cl = {-1: (0, half), 0: (0, tile), 1: (tile - half, half)}[dc]
        tr, _ = span(-dr, tile, half)
        tc, _ = span(-dc, tile, half)
        r0, c0 = r0 + half, c0 + half
        got.append(send(ext_ref.at[:, r0:r0 + rl, c0:c0 + cl], ext_ref.at[:, tr:tr + rl, tc:tc + cl], near[i]))
    for s in range(cols - 1):
        got.append(send(mine, meta_ref.at[col], c_peers[s]))
    own = pltpu.make_async_copy(mine, meta_ref.at[col], lsem.at[1])
    own.start()
    for c in got:
        c.wait_recv()
    own.wait()
    send.finish()


def pre_call(owner, offsets, obj, side, rows, cols):
    tile, half = obj.shape[1], side // 2
    big = tile + side
    copies = 8 + cols - 1
    V = pl.BlockSpec(memory_space=pltpu.VMEM)
    S = pl.BlockSpec(memory_space=pltpu.SMEM)
    return pl.pallas_call(
        functools.partial(pre_kernel, rows, cols, tile, half),
        out_shape=[jax.ShapeDtypeStruct((2, big, big), F32), jax.ShapeDtypeStruct((cols, 1, 128), jnp.int32)],
        in_specs=[S, S, pl.BlockSpec(memory_space=pltpu.HBM)],
        out_specs=[V, V],
        scratch_shapes=[
            pltpu.VMEM((1, 128), jnp.int32),
            pltpu.SemaphoreType.DMA((copies,)),
            pltpu.SemaphoreType.DMA((copies,)),
            pltpu.SemaphoreType.DMA((2,)),
        ],
        compiler_params=pltpu.CompilerParams(collective_id=0, has_side_effects=True, vmem_limit_bytes=57 * 2**20),
        name="pre",
    )(owner, offsets, obj)


def cut_kernel(rows, cols, tile, half, held, meta_ref, ext_hbm, patch_hbm, list_ref, ext, patch, esem, osem):
    row, col = lax.axis_index("row"), lax.axis_index("col")
    side = 2 * half
    big, tall, wide, most = tile + side, side + 8, side + 128, list_ref.shape[0]
    fetch = pltpu.make_async_copy(ext_hbm, ext, esem)
    fetch.start()

    def clear(p, carry):
        for k in range(4):
            list_ref[p, k] = 0
        return carry

    lax.fori_loop(0, most, clear, 0)

    def scan(s, count):
        live, r, c = jnp.int32(0), jnp.int32(0), jnp.int32(0)
        for h in range(held):
            hit = meta_ref[s, 0, h] == col
            live = jnp.where(hit, 1, live)
            r = jnp.where(hit, meta_ref[s, 0, held + 2 * h], r)
            c = jnp.where(hit, meta_ref[s, 0, held + 2 * h + 1], c)

        @pl.when((live == 1) & (count < most))
        def _():
            list_ref[count, 0] = 1
            list_ref[count, 1] = s
            list_ref[count, 2] = r
            list_ref[count, 3] = c
        return count + live

    lax.fori_loop(0, cols, scan, 0)
    fetch.wait()

    @pl.when(row == 0)
    def _():
        ext[:, :half, :] = jnp.zeros((2, half, big), F32)

    @pl.when(row == rows - 1)
    def _():
        ext[:, big - half:, :] = jnp.zeros((2, half, big), F32)

    @pl.when(col == 0)
    def _():
        ext[:, :, :half] = jnp.zeros((2, big, half), F32)

    @pl.when(col == cols - 1)
    def _():
        ext[:, :, big - half:] = jnp.zeros((2, big, half), F32)

    def out(p):
        return pltpu.make_async_copy(patch.at[p], patch_hbm.at[p], osem.at[p])

    def visit(p, carry):
        @pl.when(list_ref[p, 0] == 1)
        def _():
            r, c = list_ref[p, 2], list_ref[p, 3]
            c0 = pl.multiple_of((c // 128) * 128, 128)
            r0 = pl.multiple_of((r // 8) * 8, 8)
            for q in range(2):
                w = ext[q, pl.ds(r0, tall), pl.ds(c0, wide)]
                w = pltpu.roll(w, wide - (c - c0), 1)[:, :side]
                patch[p, q] = pltpu.roll(w, tall - (r - r0), 0)[:side]

        @pl.when(list_ref[p, 0] == 0)
        def _():
            patch[p] = jnp.zeros((2, side, side), F32)

        out(p).start()
        return carry

    lax.fori_loop(0, most, visit, 0)

    def drain(p, carry):
        out(p).wait()
        return carry

    lax.fori_loop(0, most, drain, 0)


def cut_call(meta, ext, tile, rows, cols, held, most):
    big = ext.shape[1]
    side = big - tile
    A = pl.BlockSpec(memory_space=pltpu.HBM)
    S = pl.BlockSpec(memory_space=pltpu.SMEM)
    return pl.pallas_call(
        functools.partial(cut_kernel, rows, cols, tile, side // 2, held),
        out_shape=[jax.ShapeDtypeStruct((most, 2, side, side), F32), jax.ShapeDtypeStruct((most, 4), jnp.int32)],
        in_specs=[S, A],
        out_specs=[A, S],
        scratch_shapes=[
            pltpu.VMEM((2, big, big), F32),
            pltpu.VMEM((most, 2, side, side), F32),
            pltpu.SemaphoreType.DMA,
            pltpu.SemaphoreType.DMA((most,)),
        ],
        compiler_params=pltpu.CompilerParams(vmem_limit_bytes=57 * 2**20),
        name="cut",
    )(meta, ext)


def main_kernel(rows, cols, list_ref, owner_ref, amp_hbm, patch_hbm, probe_hbm, tab_hbm,
                placed_hbm, grad_ref, pow_ref,
                placed_ref, psem, slots, amps, amp, probe, tab, patch, far, total, ratio, ebuf, hbuf, ssum,
                gsend, grecv, lsem):
    row, col = lax.axis_index("row"), lax.axis_index("col")
    c_peers = column_peers(row, col, cols)
    held, side, modes, most = amp.shape[0], amp.shape[1], probe.shape[0], patch.shape[0]
    local = [
        pltpu.make_async_copy(amp_hbm, amp, lsem.at[0]),
        pltpu.make_async_copy(probe_hbm, probe, lsem.at[1]),
        pltpu.make_async_copy(tab_hbm, tab, lsem.at[2]),
        pltpu.make_async_copy(patch_hbm, patch, lsem.at[3]),
    ]
    for copy in local:
        copy.start()
    greet(c_peers)
    send = Sends(gsend, grecv)
    local[0].wait()
    amp_copies = []
    for s in range(cols):
        to = col if s == 0 else c_peers[s - 1][1]
        which = jnp.int32(0)
        for h in range(1, held):
            which = jnp.where(owner_ref[h] == to, h, which)
        if s == 0:
            amps[col] = amp[which]
        else:
            slots[s] = amp[which]
            amp_copies.append(send(slots.at[s], amps.at[col], c_peers[s - 1]))
    local[1].wait()
    power = jnp.zeros((side, side), F32)
    for m in range(modes):
        power += probe[m, 0] * probe[m, 0] + probe[m, 1] * probe[m, 1]
    pow_ref[...] = power
    grad_ref[...] = jnp.zeros_like(grad_ref)
    ssum[...] = jnp.zeros_like(ssum)
    local[2].wait()
    local[3].wait()

    chunk = hbuf.shape[2] // modes
    chunks = side // chunk

    def left_pass(k, fields, halves):
        for m in range(modes):
            for h in range(2):
                part = dot(tab[k, h * side:(h + 1) * side], fields[m])
                for c in range(chunks):
                    rows_c = slice(c * chunk, (c + 1) * chunk)
                    halves[c, m * chunk:(m + 1) * chunk, h * side:(h + 1) * side] = part[rows_c].astype(BF16)

    def there(p, fields, halves):
        ssum[...] += patch[p, 0] * patch[p, 0] + patch[p, 1] * patch[p, 1]
        for m in range(modes):
            pr, pi = probe[m, 0], probe[m, 1]
            xr, xi = patch[p, 0], patch[p, 1]
            fields[m, :side] = (pr * xr - pi * xi).astype(BF16)
            fields[m, side:] = (pr * xi + pi * xr).astype(BF16)
        left_pass(0, fields, halves)
        for c in range(chunks):
            rows_c = slice(c * chunk, (c + 1) * chunk)
            out = dot(halves[c], tab[1])
            tot = jnp.zeros((chunk, side), F32)
            for m in range(modes):
                one = out[m * chunk:(m + 1) * chunk]
                far[p, m, rows_c] = one
                tot += one[:, :side] * one[:, :side] + one[:, side:] * one[:, side:]
            total[p, rows_c] = tot

    def there_two(k, carry):
        for u in range(2):
            there(2 * k + u, ebuf.at[u], hbuf.at[u])
        return carry

    lax.fori_loop(0, most // 2, there_two, 0)
    for p in range(most - most % 2, most):
        there(p, ebuf.at[0], hbuf.at[0])
    for copy in amp_copies:
        copy.wait_recv()

    def out(p):
        return pltpu.make_async_copy(placed_ref.at[p], placed_hbm.at[p], psem.at[p])

    def drain(p, carry):
        out(p).wait()
        return carry

    def back(p, carry):
        fields, halves = ebuf.at[0], hbuf.at[0]
        ratio[...] = amps[list_ref[p, 1]].astype(F32) * lax.rsqrt(jnp.maximum(total[p], 0.25))
        for m in range(modes):
            fields[m, :side] = (far[p, m, :, :side] * ratio[...]).astype(BF16)
            fields[m, side:] = (far[p, m, :, side:] * ratio[...]).astype(BF16)
        left_pass(2, fields, halves)
        for c in range(chunks):
            rows_c = slice(c * chunk, (c + 1) * chunk)
            ret = dot(halves[c], tab[3])
            xr, xi = patch[p, 0, rows_c], patch[p, 1, rows_c]
            nr, ni = -xr * pow_ref[rows_c], -xi * pow_ref[rows_c]
            for m in range(modes):
                one = ret[m * chunk:(m + 1) * chunk]
                rr, ri = one[:, :side], one[:, side:]
                pr, pi = probe[m, 0, rows_c], probe[m, 1, rows_c]
                nr += pr * rr + pi * ri
                ni += pr * ri - pi * rr
                at_r = 2 * m * side + c * chunk
                at_i = at_r + side
                grad_ref[at_r:at_r + chunk] += xr * rr + xi * ri
                grad_ref[at_i:at_i + chunk] += xr * ri - xi * rr
            placed_ref[p, 0, rows_c] = nr
            placed_ref[p, 1, rows_c] = ni
        out(p).start()
        return carry

    lax.fori_loop(0, most, back, 0)
    for m in range(modes):
        for q in range(2):
            grad_ref[(2 * m + q) * side:(2 * m + q + 1) * side] -= probe[m, q] * ssum[...]
    lax.fori_loop(0, most, drain, 0)
    send.finish()


def main_call(items, owner, amp, patch, probe, rows, cols):
    side, modes, most = amp.shape[1], probe.shape[0], patch.shape[0]
    copies = cols - 1
    tr, ti = tables(side)

    def left(a, b):
        return jnp.concatenate([jnp.concatenate([a, -b], 1), jnp.concatenate([b, a], 1)], 0)

    def right(a, b):
        return jnp.concatenate([jnp.concatenate([a, b], 1), jnp.concatenate([-b, a], 1)], 0)

    tab = jnp.stack([left(tr, ti), right(tr, ti), left(tr, -ti), right(tr, -ti)])
    V = pl.BlockSpec(memory_space=pltpu.VMEM)
    A = pl.BlockSpec(memory_space=pltpu.HBM)
    S = pl.BlockSpec(memory_space=pltpu.SMEM)
    return pl.pallas_call(
        functools.partial(main_kernel, rows, cols),
        out_shape=[
            jax.ShapeDtypeStruct((most, 2, side, side), F32),
            jax.ShapeDtypeStruct((modes * 2 * side, side), F32),
            jax.ShapeDtypeStruct((side, side), F32),
        ],
        in_specs=[S, S, A, A, A, A],
        out_specs=[A, V, V],
        scratch_shapes=[
            pltpu.VMEM((most, 2, side, side), F32),
            pltpu.SemaphoreType.DMA((most,)),
            pltpu.VMEM((cols, side, side), BF16),
            pltpu.VMEM((cols, side, side), BF16),
            pltpu.VMEM(amp.shape, BF16),
            pltpu.VMEM(probe.shape, F32),
            pltpu.VMEM(tab.shape, BF16),
            pltpu.VMEM((most, 2, side, side), F32),
            pltpu.VMEM((most, modes, side, 2 * side), F32),
            pltpu.VMEM((most, side, side), F32),
            pltpu.VMEM((side, side), F32),
            pltpu.VMEM((2, modes, 2 * side, side), BF16),
            pltpu.VMEM((2, 4, modes * side // 4, 2 * side), BF16),
            pltpu.VMEM((side, side), F32),
            pltpu.SemaphoreType.DMA((copies,)),
            pltpu.SemaphoreType.DMA((copies,)),
            pltpu.SemaphoreType.DMA((4,)),
        ],
        compiler_params=pltpu.CompilerParams(collective_id=2, has_side_effects=True, vmem_limit_bytes=62 * 2**20),
        name="main",
    )(items, owner, amp, patch, probe, tab)


def place_kernel(tile, half, list_ref, placed_hbm, pow_ref, rim_ref, core_ref, placed_ref, psem, num, shift):
    side = 2 * half
    big, tall, wide = tile + side, side + 8, side + 128

    def fetch(p):
        return pltpu.make_async_copy(placed_hbm.at[p], placed_ref.at[p], psem.at[p])

    def start(p, carry):
        fetch(p).start()
        return carry

    lax.fori_loop(0, list_ref.shape[0], start, 0)
    num[...] = jnp.zeros_like(num)
    shift[...] = jnp.zeros_like(shift)
    shift[2, :side, :side] = pow_ref[...]

    def visit(p, carry):
        fetch(p).wait()

        @pl.when(list_ref[p, 0] == 1)
        def _():
            r, c = list_ref[p, 2], list_ref[p, 3]
            c0 = pl.multiple_of((c // 128) * 128, 128)
            r0 = pl.multiple_of((r // 8) * 8, 8)
            for q in range(3):
                if q < 2:
                    shift[q, :side, :side] = placed_ref[p, q]
                w = pltpu.roll(pltpu.roll(shift[q], r - r0, 0), c - c0, 1)
                num[q, pl.ds(r0, tall), pl.ds(c0, wide)] += w
        return carry

    lax.fori_loop(0, list_ref.shape[0], visit, 0)
    for q in range(3):
        rim_ref[q] = num[q].astype(BF16)
        core_ref[q] = num[q, half:big - half, half:big - half]


def place_call(items, placed, power, tile):
    side = power.shape[0]
    half = side // 2
    big = tile + side
    V = pl.BlockSpec(memory_space=pltpu.VMEM)
    S = pl.BlockSpec(memory_space=pltpu.SMEM)
    return pl.pallas_call(
        functools.partial(place_kernel, tile, half),
        out_shape=[jax.ShapeDtypeStruct((3, big, big), BF16), jax.ShapeDtypeStruct((3, tile, tile), F32)],
        in_specs=[S, pl.BlockSpec(memory_space=pltpu.HBM), V],
        out_specs=[V, V],
        scratch_shapes=[
            pltpu.VMEM(placed.shape, F32),
            pltpu.SemaphoreType.DMA((placed.shape[0],)),
            pltpu.VMEM((3, big, big), F32), pltpu.VMEM((3, side + 8, side + 128), F32)],
        compiler_params=pltpu.CompilerParams(vmem_limit_bytes=50 * 2**20),
        name="place",
    )(items, placed, power)


def widen_kernel(got_ref, out_ref):
    n = got_ref.shape[2]
    for c in range(2):
        for k in range(2):
            out_ref[c * n:(c + 1) * n, 128 * k:128 * (k + 1)] = got_ref[c, k].astype(F32)


def widen_call(got):
    n = got.shape[2]
    return pl.pallas_call(widen_kernel, out_shape=jax.ShapeDtypeStruct((2 * n, 256), F32), name="widen")(got)


def on_device(object_field, probe, amplitudes, owner, offsets):
    rows, cols = lax.axis_size("row"), lax.axis_size("col")
    held = amplitudes.shape[0]
    most = 4 * (held - 1)
    side, tile = probe.shape[-1], object_field.shape[1]
    ext, meta = pre_call(owner, offsets, object_field, side, rows, cols)
    patch, items = cut_call(meta, ext, tile, rows, cols, held, most)
    placed, grad, power = main_call(items, owner, amplitudes, patch, probe, rows, cols)
    rim, core = place_call(items, placed, power, tile)
    scale = 1.0 / math.sqrt(rows * cols * held)
    object_out, gradient = post_call(rim, core, object_field, grad, rows, cols, scale)
    return (object_out, widen_call(gradient).reshape(probe.shape))


def solution(mesh):
    return jax.shard_map(
        on_device,
        mesh=mesh,
        in_specs=(
            P(None, "row", "col"),
            P(),
            P(("row", "col"), None, None),
            P(("row", "col")),
            P(("row", "col"), None),
        ),
        out_specs=(P(None, "row", "col"), P()),
        check_vma=False,
    )
```

```python
import functools
import math

import jax
import jax.numpy as jnp
import numpy as np
from jax import lax
from jax.experimental import pallas as pl
from jax.experimental.pallas import tpu as pltpu
from jax.sharding import PartitionSpec as P

F32, BF16 = jnp.float32, jnp.bfloat16
MESH = pl.DeviceIdType.MESH

def tables(side):
    series = np.arange(side, dtype=np.int32)
    angles = (series[:, None] * series[None, :] % side).astype(np.float32) * np.float32(2.0 * math.pi / side)
    factor = np.float32(1.0 / math.sqrt(side))
    re = jnp.asarray(np.cos(angles) * factor).astype(BF16)
    im = jnp.asarray(-np.sin(angles) * factor).astype(BF16)
    return re, im

def dot(a, b):
    return jnp.dot(a, b, preferred_element_type=F32)

def around(row, col, dr, dc, rows, cols):
    return lax.rem(row + dr + rows, rows), lax.rem(col + dc + cols, cols)


NEAR = [(dr, dc) for dr in (-1, 0, 1) for dc in (-1, 0, 1) if (dr, dc) != (0, 0)]


def span(step, tile, half):
    return {-1: (0, half), 0: (half, tile), 1: (half + tile, half)}[step]


def landing(step, tile, half):
    return {-1: (tile - half, half), 0: (0, tile), 1: (0, half)}[step]


def column_peers(row, col, cols):
    depth = 4
    steps = [(0, 1), (1, 0), (0, 3), (3, 0), (1, 1), (3, 3), (1, 3), (3, 1), (2, 0), (0, 2), (2, 2), (1, 2), (3, 2), (2, 1), (2, 3)]
    x, z = col // depth, lax.rem(col, depth)
    return [(row, lax.rem(x + dx, cols // depth) * depth + lax.rem(z + dz, depth)) for dx, dz in steps]


class Sends:
    def __init__(self, send_sem, recv_sem):
        self.send_sem, self.recv_sem, self.at, self.all = send_sem, recv_sem, 0, []

    def __call__(self, src, dst, device):
        n = self.at
        self.at += 1
        copy = pltpu.make_async_remote_copy(
            src_ref=src, dst_ref=dst, send_sem=self.send_sem.at[n], recv_sem=self.recv_sem.at[n],
            device_id=device, device_id_type=MESH)
        copy.start()
        self.all.append(copy)
        return copy

    def finish(self):
        for copy in self.all:
            copy.wait_send()


def greet(devices):
    barrier = pltpu.get_barrier_semaphore()
    for device in devices:
        pl.semaphore_signal(barrier, inc=1, device_id=device, device_id_type=MESH)
    pl.semaphore_wait(barrier, len(devices))


def post_kernel(rows, cols, tile, half, scale, rows_ref, cols_ref, corners_ref, core_ref, obj_ref, grad_ref, out_ref, all16,
                wsum, rim_rows, rim_cols, rim_corners, mate, sum_a, sum_b, got_a, got_b, part_a, part_b, got_a2, got_b2, gsend, grecv):
    row, col = lax.axis_index("row"), lax.axis_index("col")
    core, y = lax.rem(row, 2), row // 2
    ys = rows // 2
    other = (row + 1 - 2 * core, col)
    y_peers = [(lax.rem(y + s, ys) * 2 + core, col) for s in range(1, ys)]
    c_peers = column_peers(row, col, cols)
    near = [around(row, col, dr, dc, rows, cols) for dr, dc in NEAR]
    greet([other] + y_peers + c_peers + near)
    send = Sends(gsend, grecv)
    n = grad_ref.shape[0] // 2
    na, nb = n // ys, n // cols
    fin = n // (ys * cols)
    theirs = pl.ds(pl.multiple_of((1 - core) * n, n), n)
    mine = pl.ds(pl.multiple_of(core * n, n), n)
    pair = send(grad_ref.at[theirs], mate, other)
    rim_copies = []

    def place(i, by_rows, by_cols, at_corners):
        dr, dc = NEAR[i]
        if dc == 0:
            return by_rows.at[(dr + 1) // 2]
        if dr == 0:
            return by_cols.at[(dc + 1) // 2]
        return at_corners.at[dr + 1 + (dc + 1) // 2]

    def landed(i):
        return place(i, rim_rows, rim_cols, rim_corners)

    def send_rims(which):
        for i in which:
            rim_copies.append(send(place(i, rows_ref, cols_ref, corners_ref), landed(i), near[i]))

    send_rims([1, 6])
    pair.wait_recv()
    h = grad_ref[mine, :] + mate[...]
    sum_a[...] = h[:, :128]
    sum_b[...] = h[:, 128:]
    y_at = [lax.rem(y + s, ys) for s in range(1, ys)]
    c_at = [peer[1] for peer in c_peers]

    def piece(k, size):
        return pl.ds(pl.multiple_of(k * size, size), size)

    a1 = [send(sum_a.at[piece(y_at[s], na)], got_a.at[s], y_peers[s]) for s in range(ys - 1)]
    b1 = [send(sum_b.at[piece(c_at[s], nb)], got_b.at[s], c_peers[s]) for s in range(cols - 1)]
    for c in a1:
        c.wait_recv()
    tot = sum_a[piece(y, na), :]
    for s in range(ys - 1):
        tot += got_a[s]
    part_a[...] = tot
    a2 = [send(part_a.at[piece(c_at[s], fin)], got_a2.at[s], c_peers[s]) for s in range(cols - 1)]
    for c in b1:
        c.wait_recv()
    tot = sum_b[piece(col, nb), :]
    for s in range(cols - 1):
        tot += got_b[s]
    part_b[...] = tot
    b2 = [send(part_b.at[piece(y_at[s], fin)], got_b2.at[s], y_peers[s]) for s in range(ys - 1)]
    send_rims([3, 4])
    for c in a2:
        c.wait_recv()
    tot = part_a[piece(col, fin), :]
    for s in range(cols - 1):
        tot += got_a2[s]
    at_a = piece(y * cols + col, fin)
    all16[core, 0, at_a, :] = (tot * scale).astype(all16.dtype)
    a3 = [send(all16.at[core, 0, at_a], all16.at[core, 0, at_a], p) for p in c_peers]
    for c in b2:
        c.wait_recv()
    tot = part_b[piece(y, fin), :]
    for s in range(ys - 1):
        tot += got_b2[s]
    at_b = piece(col * ys + y, fin)
    all16[core, 1, at_b, :] = (tot * scale).astype(all16.dtype)
    b3 = [send(all16.at[core, 1, at_b], all16.at[core, 1, at_b], p) for p in y_peers]
    send_rims([0, 2, 5, 7])
    for c in a3:
        c.wait_recv()
    big_a = piece(y, na)
    a4 = [send(all16.at[core, 0, big_a], all16.at[core, 0, big_a], p) for p in y_peers]
    for c in b3:
        c.wait_recv()
    big_b = piece(col, nb)
    b4 = [send(all16.at[core, 1, big_b], all16.at[core, 1, big_b], p) for p in c_peers]
    for c in rim_copies:
        c.wait_recv()
    out_ref[...] = core_ref[0:2]
    wsum[...] = core_ref[2]
    for i, (dr, dc) in enumerate(NEAR):
        r0, rl = landing(dr, tile, half)
        c0, cl = landing(dc, tile, half)
        keep = (row != -1) & (col != -1)
        if dr:
            keep = keep & (row != (0 if dr == 1 else rows - 1))
        if dc:
            keep = keep & (col != (0 if dc == 1 else cols - 1))

        @pl.when(keep)
        def _(i=i, r0=r0, rl=rl, c0=c0, cl=cl):
            for q in range(2):
                out_ref[q, r0:r0 + rl, c0:c0 + cl] += landed(i)[q].astype(F32)
            wsum[r0:r0 + rl, c0:c0 + cl] += landed(i)[2].astype(F32)

    for q in range(2):
        out_ref[q] = obj_ref[q] + out_ref[q] / (wsum[...] + 1.0)
    for c in a4 + b4:
        c.wait_recv()
    last = send(all16.at[core], all16.at[core], other)
    last.wait_recv()
    send.finish()


def post_call(rims, core, obj, grad, rows, cols, scale):
    tile, half = obj.shape[1], rims[0].shape[2]
    total = grad.shape[0]
    ys, n = rows // 2, total // 2
    na, nb, fin = n // ys, n // cols, n // (ys * cols)
    copies = 1 + 8 + 2 * (ys - 1) + 2 * (cols - 1) + 2 * (ys - 1) + 2 * (cols - 1) + 1
    V = pl.BlockSpec(memory_space=pltpu.VMEM)
    return pl.pallas_call(
        functools.partial(post_kernel, rows, cols, tile, half, scale),
        out_shape=[jax.ShapeDtypeStruct(obj.shape, F32), jax.ShapeDtypeStruct((2, 2, n, 128), BF16)],
        in_specs=[V] * 6,
        out_specs=[V, V],
        scratch_shapes=[
            pltpu.VMEM((tile, tile), F32),
            pltpu.VMEM((2, 3, half, tile), BF16),
            pltpu.VMEM((2, 3, tile, half), BF16),
            pltpu.VMEM((4, 3, half, half), BF16),
            pltpu.VMEM((n, 256), F32),
            pltpu.VMEM((n, 128), F32),
            pltpu.VMEM((n, 128), F32),
            pltpu.VMEM((ys - 1, na, 128), F32),
            pltpu.VMEM((cols - 1, nb, 128), F32),
            pltpu.VMEM((na, 128), F32),
            pltpu.VMEM((nb, 128), F32),
            pltpu.VMEM((cols - 1, fin, 128), F32),
            pltpu.VMEM((ys - 1, fin, 128), F32),
            pltpu.SemaphoreType.DMA((copies,)),
            pltpu.SemaphoreType.DMA((copies,)),
        ],
        compiler_params=pltpu.CompilerParams(collective_id=1, has_side_effects=True, vmem_limit_bytes=40 * 2**20),
        name="post",
    )(*rims, core, obj, grad)


def pre_kernel(rows, cols, tile, half, owner_ref, offsets_ref, obj_ref, ext_ref, meta_ref, mine, gsend, grecv, lsem):
    row, col = lax.axis_index("row"), lax.axis_index("col")
    near = [around(row, col, dr, dc, rows, cols) for dr, dc in NEAR]
    c_peers = column_peers(row, col, cols)
    held = owner_ref.shape[0]
    core = pltpu.make_async_copy(obj_ref, ext_ref.at[:, half:half + tile, half:half + tile], lsem.at[0])
    core.start()
    lane = lax.broadcasted_iota(jnp.int32, (1, 128), 1)
    note = jnp.zeros((1, 128), jnp.int32)
    for h in range(held):
        note = jnp.where(lane == h, owner_ref[h], note)
        for k in range(2):
            note = jnp.where(lane == held + 2 * h + k, offsets_ref[h, k], note)
    mine[...] = note
    greet(c_peers + near)
    core.wait()
    send = Sends(gsend, grecv)
    got = []
    for i, (dr, dc) in enumerate(NEAR):
        r0, rl = {-1: (0, half), 0: (0, tile), 1: (tile - half, half)}[dr]
        c0, cl = {-1: (0, half), 0: (0, tile), 1: (tile - half, half)}[dc]
        tr, _ = span(-dr, tile, half)
        tc, _ = span(-dc, tile, half)
        r0, c0 = r0 + half, c0 + half
        got.append(send(ext_ref.at[:, r0:r0 + rl, c0:c0 + cl], ext_ref.at[:, tr:tr + rl, tc:tc + cl], near[i]))
    for s in range(cols - 1):
        got.append(send(mine, meta_ref.at[col], c_peers[s]))
    own = pltpu.make_async_copy(mine, meta_ref.at[col], lsem.at[1])
    own.start()
    for c in got:
        c.wait_recv()
    own.wait()
    send.finish()


def pre_call(owner, offsets, obj, side, rows, cols):
    tile, half = obj.shape[1], side // 2
    big = tile + side
    copies = 8 + cols - 1
    V = pl.BlockSpec(memory_space=pltpu.VMEM)
    S = pl.BlockSpec(memory_space=pltpu.SMEM)
    return pl.pallas_call(
        functools.partial(pre_kernel, rows, cols, tile, half),
        out_shape=[jax.ShapeDtypeStruct((2, big, big), F32), jax.ShapeDtypeStruct((cols, 1, 128), jnp.int32)],
        in_specs=[S, S, pl.BlockSpec(memory_space=pltpu.HBM)],
        out_specs=[V, V],
        scratch_shapes=[
            pltpu.VMEM((1, 128), jnp.int32),
            pltpu.SemaphoreType.DMA((copies,)),
            pltpu.SemaphoreType.DMA((copies,)),
            pltpu.SemaphoreType.DMA((2,)),
        ],
        compiler_params=pltpu.CompilerParams(collective_id=0, has_side_effects=True, vmem_limit_bytes=57 * 2**20),
        name="pre",
    )(owner, offsets, obj)


def cut_kernel(rows, cols, tile, half, held, meta_ref, ext_hbm, patch_hbm, list_ref, ext, patch, esem, osem):
    row, col = lax.axis_index("row"), lax.axis_index("col")
    side = 2 * half
    big, tall, wide, most = tile + side, side + 8, side + 128, list_ref.shape[0]
    fetch = pltpu.make_async_copy(ext_hbm, ext, esem)
    fetch.start()

    def clear(p, carry):
        for k in range(8):
            list_ref[p, k] = 0
        return carry

    lax.fori_loop(0, most, clear, 0)

    def scan(s, count):
        live, r, c = jnp.int32(0), jnp.int32(0), jnp.int32(0)
        for h in range(held):
            hit = meta_ref[s, 0, h] == col
            live = jnp.where(hit, 1, live)
            r = jnp.where(hit, meta_ref[s, 0, held + 2 * h], r)
            c = jnp.where(hit, meta_ref[s, 0, held + 2 * h + 1], c)

        @pl.when((live == 1) & (count < most))
        def _():
            list_ref[count, 0] = 1
            list_ref[count, 1] = s
            list_ref[count, 2] = r // 8
            list_ref[count, 3] = lax.rem(r, 8)
            list_ref[count, 4] = c // 128
            list_ref[count, 5] = lax.rem(c, 128)
        return count + live

    lax.fori_loop(0, cols, scan, 0)
    fetch.wait()

    @pl.when(row == 0)
    def _():
        ext[:, :half, :] = jnp.zeros((2, half, big), F32)

    @pl.when(row == rows - 1)
    def _():
        ext[:, big - half:, :] = jnp.zeros((2, half, big), F32)

    @pl.when(col == 0)
    def _():
        ext[:, :, :half] = jnp.zeros((2, big, half), F32)

    @pl.when(col == cols - 1)
    def _():
        ext[:, :, big - half:] = jnp.zeros((2, big, half), F32)

    def out(p):
        return pltpu.make_async_copy(patch.at[p], patch_hbm.at[p], osem.at[p])

    def visit(p, carry):
        @pl.when(list_ref[p, 0] == 1)
        def _():
            r0 = pl.multiple_of(list_ref[p, 2] * 8, 8)
            c0 = pl.multiple_of(list_ref[p, 4] * 128, 128)
            for q in range(2):
                w = ext[q, pl.ds(r0, tall), pl.ds(c0, wide)]
                w = pltpu.roll(w, wide - list_ref[p, 5], 1)[:, :side]
                patch[p, q] = pltpu.roll(w, tall - list_ref[p, 3], 0)[:side]

        @pl.when(list_ref[p, 0] == 0)
        def _():
            patch[p] = jnp.zeros((2, side, side), F32)

        out(p).start()
        return carry

    lax.fori_loop(0, most, visit, 0)

    def drain(p, carry):
        out(p).wait()
        return carry

    lax.fori_loop(0, most, drain, 0)


def cut_call(meta, ext, tile, rows, cols, held, most):
    big = ext.shape[1]
    side = big - tile
    A = pl.BlockSpec(memory_space=pltpu.HBM)
    S = pl.BlockSpec(memory_space=pltpu.SMEM)
    return pl.pallas_call(
        functools.partial(cut_kernel, rows, cols, tile, side // 2, held),
        out_shape=[jax.ShapeDtypeStruct((most, 2, side, side), F32), jax.ShapeDtypeStruct((most, 8), jnp.int32)],
        in_specs=[S, A],
        out_specs=[A, S],
        scratch_shapes=[
            pltpu.VMEM((2, big, big), F32),
            pltpu.VMEM((most, 2, side, side), F32),
            pltpu.SemaphoreType.DMA,
            pltpu.SemaphoreType.DMA((most,)),
        ],
        compiler_params=pltpu.CompilerParams(vmem_limit_bytes=57 * 2**20),
        name="cut",
    )(meta, ext)


def main_kernel(rows, cols, list_ref, owner_ref, amp_hbm, patch_hbm, probe_hbm, tab_hbm,
                placed_hbm, grad_ref, pow_ref,
                placed_ref, psem, slots, amps, amp, probe, tab, patch, far, total, ratio, ebuf, hbuf, ssum,
                gsend, grecv, lsem):
    row, col = lax.axis_index("row"), lax.axis_index("col")
    c_peers = column_peers(row, col, cols)
    held, side, modes, most = amp.shape[0], amp.shape[1], probe.shape[0], patch.shape[0]
    local = [
        pltpu.make_async_copy(amp_hbm, amp, lsem.at[0]),
        pltpu.make_async_copy(probe_hbm, probe, lsem.at[1]),
        pltpu.make_async_copy(tab_hbm, tab, lsem.at[2]),
        pltpu.make_async_copy(patch_hbm, patch, lsem.at[3]),
    ]
    for copy in local:
        copy.start()
    greet(c_peers)
    send = Sends(gsend, grecv)
    local[0].wait()
    amp_copies = []
    for s in range(cols):
        to = col if s == 0 else c_peers[s - 1][1]
        which = jnp.int32(0)
        for h in range(1, held):
            which = jnp.where(owner_ref[h] == to, h, which)
        if s == 0:
            amps[col] = amp[which]
        else:
            slots[s] = amp[which]
            amp_copies.append(send(slots.at[s], amps.at[col], c_peers[s - 1]))
    local[1].wait()
    power = jnp.zeros((side, side), F32)
    for m in range(modes):
        power += probe[m, 0] * probe[m, 0] + probe[m, 1] * probe[m, 1]
    pow_ref[...] = power
    grad_ref[...] = jnp.zeros_like(grad_ref)
    ssum[...] = jnp.zeros_like(ssum)
    local[2].wait()
    local[3].wait()

    chunk = hbuf.shape[2] // modes
    chunks = side // chunk

    def left_pass(k, fields, halves):
        for m in range(modes):
            for h in range(2):
                part = dot(tab[k, h * side:(h + 1) * side], fields[m])
                for c in range(chunks):
                    rows_c = slice(c * chunk, (c + 1) * chunk)
                    halves[c, m * chunk:(m + 1) * chunk, h * side:(h + 1) * side] = part[rows_c].astype(BF16)

    def there(p, fields, halves):
        ssum[...] += patch[p, 0] * patch[p, 0] + patch[p, 1] * patch[p, 1]
        for m in range(modes):
            pr, pi = probe[m, 0], probe[m, 1]
            xr, xi = patch[p, 0], patch[p, 1]
            fields[m, :side] = (pr * xr - pi * xi).astype(BF16)
            fields[m, side:] = (pr * xi + pi * xr).astype(BF16)
        left_pass(0, fields, halves)
        for c in range(chunks):
            rows_c = slice(c * chunk, (c + 1) * chunk)
            out = dot(halves[c], tab[1])
            tot = jnp.zeros((chunk, side), F32)
            for m in range(modes):
                one = out[m * chunk:(m + 1) * chunk]
                far[p, m, rows_c] = one
                tot += one[:, :side] * one[:, :side] + one[:, side:] * one[:, side:]
            total[p, rows_c] = tot

    def there_two(k, carry):
        for u in range(2):
            there(2 * k + u, ebuf.at[u], hbuf.at[u])
        return carry

    lax.fori_loop(0, most // 2, there_two, 0)
    for p in range(most - most % 2, most):
        there(p, ebuf.at[0], hbuf.at[0])
    for copy in amp_copies:
        copy.wait_recv()

    def out(p):
        return pltpu.make_async_copy(placed_ref.at[p], placed_hbm.at[p], psem.at[p])

    def drain(p, carry):
        out(p).wait()
        return carry

    def back(p, carry):
        fields, halves = ebuf.at[0], hbuf.at[0]
        ratio[...] = amps[list_ref[p, 1]].astype(F32) * lax.rsqrt(jnp.maximum(total[p], 0.25))
        for m in range(modes):
            fields[m, :side] = (far[p, m, :, :side] * ratio[...]).astype(BF16)
            fields[m, side:] = (far[p, m, :, side:] * ratio[...]).astype(BF16)
        left_pass(2, fields, halves)
        for c in range(chunks):
            rows_c = slice(c * chunk, (c + 1) * chunk)
            ret = dot(halves[c], tab[3])
            xr, xi = patch[p, 0, rows_c], patch[p, 1, rows_c]
            nr, ni = -xr * pow_ref[rows_c], -xi * pow_ref[rows_c]
            for m in range(modes):
                one = ret[m * chunk:(m + 1) * chunk]
                rr, ri = one[:, :side], one[:, side:]
                pr, pi = probe[m, 0, rows_c], probe[m, 1, rows_c]
                nr += pr * rr + pi * ri
                ni += pr * ri - pi * rr
                at_r = 2 * m * side + c * chunk
                at_i = at_r + side
                grad_ref[at_r:at_r + chunk] += xr * rr + xi * ri
                grad_ref[at_i:at_i + chunk] += xr * ri - xi * rr
            placed_ref[p, 0, rows_c] = nr
            placed_ref[p, 1, rows_c] = ni
        out(p).start()
        return carry

    lax.fori_loop(0, most, back, 0)
    for m in range(modes):
        for q in range(2):
            grad_ref[(2 * m + q) * side:(2 * m + q + 1) * side] -= probe[m, q] * ssum[...]
    lax.fori_loop(0, most, drain, 0)
    send.finish()


def main_call(items, owner, amp, patch, probe, rows, cols):
    side, modes, most = amp.shape[1], probe.shape[0], patch.shape[0]
    copies = cols - 1
    tr, ti = tables(side)

    def left(a, b):
        return jnp.concatenate([jnp.concatenate([a, -b], 1), jnp.concatenate([b, a], 1)], 0)

    def right(a, b):
        return jnp.concatenate([jnp.concatenate([a, b], 1), jnp.concatenate([-b, a], 1)], 0)

    tab = jnp.stack([left(tr, ti), right(tr, ti), left(tr, -ti), right(tr, -ti)])
    V = pl.BlockSpec(memory_space=pltpu.VMEM)
    A = pl.BlockSpec(memory_space=pltpu.HBM)
    S = pl.BlockSpec(memory_space=pltpu.SMEM)
    return pl.pallas_call(
        functools.partial(main_kernel, rows, cols),
        out_shape=[
            jax.ShapeDtypeStruct((most, 2, side, side), F32),
            jax.ShapeDtypeStruct((modes * 2 * side, side), F32),
            jax.ShapeDtypeStruct((side, side), F32),
        ],
        in_specs=[S, S, A, A, A, A],
        out_specs=[A, V, V],
        scratch_shapes=[
            pltpu.VMEM((most, 2, side, side), F32),
            pltpu.SemaphoreType.DMA((most,)),
            pltpu.VMEM((cols, side, side), BF16),
            pltpu.VMEM((cols, side, side), BF16),
            pltpu.VMEM(amp.shape, BF16),
            pltpu.VMEM(probe.shape, F32),
            pltpu.VMEM(tab.shape, BF16),
            pltpu.VMEM((most, 2, side, side), F32),
            pltpu.VMEM((most, modes, side, 2 * side), F32),
            pltpu.VMEM((most, side, side), F32),
            pltpu.VMEM((side, side), F32),
            pltpu.VMEM((2, modes, 2 * side, side), BF16),
            pltpu.VMEM((2, 4, modes * side // 4, 2 * side), BF16),
            pltpu.VMEM((side, side), F32),
            pltpu.SemaphoreType.DMA((copies,)),
            pltpu.SemaphoreType.DMA((copies,)),
            pltpu.SemaphoreType.DMA((4,)),
        ],
        compiler_params=pltpu.CompilerParams(collective_id=2, has_side_effects=True, vmem_limit_bytes=62 * 2**20),
        name="main",
    )(items, owner, amp, patch, probe, tab)


def place_kernel(tile, half, list_ref, placed_hbm, pow_ref, rows_ref, cols_ref, corners_ref, core_ref, placed_ref, psem, num, shift):
    side = 2 * half
    big, tall, wide = tile + side, side + 8, side + 128

    def fetch(p):
        return pltpu.make_async_copy(placed_hbm.at[p], placed_ref.at[p], psem.at[p])

    def start(p, carry):
        fetch(p).start()
        return carry

    lax.fori_loop(0, list_ref.shape[0], start, 0)
    num[...] = jnp.zeros_like(num)
    shift[...] = jnp.zeros_like(shift)
    shift[2, :side, :side] = pow_ref[...]

    def visit(p, carry):
        fetch(p).wait()

        @pl.when(list_ref[p, 0] == 1)
        def _():
            r0 = pl.multiple_of(list_ref[p, 2] * 8, 8)
            c0 = pl.multiple_of(list_ref[p, 4] * 128, 128)
            for q in range(3):
                if q < 2:
                    shift[q, :side, :side] = placed_ref[p, q]
                w = pltpu.roll(pltpu.roll(shift[q], list_ref[p, 3], 0), list_ref[p, 5], 1)
                num[q, pl.ds(r0, tall), pl.ds(c0, wide)] += w
        return carry

    lax.fori_loop(0, list_ref.shape[0], visit, 0)
    for q in range(3):
        for dr, dc in NEAR:
            r0, rl = span(dr, tile, half)
            c0, cl = span(dc, tile, half)
            rim = num[q, r0:r0 + rl, c0:c0 + cl].astype(BF16)
            if dc == 0:
                rows_ref[(dr + 1) // 2, q] = rim
            elif dr == 0:
                cols_ref[(dc + 1) // 2, q] = rim
            else:
                corners_ref[dr + 1 + (dc + 1) // 2, q] = rim
        core_ref[q] = num[q, half:big - half, half:big - half]


def place_call(items, placed, power, tile):
    side = power.shape[0]
    half = side // 2
    big = tile + side
    V = pl.BlockSpec(memory_space=pltpu.VMEM)
    S = pl.BlockSpec(memory_space=pltpu.SMEM)
    return pl.pallas_call(
        functools.partial(place_kernel, tile, half),
        out_shape=[
            jax.ShapeDtypeStruct((2, 3, half, tile), BF16),
            jax.ShapeDtypeStruct((2, 3, tile, half), BF16),
            jax.ShapeDtypeStruct((4, 3, half, half), BF16),
            jax.ShapeDtypeStruct((3, tile, tile), F32)],
        in_specs=[S, pl.BlockSpec(memory_space=pltpu.HBM), V],
        out_specs=[V, V, V, V],
        scratch_shapes=[
            pltpu.VMEM(placed.shape, F32),
            pltpu.SemaphoreType.DMA((placed.shape[0],)),
            pltpu.VMEM((3, big, big), F32), pltpu.VMEM((3, side + 8, side + 128), F32)],
        compiler_params=pltpu.CompilerParams(vmem_limit_bytes=46 * 2**20),
        name="place",
    )(items, placed, power)


def finish_kernel(obj_ref, got_ref, out_hbm, grad_hbm, wide, sem):
    n = got_ref.shape[2]
    whole = pltpu.make_async_copy(obj_ref, out_hbm, sem.at[4])
    whole.start()
    parts = []
    for k in range(4):
        c, at = k // 2, (k % 2) * (n // 2)
        rows_k = pl.ds(k * (n // 2), n // 2)
        for h in range(2):
            wide[rows_k, 128 * h:128 * (h + 1)] = got_ref[c, h, at:at + n // 2].astype(F32)
        part = pltpu.make_async_copy(wide.at[rows_k], grad_hbm.at[rows_k], sem.at[k])
        part.start()
        parts.append(part)
    for part in parts:
        part.wait()
    whole.wait()


def finish_call(obj, got):
    n = got.shape[2]
    V = pl.BlockSpec(memory_space=pltpu.VMEM)
    A = pl.BlockSpec(memory_space=pltpu.HBM)
    return pl.pallas_call(
        finish_kernel,
        out_shape=[jax.ShapeDtypeStruct(obj.shape, F32), jax.ShapeDtypeStruct((2 * n, 256), F32)],
        in_specs=[V, V],
        out_specs=[A, A],
        scratch_shapes=[pltpu.VMEM((2 * n, 256), F32), pltpu.SemaphoreType.DMA((5,))],
        compiler_params=pltpu.CompilerParams(vmem_limit_bytes=16 * 2**20),
        name="finish",
    )(obj, got)


def on_device(object_field, probe, amplitudes, owner, offsets):
    rows, cols = lax.axis_size("row"), lax.axis_size("col")
    held = amplitudes.shape[0]
    most = 4 * (held - 1)
    side, tile = probe.shape[-1], object_field.shape[1]
    ext, meta = pre_call(owner, offsets, object_field, side, rows, cols)
    patch, items = cut_call(meta, ext, tile, rows, cols, held, most)
    placed, grad, power = main_call(items, owner, amplitudes, patch, probe, rows, cols)
    *rims, core = place_call(items, placed, power, tile)
    scale = 1.0 / math.sqrt(rows * cols * held)
    object_out, gradient = post_call(rims, core, object_field, grad, rows, cols, scale)
    object_out, gradient = finish_call(object_out, gradient)
    return (object_out, gradient.reshape(probe.shape))


def solution(mesh):
    return jax.shard_map(
        on_device,
        mesh=mesh,
        in_specs=(
            P(None, "row", "col"),
            P(),
            P(("row", "col"), None, None),
            P(("row", "col")),
            P(("row", "col"), None),
        ),
        out_specs=(P(None, "row", "col"), P()),
        check_vma=False,
    )
```

```python
import functools
import math

import jax
import jax.numpy as jnp
import numpy as np
from jax import lax
from jax.experimental import pallas as pl
from jax.experimental.pallas import tpu as pltpu
from jax.sharding import PartitionSpec as P

F32, BF16 = jnp.float32, jnp.bfloat16
MESH = pl.DeviceIdType.MESH

def tables(side):
    series = np.arange(side, dtype=np.int32)
    angles = (series[:, None] * series[None, :] % side).astype(np.float32) * np.float32(2.0 * math.pi / side)
    factor = np.float32(1.0 / math.sqrt(side))
    re = jnp.asarray(np.cos(angles) * factor).astype(BF16)
    im = jnp.asarray(-np.sin(angles) * factor).astype(BF16)
    return re, im

def dot(a, b):
    return jnp.dot(a, b, preferred_element_type=F32)

def moved_back(w, rows, lanes):
    tall, wide = w.shape
    t = pltpu.roll(w.reshape(tall // 8, 8, wide), lax.rem(8 - rows, 8), 1)
    sub = lax.broadcasted_iota(jnp.int32, (tall // 8 - 1, 8, wide), 1)
    w = jnp.where(sub < 8 - rows, t[:-1], t[1:]).reshape(tall - 8, wide)
    lane = lax.broadcasted_iota(jnp.int32, (tall - 8, 128), 1)
    parts = [pltpu.roll(w[:, k:k + 128], lax.rem(128 - lanes, 128), 1) for k in range(0, wide, 128)]
    return jnp.concatenate([jnp.where(lane < 128 - lanes, a, b) for a, b in zip(parts[:-1], parts[1:])], 1)


def moved_on(w, rows, lanes):
    tall, wide = w.shape
    lane = lax.broadcasted_iota(jnp.int32, (tall, 128), 1)
    none = jnp.zeros((tall, 128), F32)
    parts = [none] + [pltpu.roll(w[:, k:k + 128], lanes, 1) for k in range(0, wide, 128)] + [none]
    w = jnp.concatenate([jnp.where(lane < lanes, a, b) for a, b in zip(parts[:-1], parts[1:])], 1)
    wide += 128
    t = pltpu.roll(w.reshape(tall // 8, 8, wide), rows, 1)
    none = jnp.zeros((1, 8, wide), F32)
    sub = lax.broadcasted_iota(jnp.int32, (tall // 8 + 1, 8, wide), 1)
    both = jnp.where(sub < rows, jnp.concatenate([none, t], 0), jnp.concatenate([t, none], 0))
    return both.reshape(tall + 8, wide)


def around(row, col, dr, dc, rows, cols):
    return lax.rem(row + dr + rows, rows), lax.rem(col + dc + cols, cols)


NEAR = [(dr, dc) for dr in (-1, 0, 1) for dc in (-1, 0, 1) if (dr, dc) != (0, 0)]


def span(step, tile, half):
    return {-1: (0, half), 0: (half, tile), 1: (half + tile, half)}[step]


def landing(step, tile, half):
    return {-1: (tile - half, half), 0: (0, tile), 1: (0, half)}[step]


def column_peers(row, col, cols):
    depth = 4
    steps = [(0, 1), (1, 0), (0, 3), (3, 0), (1, 1), (3, 3), (1, 3), (3, 1), (2, 0), (0, 2), (2, 2), (1, 2), (3, 2), (2, 1), (2, 3)]
    x, z = col // depth, lax.rem(col, depth)
    return [(row, lax.rem(x + dx, cols // depth) * depth + lax.rem(z + dz, depth)) for dx, dz in steps]


class Sends:
    def __init__(self, send_sem, recv_sem):
        self.send_sem, self.recv_sem, self.at, self.all = send_sem, recv_sem, 0, []

    def __call__(self, src, dst, device):
        n = self.at
        self.at += 1
        copy = pltpu.make_async_remote_copy(
            src_ref=src, dst_ref=dst, send_sem=self.send_sem.at[n], recv_sem=self.recv_sem.at[n],
            device_id=device, device_id_type=MESH)
        copy.start()
        self.all.append(copy)
        return copy

    def finish(self):
        for copy in self.all:
            copy.wait_send()


def greet(devices):
    barrier = pltpu.get_barrier_semaphore()
    for device in devices:
        pl.semaphore_signal(barrier, inc=1, device_id=device, device_id_type=MESH)
    pl.semaphore_wait(barrier, len(devices))


def post_kernel(rows, cols, tile, half, scale, rows_ref, cols_ref, corners_ref, core_ref, obj_ref, grad_ref, out_ref, all16,
                wsum, rim_rows, rim_cols, rim_corners, mate, sum_a, sum_b, got_a, got_b, part_a, part_b, got_a2, got_b2, gsend, grecv):
    row, col = lax.axis_index("row"), lax.axis_index("col")
    core, y = lax.rem(row, 2), row // 2
    ys = rows // 2
    other = (row + 1 - 2 * core, col)
    y_peers = [(lax.rem(y + s, ys) * 2 + core, col) for s in range(1, ys)]
    c_peers = column_peers(row, col, cols)
    near = [around(row, col, dr, dc, rows, cols) for dr, dc in NEAR]
    greet([other] + y_peers + c_peers + near)
    send = Sends(gsend, grecv)
    n = grad_ref.shape[0] // 2
    na, nb = n // ys, n // cols
    fin = n // (ys * cols)
    theirs = pl.ds(pl.multiple_of((1 - core) * n, n), n)
    mine = pl.ds(pl.multiple_of(core * n, n), n)
    pair = send(grad_ref.at[theirs], mate, other)
    rim_copies = []

    def place(i, by_rows, by_cols, at_corners):
        dr, dc = NEAR[i]
        if dc == 0:
            return by_rows.at[(dr + 1) // 2]
        if dr == 0:
            return by_cols.at[(dc + 1) // 2]
        return at_corners.at[dr + 1 + (dc + 1) // 2]

    def landed(i):
        return place(i, rim_rows, rim_cols, rim_corners)

    def send_rims(which):
        for i in which:
            rim_copies.append(send(place(i, rows_ref, cols_ref, corners_ref), landed(i), near[i]))

    send_rims([1, 6])
    pair.wait_recv()
    h = grad_ref[mine, :] + mate[...]
    sum_a[...] = h[:, :128]
    sum_b[...] = h[:, 128:]
    y_at = [lax.rem(y + s, ys) for s in range(1, ys)]
    c_at = [peer[1] for peer in c_peers]

    def piece(k, size):
        return pl.ds(pl.multiple_of(k * size, size), size)

    a1 = [send(sum_a.at[piece(y_at[s], na)], got_a.at[s], y_peers[s]) for s in range(ys - 1)]
    b1 = [send(sum_b.at[piece(c_at[s], nb)], got_b.at[s], c_peers[s]) for s in range(cols - 1)]
    for c in a1:
        c.wait_recv()
    tot = sum_a[piece(y, na), :]
    for s in range(ys - 1):
        tot += got_a[s]
    part_a[...] = tot
    a2 = [send(part_a.at[piece(c_at[s], fin)], got_a2.at[s], c_peers[s]) for s in range(cols - 1)]
    for c in b1:
        c.wait_recv()
    tot = sum_b[piece(col, nb), :]
    for s in range(cols - 1):
        tot += got_b[s]
    part_b[...] = tot
    b2 = [send(part_b.at[piece(y_at[s], fin)], got_b2.at[s], y_peers[s]) for s in range(ys - 1)]
    send_rims([3, 4])
    for c in a2:
        c.wait_recv()
    tot = part_a[piece(col, fin), :]
    for s in range(cols - 1):
        tot += got_a2[s]
    at_a = piece(y * cols + col, fin)
    all16[core, 0, at_a, :] = (tot * scale).astype(all16.dtype)
    a3 = [send(all16.at[core, 0, at_a], all16.at[core, 0, at_a], p) for p in c_peers]
    for c in b2:
        c.wait_recv()
    tot = part_b[piece(y, fin), :]
    for s in range(ys - 1):
        tot += got_b2[s]
    at_b = piece(col * ys + y, fin)
    all16[core, 1, at_b, :] = (tot * scale).astype(all16.dtype)
    b3 = [send(all16.at[core, 1, at_b], all16.at[core, 1, at_b], p) for p in y_peers]
    send_rims([0, 2, 5, 7])
    for c in a3:
        c.wait_recv()
    big_a = piece(y, na)
    a4 = [send(all16.at[core, 0, big_a], all16.at[core, 0, big_a], p) for p in y_peers]
    for c in b3:
        c.wait_recv()
    big_b = piece(col, nb)
    b4 = [send(all16.at[core, 1, big_b], all16.at[core, 1, big_b], p) for p in c_peers]
    for c in rim_copies:
        c.wait_recv()
    out_ref[...] = core_ref[0:2]
    wsum[...] = core_ref[2]
    for i, (dr, dc) in enumerate(NEAR):
        r0, rl = landing(dr, tile, half)
        c0, cl = landing(dc, tile, half)
        keep = (row != -1) & (col != -1)
        if dr:
            keep = keep & (row != (0 if dr == 1 else rows - 1))
        if dc:
            keep = keep & (col != (0 if dc == 1 else cols - 1))

        @pl.when(keep)
        def _(i=i, r0=r0, rl=rl, c0=c0, cl=cl):
            for q in range(2):
                out_ref[q, r0:r0 + rl, c0:c0 + cl] += landed(i)[q].astype(F32)
            wsum[r0:r0 + rl, c0:c0 + cl] += landed(i)[2].astype(F32)

    for q in range(2):
        out_ref[q] = obj_ref[q] + out_ref[q] / (wsum[...] + 1.0)
    for c in a4 + b4:
        c.wait_recv()
    last = send(all16.at[core], all16.at[core], other)
    last.wait_recv()
    send.finish()


def post_call(rims, core, obj, grad, rows, cols, scale):
    tile, half = obj.shape[1], rims[0].shape[2]
    total = grad.shape[0]
    ys, n = rows // 2, total // 2
    na, nb, fin = n // ys, n // cols, n // (ys * cols)
    copies = 1 + 8 + 2 * (ys - 1) + 2 * (cols - 1) + 2 * (ys - 1) + 2 * (cols - 1) + 1
    V = pl.BlockSpec(memory_space=pltpu.VMEM)
    return pl.pallas_call(
        functools.partial(post_kernel, rows, cols, tile, half, scale),
        out_shape=[jax.ShapeDtypeStruct(obj.shape, F32), jax.ShapeDtypeStruct((2, 2, n, 128), BF16)],
        in_specs=[V] * 6,
        out_specs=[V, V],
        scratch_shapes=[
            pltpu.VMEM((tile, tile), F32),
            pltpu.VMEM((2, 3, half, tile), BF16),
            pltpu.VMEM((2, 3, tile, half), BF16),
            pltpu.VMEM((4, 3, half, half), BF16),
            pltpu.VMEM((n, 256), F32),
            pltpu.VMEM((n, 128), F32),
            pltpu.VMEM((n, 128), F32),
            pltpu.VMEM((ys - 1, na, 128), F32),
            pltpu.VMEM((cols - 1, nb, 128), F32),
            pltpu.VMEM((na, 128), F32),
            pltpu.VMEM((nb, 128), F32),
            pltpu.VMEM((cols - 1, fin, 128), F32),
            pltpu.VMEM((ys - 1, fin, 128), F32),
            pltpu.SemaphoreType.DMA((copies,)),
            pltpu.SemaphoreType.DMA((copies,)),
        ],
        compiler_params=pltpu.CompilerParams(collective_id=1, has_side_effects=True, vmem_limit_bytes=40 * 2**20),
        name="post",
    )(*rims, core, obj, grad)


def pre_kernel(rows, cols, tile, half, owner_ref, offsets_ref, obj_ref, ext_ref, meta_ref,
               mine, out_rows, out_cols, in_rows, in_cols, in_corners, gsend, grecv, lsem):
    row, col = lax.axis_index("row"), lax.axis_index("col")
    near = [around(row, col, dr, dc, rows, cols) for dr, dc in NEAR]
    c_peers = column_peers(row, col, cols)
    held = owner_ref.shape[0]
    core = pltpu.make_async_copy(obj_ref, ext_ref.at[:, half:half + tile, half:half + tile], lsem.at[0])
    core.start()
    lane = lax.broadcasted_iota(jnp.int32, (1, 128), 1)
    note = jnp.zeros((1, 128), jnp.int32)
    for h in range(held):
        note = jnp.where(lane == h, owner_ref[h], note)
        for k in range(2):
            note = jnp.where(lane == held + 2 * h + k, offsets_ref[h, k], note)
    mine[...] = note
    core.wait()
    lead, end = 16, half + tile

    def code(out, x):
        top = jnp.max(jnp.abs(x), axis=0, keepdims=True)
        power = jnp.floor(jnp.log2(jnp.maximum(top, 1e-30)))
        out[:lead] = jnp.broadcast_to(power, (lead, x.shape[1])).astype(jnp.int32).astype(jnp.int16)
        x = jnp.clip(jnp.round(x * jnp.exp2(14.0 - power)), -32767.0, 32767.0)
        out[lead:] = x.astype(jnp.int32).astype(jnp.int16)

    for q in range(2):
        for k, at in enumerate((half, end - half)):
            code(out_rows.at[k, q], ext_ref[q, at:at + half, half:end])
            code(out_cols.at[k, q], ext_ref[q, half:end, at:at + half])
    greet(c_peers + near)
    send = Sends(gsend, grecv)
    got = []

    def edge(dr, dc):
        if dc == 0:
            return out_rows.at[(dr + 1) // 2]
        if dr == 0:
            return out_cols.at[(dc + 1) // 2]
        at = 0 if dc < 0 else tile - half
        return out_rows.at[(dr + 1) // 2, :, :, at:at + half]

    def landed(dr, dc):
        if dc == 0:
            return in_rows.at[(dr + 1) // 2]
        if dr == 0:
            return in_cols.at[(dc + 1) // 2]
        return in_corners.at[dr + 1 + (dc + 1) // 2]

    for i, (dr, dc) in enumerate(NEAR):
        got.append(send(edge(dr, dc), landed(dr, dc), near[i]))
    for s in range(cols - 1):
        got.append(send(mine, meta_ref.at[col], c_peers[s]))
    own = pltpu.make_async_copy(mine, meta_ref.at[col], lsem.at[1])
    own.start()
    for c in got:
        c.wait_recv()
    own.wait()
    for dr, dc in NEAR:
        tr, rl = span(-dr, tile, half)
        tc, cl = span(-dc, tile, half)
        ref = landed(dr, dc)
        for q in range(2):
            power = ref[q, :lead].astype(jnp.int32).astype(F32)[:1]
            ext_ref[q, tr:tr + rl, tc:tc + cl] = ref[q, lead:].astype(jnp.int32).astype(F32) * jnp.exp2(power - 14.0)
    send.finish()
    big = tile + 2 * half

    @pl.when(row == 0)
    def _():
        ext_ref[:, :half, :] = jnp.zeros((2, half, big), F32)

    @pl.when(row == rows - 1)
    def _():
        ext_ref[:, big - half:, :] = jnp.zeros((2, half, big), F32)

    @pl.when(col == 0)
    def _():
        ext_ref[:, :, :half] = jnp.zeros((2, big, half), F32)

    @pl.when(col == cols - 1)
    def _():
        ext_ref[:, :, big - half:] = jnp.zeros((2, big, half), F32)


def pre_call(owner, offsets, obj, side, rows, cols):
    tile, half = obj.shape[1], side // 2
    big = tile + side
    copies = 8 + cols - 1
    V = pl.BlockSpec(memory_space=pltpu.VMEM)
    S = pl.BlockSpec(memory_space=pltpu.SMEM)
    return pl.pallas_call(
        functools.partial(pre_kernel, rows, cols, tile, half),
        out_shape=[jax.ShapeDtypeStruct((2, big, big), F32), jax.ShapeDtypeStruct((cols, 1, 128), jnp.int32)],
        in_specs=[S, S, pl.BlockSpec(memory_space=pltpu.HBM)],
        out_specs=[V, V],
        scratch_shapes=[
            pltpu.VMEM((1, 128), jnp.int32),
            pltpu.VMEM((2, 2, half + 16, tile), jnp.int16),
            pltpu.VMEM((2, 2, tile + 16, half), jnp.int16),
            pltpu.VMEM((2, 2, half + 16, tile), jnp.int16),
            pltpu.VMEM((2, 2, tile + 16, half), jnp.int16),
            pltpu.VMEM((4, 2, half + 16, half), jnp.int16),
            pltpu.SemaphoreType.DMA((copies,)),
            pltpu.SemaphoreType.DMA((copies,)),
            pltpu.SemaphoreType.DMA((2,)),
        ],
        compiler_params=pltpu.CompilerParams(collective_id=0, has_side_effects=True, vmem_limit_bytes=32 * 2**20),
        name="pre",
    )(owner, offsets, obj)


def cut_kernel(cols, half, held, meta_ref, ext, patch_hbm, list_ref, patch, osem):
    col = lax.axis_index("col")
    side = 2 * half
    tall, wide, most = side + 8, side + 128, list_ref.shape[0]

    def clear(p, carry):
        for k in range(8):
            list_ref[p, k] = 0
        return carry

    lax.fori_loop(0, most, clear, 0)

    def scan(s, count):
        live, r, c = jnp.int32(0), jnp.int32(0), jnp.int32(0)
        for h in range(held):
            hit = meta_ref[s, 0, h] == col
            live = jnp.where(hit, 1, live)
            r = jnp.where(hit, meta_ref[s, 0, held + 2 * h], r)
            c = jnp.where(hit, meta_ref[s, 0, held + 2 * h + 1], c)

        @pl.when((live == 1) & (count < most))
        def _():
            list_ref[count, 0] = 1
            list_ref[count, 1] = s
            list_ref[count, 2] = r // 8
            list_ref[count, 3] = lax.rem(r, 8)
            list_ref[count, 4] = c // 128
            list_ref[count, 5] = lax.rem(c, 128)
        return count + live

    lax.fori_loop(0, cols, scan, 0)

    def out(p):
        return pltpu.make_async_copy(patch.at[p], patch_hbm.at[p], osem.at[p])

    def visit(p, carry):
        @pl.when(list_ref[p, 0] == 1)
        def _():
            r0 = pl.multiple_of(list_ref[p, 2] * 8, 8)
            c0 = pl.multiple_of(list_ref[p, 4] * 128, 128)
            for q in range(2):
                w = ext[q, pl.ds(r0, tall), pl.ds(c0, wide)]
                patch[p, q] = moved_back(w, list_ref[p, 3], list_ref[p, 5])

        @pl.when(list_ref[p, 0] == 0)
        def _():
            patch[p] = jnp.zeros((2, side, side), F32)

        out(p).start()
        return carry

    lax.fori_loop(0, most, visit, 0)

    def drain(p, carry):
        out(p).wait()
        return carry

    lax.fori_loop(0, most, drain, 0)


def cut_call(meta, ext, tile, cols, held, most):
    big = ext.shape[1]
    side = big - tile
    A = pl.BlockSpec(memory_space=pltpu.HBM)
    S = pl.BlockSpec(memory_space=pltpu.SMEM)
    return pl.pallas_call(
        functools.partial(cut_kernel, cols, side // 2, held),
        out_shape=[jax.ShapeDtypeStruct((most, 2, side, side), F32), jax.ShapeDtypeStruct((most, 8), jnp.int32)],
        in_specs=[S, pl.BlockSpec(memory_space=pltpu.VMEM)],
        out_specs=[A, S],
        scratch_shapes=[
            pltpu.VMEM((most, 2, side, side), F32),
            pltpu.SemaphoreType.DMA((most,)),
        ],
        compiler_params=pltpu.CompilerParams(vmem_limit_bytes=47 * 2**20),
        name="cut",
    )(meta, ext)


def main_kernel(rows, cols, list_ref, owner_ref, amp_hbm, patch_hbm, probe_hbm, tab_hbm,
                placed_hbm, grad_ref, pow_ref,
                placed_ref, psem, slots, amps, amp, probe, tab, patch, far, total, ratio, ebuf, hbuf, ssum,
                gsend, grecv, lsem):
    row, col = lax.axis_index("row"), lax.axis_index("col")
    c_peers = column_peers(row, col, cols)
    held, side, modes, most = amp.shape[0], amp.shape[1], probe.shape[0], patch.shape[0]
    local = [
        pltpu.make_async_copy(amp_hbm, amp, lsem.at[0]),
        pltpu.make_async_copy(probe_hbm, probe, lsem.at[1]),
        pltpu.make_async_copy(tab_hbm, tab, lsem.at[2]),
        pltpu.make_async_copy(patch_hbm, patch, lsem.at[3]),
    ]
    for copy in local:
        copy.start()
    greet(c_peers)
    send = Sends(gsend, grecv)
    local[0].wait()
    amp_copies = []
    for s in range(cols):
        to = col if s == 0 else c_peers[s - 1][1]
        which = jnp.int32(0)
        for h in range(1, held):
            which = jnp.where(owner_ref[h] == to, h, which)
        if s == 0:
            amps[col] = amp[which]
        else:
            slots[s] = amp[which]
            amp_copies.append(send(slots.at[s], amps.at[col], c_peers[s - 1]))
    local[1].wait()
    power = jnp.zeros((side, side), F32)
    for m in range(modes):
        power += probe[m, 0] * probe[m, 0] + probe[m, 1] * probe[m, 1]
    pow_ref[...] = power
    grad_ref[...] = jnp.zeros_like(grad_ref)
    ssum[...] = jnp.zeros_like(ssum)
    local[2].wait()
    local[3].wait()

    chunk = hbuf.shape[2] // modes
    chunks = side // chunk

    def left_pass(k, fields, halves):
        for m in range(modes):
            for h in range(2):
                part = dot(tab[k, h * side:(h + 1) * side], fields[m])
                for c in range(chunks):
                    rows_c = slice(c * chunk, (c + 1) * chunk)
                    halves[c, m * chunk:(m + 1) * chunk, h * side:(h + 1) * side] = part[rows_c].astype(BF16)

    def there(p, fields, halves):
        ssum[...] += patch[p, 0] * patch[p, 0] + patch[p, 1] * patch[p, 1]
        for m in range(modes):
            pr, pi = probe[m, 0], probe[m, 1]
            xr, xi = patch[p, 0], patch[p, 1]
            fields[m, :side] = (pr * xr - pi * xi).astype(BF16)
            fields[m, side:] = (pr * xi + pi * xr).astype(BF16)
        left_pass(0, fields, halves)
        for c in range(chunks):
            rows_c = slice(c * chunk, (c + 1) * chunk)
            out = dot(halves[c], tab[1])
            tot = jnp.zeros((chunk, side), F32)
            for m in range(modes):
                one = out[m * chunk:(m + 1) * chunk]
                far[p, m, rows_c] = one
                tot += one[:, :side] * one[:, :side] + one[:, side:] * one[:, side:]
            total[p, rows_c] = tot

    def there_two(k, carry):
        for u in range(2):
            there(2 * k + u, ebuf.at[u], hbuf.at[u])
        return carry

    lax.fori_loop(0, most // 2, there_two, 0)
    for p in range(most - most % 2, most):
        there(p, ebuf.at[0], hbuf.at[0])
    for copy in amp_copies:
        copy.wait_recv()

    def out(p):
        return pltpu.make_async_copy(placed_ref.at[p], placed_hbm.at[p], psem.at[p])

    def drain(p, carry):
        out(p).wait()
        return carry

    def back(p, carry):
        fields, halves = ebuf.at[0], hbuf.at[0]
        ratio[...] = amps[list_ref[p, 1]].astype(F32) * lax.rsqrt(jnp.maximum(total[p], 0.25))
        for m in range(modes):
            fields[m, :side] = (far[p, m, :, :side] * ratio[...]).astype(BF16)
            fields[m, side:] = (far[p, m, :, side:] * ratio[...]).astype(BF16)
        left_pass(2, fields, halves)
        for c in range(chunks):
            rows_c = slice(c * chunk, (c + 1) * chunk)
            ret = dot(halves[c], tab[3])
            xr, xi = patch[p, 0, rows_c], patch[p, 1, rows_c]
            nr, ni = -xr * pow_ref[rows_c], -xi * pow_ref[rows_c]
            for m in range(modes):
                one = ret[m * chunk:(m + 1) * chunk]
                rr, ri = one[:, :side], one[:, side:]
                pr, pi = probe[m, 0, rows_c], probe[m, 1, rows_c]
                nr += pr * rr + pi * ri
                ni += pr * ri - pi * rr
                at_r = 2 * m * side + c * chunk
                at_i = at_r + side
                grad_ref[at_r:at_r + chunk] += xr * rr + xi * ri
                grad_ref[at_i:at_i + chunk] += xr * ri - xi * rr
            placed_ref[p, 0, rows_c] = nr
            placed_ref[p, 1, rows_c] = ni
        out(p).start()
        return carry

    lax.fori_loop(0, most, back, 0)
    for m in range(modes):
        for q in range(2):
            grad_ref[(2 * m + q) * side:(2 * m + q + 1) * side] -= probe[m, q] * ssum[...]
    lax.fori_loop(0, most, drain, 0)
    send.finish()


def main_call(items, owner, amp, patch, probe, rows, cols):
    side, modes, most = amp.shape[1], probe.shape[0], patch.shape[0]
    copies = cols - 1
    tr, ti = tables(side)

    def left(a, b):
        return jnp.concatenate([jnp.concatenate([a, -b], 1), jnp.concatenate([b, a], 1)], 0)

    def right(a, b):
        return jnp.concatenate([jnp.concatenate([a, b], 1), jnp.concatenate([-b, a], 1)], 0)

    tab = jnp.stack([left(tr, ti), right(tr, ti), left(tr, -ti), right(tr, -ti)])
    V = pl.BlockSpec(memory_space=pltpu.VMEM)
    A = pl.BlockSpec(memory_space=pltpu.HBM)
    S = pl.BlockSpec(memory_space=pltpu.SMEM)
    return pl.pallas_call(
        functools.partial(main_kernel, rows, cols),
        out_shape=[
            jax.ShapeDtypeStruct((most, 2, side, side), F32),
            jax.ShapeDtypeStruct((modes * 2 * side, side), F32),
            jax.ShapeDtypeStruct((side, side), F32),
        ],
        in_specs=[S, S, A, A, A, A],
        out_specs=[A, V, V],
        scratch_shapes=[
            pltpu.VMEM((most, 2, side, side), F32),
            pltpu.SemaphoreType.DMA((most,)),
            pltpu.VMEM((cols, side, side), BF16),
            pltpu.VMEM((cols, side, side), BF16),
            pltpu.VMEM(amp.shape, BF16),
            pltpu.VMEM(probe.shape, F32),
            pltpu.VMEM(tab.shape, BF16),
            pltpu.VMEM((most, 2, side, side), F32),
            pltpu.VMEM((most, modes, side, 2 * side), F32),
            pltpu.VMEM((most, side, side), F32),
            pltpu.VMEM((side, side), F32),
            pltpu.VMEM((2, modes, 2 * side, side), BF16),
            pltpu.VMEM((2, 4, modes * side // 4, 2 * side), BF16),
            pltpu.VMEM((side, side), F32),
            pltpu.SemaphoreType.DMA((copies,)),
            pltpu.SemaphoreType.DMA((copies,)),
            pltpu.SemaphoreType.DMA((4,)),
        ],
        compiler_params=pltpu.CompilerParams(collective_id=2, has_side_effects=True, vmem_limit_bytes=62 * 2**20),
        name="main",
    )(items, owner, amp, patch, probe, tab)


def place_kernel(tile, half, list_ref, placed_hbm, pow_ref, rows_ref, cols_ref, corners_ref, core_ref, placed_ref, psem, num):
    side = 2 * half
    big, tall, wide = tile + side, side + 8, side + 128

    def fetch(p):
        return pltpu.make_async_copy(placed_hbm.at[p], placed_ref.at[p], psem.at[p])

    def start(p, carry):
        fetch(p).start()
        return carry

    lax.fori_loop(0, list_ref.shape[0], start, 0)
    num[...] = jnp.zeros_like(num)

    def visit(p, carry):
        fetch(p).wait()

        @pl.when(list_ref[p, 0] == 1)
        def _():
            r0 = pl.multiple_of(list_ref[p, 2] * 8, 8)
            c0 = pl.multiple_of(list_ref[p, 4] * 128, 128)
            for q in range(3):
                w = moved_on(placed_ref[p, q] if q < 2 else pow_ref[...], list_ref[p, 3], list_ref[p, 5])
                num[q, pl.ds(r0, tall), pl.ds(c0, wide)] += w
        return carry

    lax.fori_loop(0, list_ref.shape[0], visit, 0)
    for q in range(3):
        for dr, dc in NEAR:
            r0, rl = span(dr, tile, half)
            c0, cl = span(dc, tile, half)
            rim = num[q, r0:r0 + rl, c0:c0 + cl].astype(BF16)
            if dc == 0:
                rows_ref[(dr + 1) // 2, q] = rim
            elif dr == 0:
                cols_ref[(dc + 1) // 2, q] = rim
            else:
                corners_ref[dr + 1 + (dc + 1) // 2, q] = rim
        core_ref[q] = num[q, half:big - half, half:big - half]


def place_call(items, placed, power, tile):
    side = power.shape[0]
    half = side // 2
    big = tile + side
    V = pl.BlockSpec(memory_space=pltpu.VMEM)
    S = pl.BlockSpec(memory_space=pltpu.SMEM)
    return pl.pallas_call(
        functools.partial(place_kernel, tile, half),
        out_shape=[
            jax.ShapeDtypeStruct((2, 3, half, tile), BF16),
            jax.ShapeDtypeStruct((2, 3, tile, half), BF16),
            jax.ShapeDtypeStruct((4, 3, half, half), BF16),
            jax.ShapeDtypeStruct((3, tile, tile), F32)],
        in_specs=[S, pl.BlockSpec(memory_space=pltpu.HBM), V],
        out_specs=[V, V, V, V],
        scratch_shapes=[
            pltpu.VMEM(placed.shape, F32),
            pltpu.SemaphoreType.DMA((placed.shape[0],)),
            pltpu.VMEM((3, big, big), F32)],
        compiler_params=pltpu.CompilerParams(vmem_limit_bytes=46 * 2**20),
        name="place",
    )(items, placed, power)


def finish_kernel(obj_ref, got_ref, out_hbm, grad_hbm, wide, sem):
    n = got_ref.shape[2]
    whole = pltpu.make_async_copy(obj_ref, out_hbm, sem.at[4])
    whole.start()
    parts = []
    for k in range(4):
        c, at = k // 2, (k % 2) * (n // 2)
        rows_k = pl.ds(k * (n // 2), n // 2)
        for h in range(2):
            wide[rows_k, 128 * h:128 * (h + 1)] = got_ref[c, h, at:at + n // 2].astype(F32)
        part = pltpu.make_async_copy(wide.at[rows_k], grad_hbm.at[rows_k], sem.at[k])
        part.start()
        parts.append(part)
    for part in parts:
        part.wait()
    whole.wait()


def finish_call(obj, got):
    n = got.shape[2]
    V = pl.BlockSpec(memory_space=pltpu.VMEM)
    A = pl.BlockSpec(memory_space=pltpu.HBM)
    return pl.pallas_call(
        finish_kernel,
        out_shape=[jax.ShapeDtypeStruct(obj.shape, F32), jax.ShapeDtypeStruct((2 * n, 256), F32)],
        in_specs=[V, V],
        out_specs=[A, A],
        scratch_shapes=[pltpu.VMEM((2 * n, 256), F32), pltpu.SemaphoreType.DMA((5,))],
        compiler_params=pltpu.CompilerParams(vmem_limit_bytes=16 * 2**20),
        name="finish",
    )(obj, got)


def on_device(object_field, probe, amplitudes, owner, offsets):
    rows, cols = lax.axis_size("row"), lax.axis_size("col")
    held = amplitudes.shape[0]
    most = 4 * (held - 1)
    side, tile = probe.shape[-1], object_field.shape[1]
    ext, meta = pre_call(owner, offsets, object_field, side, rows, cols)
    patch, items = cut_call(meta, ext, tile, cols, held, most)
    placed, grad, power = main_call(items, owner, amplitudes, patch, probe, rows, cols)
    *rims, core = place_call(items, placed, power, tile)
    scale = 1.0 / math.sqrt(rows * cols * held)
    object_out, gradient = post_call(rims, core, object_field, grad, rows, cols, scale)
    object_out, gradient = finish_call(object_out, gradient)
    return (object_out, gradient.reshape(probe.shape))


def solution(mesh):
    return jax.shard_map(
        on_device,
        mesh=mesh,
        in_specs=(
            P(None, "row", "col"),
            P(),
            P(("row", "col"), None, None),
            P(("row", "col")),
            P(("row", "col"), None),
        ),
        out_specs=(P(None, "row", "col"), P()),
        check_vma=False,
    )
```

```python
import functools
import math

import jax
import jax.numpy as jnp
import numpy as np
from jax import lax
from jax.experimental import pallas as pl
from jax.experimental.pallas import tpu as pltpu
from jax.sharding import PartitionSpec as P

F32, BF16 = jnp.float32, jnp.bfloat16
MESH = pl.DeviceIdType.MESH

def tables(side):
    series = np.arange(side, dtype=np.int32)
    angles = (series[:, None] * series[None, :] % side).astype(np.float32) * np.float32(2.0 * math.pi / side)
    factor = np.float32(1.0 / math.sqrt(side))
    re = jnp.asarray(np.cos(angles) * factor).astype(BF16)
    im = jnp.asarray(-np.sin(angles) * factor).astype(BF16)
    return re, im

def dot(a, b):
    return jnp.dot(a, b, preferred_element_type=F32)

def moved_back(w, rows, lanes):
    tall, wide = w.shape
    t = pltpu.roll(w.reshape(tall // 8, 8, wide), lax.rem(8 - rows, 8), 1)
    sub = lax.broadcasted_iota(jnp.int32, (tall // 8 - 1, 8, wide), 1)
    w = jnp.where(sub < 8 - rows, t[:-1], t[1:]).reshape(tall - 8, wide)
    lane = lax.broadcasted_iota(jnp.int32, (tall - 8, 128), 1)
    parts = [pltpu.roll(w[:, k:k + 128], lax.rem(128 - lanes, 128), 1) for k in range(0, wide, 128)]
    return jnp.concatenate([jnp.where(lane < 128 - lanes, a, b) for a, b in zip(parts[:-1], parts[1:])], 1)


def moved_on(w, rows, lanes):
    tall, wide = w.shape
    lane = lax.broadcasted_iota(jnp.int32, (tall, 128), 1)
    none = jnp.zeros((tall, 128), F32)
    parts = [none] + [pltpu.roll(w[:, k:k + 128], lanes, 1) for k in range(0, wide, 128)] + [none]
    w = jnp.concatenate([jnp.where(lane < lanes, a, b) for a, b in zip(parts[:-1], parts[1:])], 1)
    wide += 128
    t = pltpu.roll(w.reshape(tall // 8, 8, wide), rows, 1)
    none = jnp.zeros((1, 8, wide), F32)
    sub = lax.broadcasted_iota(jnp.int32, (tall // 8 + 1, 8, wide), 1)
    both = jnp.where(sub < rows, jnp.concatenate([none, t], 0), jnp.concatenate([t, none], 0))
    return both.reshape(tall + 8, wide)


def around(row, col, dr, dc, rows, cols):
    return lax.rem(row + dr + rows, rows), lax.rem(col + dc + cols, cols)


NEAR = [(dr, dc) for dr in (-1, 0, 1) for dc in (-1, 0, 1) if (dr, dc) != (0, 0)]


def span(step, tile, half):
    return {-1: (0, half), 0: (half, tile), 1: (half + tile, half)}[step]


def landing(step, tile, half):
    return {-1: (tile - half, half), 0: (0, tile), 1: (0, half)}[step]


EARLY = [(1, 0), (3, 0), (2, 0), (2, 1), (2, 3), (2, 2)]
LATE = [(0, 1), (0, 3), (1, 1), (3, 3), (1, 3), (3, 1), (0, 2), (1, 2), (3, 2)]
DEPTH = 4


def stepped(col, cols, step):
    x, z = col // DEPTH, lax.rem(col, DEPTH)
    return lax.rem(x + step[0], cols // DEPTH) * DEPTH + lax.rem(z + step[1], DEPTH)


def column_peers(row, col, cols, steps):
    return [(row, stepped(col, cols, step)) for step in steps]


def senders(col, cols, steps):
    return [stepped(col, cols, (cols // DEPTH - dx, DEPTH - dz)) for dx, dz in steps]


def owned_by(to, owner_ref, held):
    which = jnp.int32(0)
    for h in range(1, held):
        which = jnp.where(owner_ref[h] == to, h, which)
    return which


class Sends:
    def __init__(self, send_sem, recv_sem):
        self.send_sem, self.recv_sem, self.at, self.all = send_sem, recv_sem, 0, []

    def __call__(self, src, dst, device):
        n = self.at
        self.at += 1
        copy = pltpu.make_async_remote_copy(
            src_ref=src, dst_ref=dst, send_sem=self.send_sem.at[n], recv_sem=self.recv_sem.at[n],
            device_id=device, device_id_type=MESH)
        copy.start()
        self.all.append(copy)
        return copy

    def finish(self):
        for copy in self.all:
            copy.wait_send()


def greet(devices):
    barrier = pltpu.get_barrier_semaphore()
    for device in devices:
        pl.semaphore_signal(barrier, inc=1, device_id=device, device_id_type=MESH)
    pl.semaphore_wait(barrier, len(devices))


def post_kernel(rows, cols, tile, half, scale, rows_ref, cols_ref, corners_ref, core_ref, obj_ref, grad_ref, out_ref, all16,
                wsum, rim_rows, rim_cols, rim_corners, mate, sum_a, sum_b, got_a, got_b, part_a, part_b, got_a2, got_b2, gsend, grecv):
    row, col = lax.axis_index("row"), lax.axis_index("col")
    core, y = lax.rem(row, 2), row // 2
    ys = rows // 2
    other = (row + 1 - 2 * core, col)
    y_peers = [(lax.rem(y + s, ys) * 2 + core, col) for s in range(1, ys)]
    c_peers = column_peers(row, col, cols, LATE + EARLY)
    near = [around(row, col, dr, dc, rows, cols) for dr, dc in NEAR]
    greet([other] + y_peers + c_peers + near)
    send = Sends(gsend, grecv)
    n = grad_ref.shape[0] // 2
    na, nb = n // ys, n // cols
    fin = n // (ys * cols)
    theirs = pl.ds(pl.multiple_of((1 - core) * n, n), n)
    mine = pl.ds(pl.multiple_of(core * n, n), n)
    pair = send(grad_ref.at[theirs], mate, other)
    rim_copies = []

    def place(i, by_rows, by_cols, at_corners):
        dr, dc = NEAR[i]
        if dc == 0:
            return by_rows.at[(dr + 1) // 2]
        if dr == 0:
            return by_cols.at[(dc + 1) // 2]
        return at_corners.at[dr + 1 + (dc + 1) // 2]

    def landed(i):
        return place(i, rim_rows, rim_cols, rim_corners)

    def send_rims(which):
        for i in which:
            rim_copies.append(send(place(i, rows_ref, cols_ref, corners_ref), landed(i), near[i]))

    send_rims([1, 6])
    pair.wait_recv()
    h = grad_ref[mine, :] + mate[...]
    sum_a[...] = h[:, :128]
    sum_b[...] = h[:, 128:]
    y_at = [lax.rem(y + s, ys) for s in range(1, ys)]
    c_at = [peer[1] for peer in c_peers]

    def piece(k, size):
        return pl.ds(pl.multiple_of(k * size, size), size)

    a1 = [send(sum_a.at[piece(y_at[s], na)], got_a.at[s], y_peers[s]) for s in range(ys - 1)]
    b1 = [send(sum_b.at[piece(c_at[s], nb)], got_b.at[s], c_peers[s]) for s in range(cols - 1)]
    for c in a1:
        c.wait_recv()
    tot = sum_a[piece(y, na), :]
    for s in range(ys - 1):
        tot += got_a[s]
    part_a[...] = tot
    a2 = [send(part_a.at[piece(c_at[s], fin)], got_a2.at[s], c_peers[s]) for s in range(cols - 1)]
    for c in b1:
        c.wait_recv()
    tot = sum_b[piece(col, nb), :]
    for s in range(cols - 1):
        tot += got_b[s]
    part_b[...] = tot
    b2 = [send(part_b.at[piece(y_at[s], fin)], got_b2.at[s], y_peers[s]) for s in range(ys - 1)]
    send_rims([3, 4])
    for c in a2:
        c.wait_recv()
    tot = part_a[piece(col, fin), :]
    for s in range(cols - 1):
        tot += got_a2[s]
    at_a = piece(y * cols + col, fin)
    all16[core, 0, at_a, :] = (tot * scale).astype(all16.dtype)
    a3 = [send(all16.at[core, 0, at_a], all16.at[core, 0, at_a], p) for p in c_peers]
    for c in b2:
        c.wait_recv()
    tot = part_b[piece(y, fin), :]
    for s in range(ys - 1):
        tot += got_b2[s]
    at_b = piece(col * ys + y, fin)
    all16[core, 1, at_b, :] = (tot * scale).astype(all16.dtype)
    b3 = [send(all16.at[core, 1, at_b], all16.at[core, 1, at_b], p) for p in y_peers]
    send_rims([0, 2, 5, 7])
    for c in a3:
        c.wait_recv()
    big_a = piece(y, na)
    a4 = [send(all16.at[core, 0, big_a], all16.at[core, 0, big_a], p) for p in y_peers]
    for c in b3:
        c.wait_recv()
    big_b = piece(col, nb)
    b4 = [send(all16.at[core, 1, big_b], all16.at[core, 1, big_b], p) for p in c_peers]
    for c in rim_copies:
        c.wait_recv()
    out_ref[...] = core_ref[0:2]
    wsum[...] = core_ref[2]
    for i, (dr, dc) in enumerate(NEAR):
        r0, rl = landing(dr, tile, half)
        c0, cl = landing(dc, tile, half)
        keep = (row != -1) & (col != -1)
        if dr:
            keep = keep & (row != (0 if dr == 1 else rows - 1))
        if dc:
            keep = keep & (col != (0 if dc == 1 else cols - 1))

        @pl.when(keep)
        def _(i=i, r0=r0, rl=rl, c0=c0, cl=cl):
            for q in range(2):
                out_ref[q, r0:r0 + rl, c0:c0 + cl] += landed(i)[q].astype(F32)
            wsum[r0:r0 + rl, c0:c0 + cl] += landed(i)[2].astype(F32)

    for q in range(2):
        out_ref[q] = obj_ref[q] + out_ref[q] / (wsum[...] + 1.0)
    for c in a4 + b4:
        c.wait_recv()
    last = send(all16.at[core], all16.at[core], other)
    last.wait_recv()
    send.finish()


def post_call(rims, core, obj, grad, rows, cols, scale):
    tile, half = obj.shape[1], rims[0].shape[2]
    total = grad.shape[0]
    ys, n = rows // 2, total // 2
    na, nb, fin = n // ys, n // cols, n // (ys * cols)
    copies = 1 + 8 + 2 * (ys - 1) + 2 * (cols - 1) + 2 * (ys - 1) + 2 * (cols - 1) + 1
    V = pl.BlockSpec(memory_space=pltpu.VMEM)
    return pl.pallas_call(
        functools.partial(post_kernel, rows, cols, tile, half, scale),
        out_shape=[jax.ShapeDtypeStruct(obj.shape, F32), jax.ShapeDtypeStruct((2, 2, n, 128), BF16)],
        in_specs=[V] * 6,
        out_specs=[V, V],
        scratch_shapes=[
            pltpu.VMEM((tile, tile), F32),
            pltpu.VMEM((2, 3, half, tile), BF16),
            pltpu.VMEM((2, 3, tile, half), BF16),
            pltpu.VMEM((4, 3, half, half), BF16),
            pltpu.VMEM((n, 256), F32),
            pltpu.VMEM((n, 128), F32),
            pltpu.VMEM((n, 128), F32),
            pltpu.VMEM((ys - 1, na, 128), F32),
            pltpu.VMEM((cols - 1, nb, 128), F32),
            pltpu.VMEM((na, 128), F32),
            pltpu.VMEM((nb, 128), F32),
            pltpu.VMEM((cols - 1, fin, 128), F32),
            pltpu.VMEM((ys - 1, fin, 128), F32),
            pltpu.SemaphoreType.DMA((copies,)),
            pltpu.SemaphoreType.DMA((copies,)),
        ],
        compiler_params=pltpu.CompilerParams(collective_id=1, has_side_effects=True, vmem_limit_bytes=40 * 2**20),
        name="post",
    )(*rims, core, obj, grad)


def pre_kernel(rows, cols, tile, half, owner_ref, offsets_ref, obj_ref, amp_hbm, ext_ref, meta_ref, early_ref,
               amp, slots, mine, out_rows, out_cols, in_rows, in_cols, in_corners, gsend, grecv, lsem):
    row, col = lax.axis_index("row"), lax.axis_index("col")
    near = [around(row, col, dr, dc, rows, cols) for dr, dc in NEAR]
    c_peers = column_peers(row, col, cols, LATE + EARLY)
    held = owner_ref.shape[0]
    core = pltpu.make_async_copy(obj_ref, ext_ref.at[:, half:half + tile, half:half + tile], lsem.at[0])
    core.start()
    own_amp = pltpu.make_async_copy(amp_hbm, amp, lsem.at[2])
    own_amp.start()
    lane = lax.broadcasted_iota(jnp.int32, (1, 128), 1)
    note = jnp.zeros((1, 128), jnp.int32)
    for h in range(held):
        note = jnp.where(lane == h, owner_ref[h], note)
        for k in range(2):
            note = jnp.where(lane == held + 2 * h + k, offsets_ref[h, k], note)
    mine[...] = note
    core.wait()
    lead, end = 16, half + tile

    def code(out, x):
        top = jnp.max(jnp.abs(x), axis=0, keepdims=True)
        power = jnp.floor(jnp.log2(jnp.maximum(top, 1e-30)))
        out[:lead] = jnp.broadcast_to(power, (lead, x.shape[1])).astype(jnp.int32).astype(jnp.int16)
        x = jnp.clip(jnp.round(x * jnp.exp2(14.0 - power)), -32767.0, 32767.0)
        out[lead:] = x.astype(jnp.int32).astype(jnp.int16)

    for q in range(2):
        for k, at in enumerate((half, end - half)):
            code(out_rows.at[k, q], ext_ref[q, at:at + half, half:end])
            code(out_cols.at[k, q], ext_ref[q, half:end, at:at + half])
    greet(c_peers + near)
    send = Sends(gsend, grecv)
    got = []

    def edge(dr, dc):
        if dc == 0:
            return out_rows.at[(dr + 1) // 2]
        if dr == 0:
            return out_cols.at[(dc + 1) // 2]
        at = 0 if dc < 0 else tile - half
        return out_rows.at[(dr + 1) // 2, :, :, at:at + half]

    def landed(dr, dc):
        if dc == 0:
            return in_rows.at[(dr + 1) // 2]
        if dr == 0:
            return in_cols.at[(dc + 1) // 2]
        return in_corners.at[dr + 1 + (dc + 1) // 2]

    for i, (dr, dc) in enumerate(NEAR):
        got.append(send(edge(dr, dc), landed(dr, dc), near[i]))
    for s in range(cols - 1):
        got.append(send(mine, meta_ref.at[col], c_peers[s]))
    own_amp.wait()
    for k, peer in enumerate(column_peers(row, col, cols, EARLY)):
        slots[k] = amp[owned_by(peer[1], owner_ref, held)]
        got.append(send(slots.at[k], early_ref.at[k], peer))
    own = pltpu.make_async_copy(mine, meta_ref.at[col], lsem.at[1])
    own.start()
    for c in got:
        c.wait_recv()
    own.wait()
    for dr, dc in NEAR:
        tr, rl = span(-dr, tile, half)
        tc, cl = span(-dc, tile, half)
        ref = landed(dr, dc)
        for q in range(2):
            power = ref[q, :lead].astype(jnp.int32).astype(F32)[:1]
            ext_ref[q, tr:tr + rl, tc:tc + cl] = ref[q, lead:].astype(jnp.int32).astype(F32) * jnp.exp2(power - 14.0)
    send.finish()
    big = tile + 2 * half

    @pl.when(row == 0)
    def _():
        ext_ref[:, :half, :] = jnp.zeros((2, half, big), F32)

    @pl.when(row == rows - 1)
    def _():
        ext_ref[:, big - half:, :] = jnp.zeros((2, half, big), F32)

    @pl.when(col == 0)
    def _():
        ext_ref[:, :, :half] = jnp.zeros((2, big, half), F32)

    @pl.when(col == cols - 1)
    def _():
        ext_ref[:, :, big - half:] = jnp.zeros((2, big, half), F32)


def pre_call(owner, offsets, obj, amp, rows, cols):
    side, early = amp.shape[1], len(EARLY)
    tile, half = obj.shape[1], side // 2
    big = tile + side
    copies = 8 + cols - 1 + early
    V = pl.BlockSpec(memory_space=pltpu.VMEM)
    S = pl.BlockSpec(memory_space=pltpu.SMEM)
    return pl.pallas_call(
        functools.partial(pre_kernel, rows, cols, tile, half),
        out_shape=[
            jax.ShapeDtypeStruct((2, big, big), F32), jax.ShapeDtypeStruct((cols, 1, 128), jnp.int32),
            jax.ShapeDtypeStruct((early, side, side), BF16),
        ],
        in_specs=[S, S, pl.BlockSpec(memory_space=pltpu.HBM), pl.BlockSpec(memory_space=pltpu.HBM)],
        out_specs=[V, V, V],
        scratch_shapes=[
            pltpu.VMEM(amp.shape, BF16),
            pltpu.VMEM((early, side, side), BF16),
            pltpu.VMEM((1, 128), jnp.int32),
            pltpu.VMEM((2, 2, half + 16, tile), jnp.int16),
            pltpu.VMEM((2, 2, tile + 16, half), jnp.int16),
            pltpu.VMEM((2, 2, half + 16, tile), jnp.int16),
            pltpu.VMEM((2, 2, tile + 16, half), jnp.int16),
            pltpu.VMEM((4, 2, half + 16, half), jnp.int16),
            pltpu.SemaphoreType.DMA((copies,)),
            pltpu.SemaphoreType.DMA((copies,)),
            pltpu.SemaphoreType.DMA((3,)),
        ],
        compiler_params=pltpu.CompilerParams(collective_id=0, has_side_effects=True, vmem_limit_bytes=32 * 2**20),
        name="pre",
    )(owner, offsets, obj, amp)


def cut_kernel(cols, half, held, meta_ref, ext, patch_hbm, list_ref, patch, osem):
    col = lax.axis_index("col")
    side = 2 * half
    tall, wide, most = side + 8, side + 128, list_ref.shape[0]

    def clear(p, carry):
        for k in range(8):
            list_ref[p, k] = 0
        return carry

    lax.fori_loop(0, most, clear, 0)

    def scan(s, count):
        live, r, c = jnp.int32(0), jnp.int32(0), jnp.int32(0)
        for h in range(held):
            hit = meta_ref[s, 0, h] == col
            live = jnp.where(hit, 1, live)
            r = jnp.where(hit, meta_ref[s, 0, held + 2 * h], r)
            c = jnp.where(hit, meta_ref[s, 0, held + 2 * h + 1], c)

        @pl.when((live == 1) & (count < most))
        def _():
            list_ref[count, 0] = 1
            list_ref[count, 1] = s
            list_ref[count, 2] = r // 8
            list_ref[count, 3] = lax.rem(r, 8)
            list_ref[count, 4] = c // 128
            list_ref[count, 5] = lax.rem(c, 128)
        return count + live

    lax.fori_loop(0, cols, scan, 0)

    def out(p):
        return pltpu.make_async_copy(patch.at[p], patch_hbm.at[p], osem.at[p])

    def visit(p, carry):
        @pl.when(list_ref[p, 0] == 1)
        def _():
            r0 = pl.multiple_of(list_ref[p, 2] * 8, 8)
            c0 = pl.multiple_of(list_ref[p, 4] * 128, 128)
            for q in range(2):
                w = ext[q, pl.ds(r0, tall), pl.ds(c0, wide)]
                patch[p, q] = moved_back(w, list_ref[p, 3], list_ref[p, 5])

        @pl.when(list_ref[p, 0] == 0)
        def _():
            patch[p] = jnp.zeros((2, side, side), F32)

        out(p).start()
        return carry

    lax.fori_loop(0, most, visit, 0)

    def drain(p, carry):
        out(p).wait()
        return carry

    lax.fori_loop(0, most, drain, 0)


def cut_call(meta, ext, tile, cols, held, most):
    big = ext.shape[1]
    side = big - tile
    A = pl.BlockSpec(memory_space=pltpu.HBM)
    S = pl.BlockSpec(memory_space=pltpu.SMEM)
    return pl.pallas_call(
        functools.partial(cut_kernel, cols, side // 2, held),
        out_shape=[jax.ShapeDtypeStruct((most, 2, side, side), F32), jax.ShapeDtypeStruct((most, 8), jnp.int32)],
        in_specs=[S, pl.BlockSpec(memory_space=pltpu.VMEM)],
        out_specs=[A, S],
        scratch_shapes=[
            pltpu.VMEM((most, 2, side, side), F32),
            pltpu.SemaphoreType.DMA((most,)),
        ],
        compiler_params=pltpu.CompilerParams(vmem_limit_bytes=47 * 2**20),
        name="cut",
    )(meta, ext)


def main_kernel(rows, cols, list_ref, owner_ref, amp_hbm, early_hbm, patch_hbm, probe_hbm, tab_hbm,
                placed_hbm, grad_ref, pow_ref,
                placed_ref, psem, slots, amps, amp, probe, tab, patch, far, total, ratio, ebuf, hbuf, ssum,
                gsend, grecv, lsem):
    row, col = lax.axis_index("row"), lax.axis_index("col")
    c_peers = column_peers(row, col, cols, LATE)
    held, side, modes, most = amp.shape[0], amp.shape[1], probe.shape[0], patch.shape[0]
    local = [
        pltpu.make_async_copy(amp_hbm, amp, lsem.at[0]),
        pltpu.make_async_copy(probe_hbm, probe, lsem.at[1]),
        pltpu.make_async_copy(tab_hbm, tab, lsem.at[2]),
        pltpu.make_async_copy(patch_hbm, patch, lsem.at[3]),
    ]
    for copy in local:
        copy.start()
    early = [
        pltpu.make_async_copy(early_hbm.at[k], amps.at[at], lsem.at[4 + k])
        for k, at in enumerate(senders(col, cols, EARLY))
    ]
    for copy in early:
        copy.start()
    greet(c_peers)
    send = Sends(gsend, grecv)
    local[0].wait()
    amp_copies = []
    for k, peer in enumerate(c_peers):
        slots[k] = amp[owned_by(peer[1], owner_ref, held)]
        amp_copies.append(send(slots.at[k], amps.at[col], peer))
    amps[col] = amp[owned_by(col, owner_ref, held)]
    local[1].wait()
    power = jnp.zeros((side, side), F32)
    for m in range(modes):
        power += probe[m, 0] * probe[m, 0] + probe[m, 1] * probe[m, 1]
    pow_ref[...] = power
    grad_ref[...] = jnp.zeros_like(grad_ref)
    ssum[...] = jnp.zeros_like(ssum)
    local[2].wait()
    local[3].wait()

    chunk = hbuf.shape[2] // modes
    chunks = side // chunk

    def left_pass(k, fields, halves):
        for m in range(modes):
            for h in range(2):
                part = dot(tab[k, h * side:(h + 1) * side], fields[m])
                for c in range(chunks):
                    rows_c = slice(c * chunk, (c + 1) * chunk)
                    halves[c, m * chunk:(m + 1) * chunk, h * side:(h + 1) * side] = part[rows_c].astype(BF16)

    def there(p, fields, halves):
        ssum[...] += patch[p, 0] * patch[p, 0] + patch[p, 1] * patch[p, 1]
        for m in range(modes):
            pr, pi = probe[m, 0], probe[m, 1]
            xr, xi = patch[p, 0], patch[p, 1]
            fields[m, :side] = (pr * xr - pi * xi).astype(BF16)
            fields[m, side:] = (pr * xi + pi * xr).astype(BF16)
        left_pass(0, fields, halves)
        for c in range(chunks):
            rows_c = slice(c * chunk, (c + 1) * chunk)
            out = dot(halves[c], tab[1])
            tot = jnp.zeros((chunk, side), F32)
            for m in range(modes):
                one = out[m * chunk:(m + 1) * chunk]
                far[p, m, rows_c] = one
                tot += one[:, :side] * one[:, :side] + one[:, side:] * one[:, side:]
            total[p, rows_c] = tot

    def there_two(k, carry):
        for u in range(2):
            there(2 * k + u, ebuf.at[u], hbuf.at[u])
        return carry

    lax.fori_loop(0, most // 2, there_two, 0)
    for p in range(most - most % 2, most):
        there(p, ebuf.at[0], hbuf.at[0])
    for copy in amp_copies:
        copy.wait_recv()
    for copy in early:
        copy.wait()

    def out(p):
        return pltpu.make_async_copy(placed_ref.at[p], placed_hbm.at[p], psem.at[p])

    def drain(p, carry):
        out(p).wait()
        return carry

    def back(p, carry):
        fields, halves = ebuf.at[0], hbuf.at[0]
        ratio[...] = amps[list_ref[p, 1]].astype(F32) * lax.rsqrt(jnp.maximum(total[p], 0.25))
        for m in range(modes):
            fields[m, :side] = (far[p, m, :, :side] * ratio[...]).astype(BF16)
            fields[m, side:] = (far[p, m, :, side:] * ratio[...]).astype(BF16)
        left_pass(2, fields, halves)
        for c in range(chunks):
            rows_c = slice(c * chunk, (c + 1) * chunk)
            ret = dot(halves[c], tab[3])
            xr, xi = patch[p, 0, rows_c], patch[p, 1, rows_c]
            nr, ni = -xr * pow_ref[rows_c], -xi * pow_ref[rows_c]
            for m in range(modes):
                one = ret[m * chunk:(m + 1) * chunk]
                rr, ri = one[:, :side], one[:, side:]
                pr, pi = probe[m, 0, rows_c], probe[m, 1, rows_c]
                nr += pr * rr + pi * ri
                ni += pr * ri - pi * rr
                at_r = 2 * m * side + c * chunk
                at_i = at_r + side
                grad_ref[at_r:at_r + chunk] += xr * rr + xi * ri
                grad_ref[at_i:at_i + chunk] += xr * ri - xi * rr
            placed_ref[p, 0, rows_c] = nr
            placed_ref[p, 1, rows_c] = ni
        out(p).start()
        return carry

    lax.fori_loop(0, most, back, 0)
    for m in range(modes):
        for q in range(2):
            grad_ref[(2 * m + q) * side:(2 * m + q + 1) * side] -= probe[m, q] * ssum[...]
    lax.fori_loop(0, most, drain, 0)
    send.finish()


def main_call(items, owner, amp, early, patch, probe, rows, cols):
    side, modes, most = amp.shape[1], probe.shape[0], patch.shape[0]
    copies = len(LATE)
    tr, ti = tables(side)

    def left(a, b):
        return jnp.concatenate([jnp.concatenate([a, -b], 1), jnp.concatenate([b, a], 1)], 0)

    def right(a, b):
        return jnp.concatenate([jnp.concatenate([a, b], 1), jnp.concatenate([-b, a], 1)], 0)

    tab = jnp.stack([left(tr, ti), right(tr, ti), left(tr, -ti), right(tr, -ti)])
    V = pl.BlockSpec(memory_space=pltpu.VMEM)
    A = pl.BlockSpec(memory_space=pltpu.HBM)
    S = pl.BlockSpec(memory_space=pltpu.SMEM)
    return pl.pallas_call(
        functools.partial(main_kernel, rows, cols),
        out_shape=[
            jax.ShapeDtypeStruct((most, 2, side, side), F32),
            jax.ShapeDtypeStruct((modes * 2 * side, side), F32),
            jax.ShapeDtypeStruct((side, side), F32),
        ],
        in_specs=[S, S, A, A, A, A, A],
        out_specs=[A, V, V],
        scratch_shapes=[
            pltpu.VMEM((most, 2, side, side), F32),
            pltpu.SemaphoreType.DMA((most,)),
            pltpu.VMEM((copies, side, side), BF16),
            pltpu.VMEM((cols, side, side), BF16),
            pltpu.VMEM(amp.shape, BF16),
            pltpu.VMEM(probe.shape, F32),
            pltpu.VMEM(tab.shape, BF16),
            pltpu.VMEM((most, 2, side, side), F32),
            pltpu.VMEM((most, modes, side, 2 * side), F32),
            pltpu.VMEM((most, side, side), F32),
            pltpu.VMEM((side, side), F32),
            pltpu.VMEM((2, modes, 2 * side, side), BF16),
            pltpu.VMEM((2, 4, modes * side // 4, 2 * side), BF16),
            pltpu.VMEM((side, side), F32),
            pltpu.SemaphoreType.DMA((copies,)),
            pltpu.SemaphoreType.DMA((copies,)),
            pltpu.SemaphoreType.DMA((4 + len(EARLY),)),
        ],
        compiler_params=pltpu.CompilerParams(collective_id=2, has_side_effects=True, vmem_limit_bytes=62 * 2**20),
        name="main",
    )(items, owner, amp, early, patch, probe, tab)


def place_kernel(tile, half, list_ref, placed_hbm, pow_ref, rows_ref, cols_ref, corners_ref, core_ref, placed_ref, psem, num):
    side = 2 * half
    big, tall, wide = tile + side, side + 8, side + 128

    def fetch(p):
        return pltpu.make_async_copy(placed_hbm.at[p], placed_ref.at[p], psem.at[p])

    def start(p, carry):
        fetch(p).start()
        return carry

    lax.fori_loop(0, list_ref.shape[0], start, 0)
    num[...] = jnp.zeros_like(num)

    def visit(p, carry):
        fetch(p).wait()

        @pl.when(list_ref[p, 0] == 1)
        def _():
            r0 = pl.multiple_of(list_ref[p, 2] * 8, 8)
            c0 = pl.multiple_of(list_ref[p, 4] * 128, 128)
            for q in range(3):
                w = moved_on(placed_ref[p, q] if q < 2 else pow_ref[...], list_ref[p, 3], list_ref[p, 5])
                num[q, pl.ds(r0, tall), pl.ds(c0, wide)] += w
        return carry

    lax.fori_loop(0, list_ref.shape[0], visit, 0)
    for q in range(3):
        for dr, dc in NEAR:
            r0, rl = span(dr, tile, half)
            c0, cl = span(dc, tile, half)
            rim = num[q, r0:r0 + rl, c0:c0 + cl].astype(BF16)
            if dc == 0:
                rows_ref[(dr + 1) // 2, q] = rim
            elif dr == 0:
                cols_ref[(dc + 1) // 2, q] = rim
            else:
                corners_ref[dr + 1 + (dc + 1) // 2, q] = rim
        core_ref[q] = num[q, half:big - half, half:big - half]


def place_call(items, placed, power, tile):
    side = power.shape[0]
    half = side // 2
    big = tile + side
    V = pl.BlockSpec(memory_space=pltpu.VMEM)
    S = pl.BlockSpec(memory_space=pltpu.SMEM)
    return pl.pallas_call(
        functools.partial(place_kernel, tile, half),
        out_shape=[
            jax.ShapeDtypeStruct((2, 3, half, tile), BF16),
            jax.ShapeDtypeStruct((2, 3, tile, half), BF16),
            jax.ShapeDtypeStruct((4, 3, half, half), BF16),
            jax.ShapeDtypeStruct((3, tile, tile), F32)],
        in_specs=[S, pl.BlockSpec(memory_space=pltpu.HBM), V],
        out_specs=[V, V, V, V],
        scratch_shapes=[
            pltpu.VMEM(placed.shape, F32),
            pltpu.SemaphoreType.DMA((placed.shape[0],)),
            pltpu.VMEM((3, big, big), F32)],
        compiler_params=pltpu.CompilerParams(vmem_limit_bytes=46 * 2**20),
        name="place",
    )(items, placed, power)


def finish_kernel(obj_ref, got_ref, out_hbm, grad_hbm, wide, sem):
    n = got_ref.shape[2]
    whole = pltpu.make_async_copy(obj_ref, out_hbm, sem.at[4])
    whole.start()
    parts = []
    for k in range(4):
        c, at = k // 2, (k % 2) * (n // 2)
        rows_k = pl.ds(k * (n // 2), n // 2)
        for h in range(2):
            wide[rows_k, 128 * h:128 * (h + 1)] = got_ref[c, h, at:at + n // 2].astype(F32)
        part = pltpu.make_async_copy(wide.at[rows_k], grad_hbm.at[rows_k], sem.at[k])
        part.start()
        parts.append(part)
    for part in parts:
        part.wait()
    whole.wait()


def finish_call(obj, got):
    n = got.shape[2]
    V = pl.BlockSpec(memory_space=pltpu.VMEM)
    A = pl.BlockSpec(memory_space=pltpu.HBM)
    return pl.pallas_call(
        finish_kernel,
        out_shape=[jax.ShapeDtypeStruct(obj.shape, F32), jax.ShapeDtypeStruct((2 * n, 256), F32)],
        in_specs=[V, V],
        out_specs=[A, A],
        scratch_shapes=[pltpu.VMEM((2 * n, 256), F32), pltpu.SemaphoreType.DMA((5,))],
        compiler_params=pltpu.CompilerParams(vmem_limit_bytes=16 * 2**20),
        name="finish",
    )(obj, got)


def on_device(object_field, probe, amplitudes, owner, offsets):
    rows, cols = lax.axis_size("row"), lax.axis_size("col")
    held = amplitudes.shape[0]
    most = 4 * (held - 1)
    tile = object_field.shape[1]
    ext, meta, early = pre_call(owner, offsets, object_field, amplitudes, rows, cols)
    patch, items = cut_call(meta, ext, tile, cols, held, most)
    placed, grad, power = main_call(items, owner, amplitudes, early, patch, probe, rows, cols)
    *rims, core = place_call(items, placed, power, tile)
    scale = 1.0 / math.sqrt(rows * cols * held)
    object_out, gradient = post_call(rims, core, object_field, grad, rows, cols, scale)
    object_out, gradient = finish_call(object_out, gradient)
    return (object_out, gradient.reshape(probe.shape))


def solution(mesh):
    return jax.shard_map(
        on_device,
        mesh=mesh,
        in_specs=(
            P(None, "row", "col"),
            P(),
            P(("row", "col"), None, None),
            P(("row", "col")),
            P(("row", "col"), None),
        ),
        out_specs=(P(None, "row", "col"), P()),
        check_vma=False,
    )
```

```python
import functools
import math

import jax
import jax.numpy as jnp
import numpy as np
from jax import lax
from jax.experimental import pallas as pl
from jax.experimental.pallas import tpu as pltpu
from jax.sharding import PartitionSpec as P

F32, BF16 = jnp.float32, jnp.bfloat16
MESH = pl.DeviceIdType.MESH

def tables(side):
    series = np.arange(side, dtype=np.int32)
    angles = (series[:, None] * series[None, :] % side).astype(np.float32) * np.float32(2.0 * math.pi / side)
    factor = np.float32(1.0 / math.sqrt(side))
    re = jnp.asarray(np.cos(angles) * factor).astype(BF16)
    im = jnp.asarray(-np.sin(angles) * factor).astype(BF16)
    return re, im

def dot(a, b):
    return jnp.dot(a, b, preferred_element_type=F32)

def moved_back(w, rows, lanes):
    tall, wide = w.shape
    t = pltpu.roll(w.reshape(tall // 8, 8, wide), lax.rem(8 - rows, 8), 1)
    sub = lax.broadcasted_iota(jnp.int32, (tall // 8 - 1, 8, wide), 1)
    w = jnp.where(sub < 8 - rows, t[:-1], t[1:]).reshape(tall - 8, wide)
    lane = lax.broadcasted_iota(jnp.int32, (tall - 8, 128), 1)
    parts = [pltpu.roll(w[:, k:k + 128], lax.rem(128 - lanes, 128), 1) for k in range(0, wide, 128)]
    return jnp.concatenate([jnp.where(lane < 128 - lanes, a, b) for a, b in zip(parts[:-1], parts[1:])], 1)


def moved_on(w, rows, lanes):
    tall, wide = w.shape
    lane = lax.broadcasted_iota(jnp.int32, (tall, 128), 1)
    none = jnp.zeros((tall, 128), F32)
    parts = [none] + [pltpu.roll(w[:, k:k + 128], lanes, 1) for k in range(0, wide, 128)] + [none]
    w = jnp.concatenate([jnp.where(lane < lanes, a, b) for a, b in zip(parts[:-1], parts[1:])], 1)
    wide += 128
    t = pltpu.roll(w.reshape(tall // 8, 8, wide), rows, 1)
    none = jnp.zeros((1, 8, wide), F32)
    sub = lax.broadcasted_iota(jnp.int32, (tall // 8 + 1, 8, wide), 1)
    both = jnp.where(sub < rows, jnp.concatenate([none, t], 0), jnp.concatenate([t, none], 0))
    return both.reshape(tall + 8, wide)


def around(row, col, dr, dc, rows, cols):
    return lax.rem(row + dr + rows, rows), lax.rem(col + dc + cols, cols)


NEAR = [(dr, dc) for dr in (-1, 0, 1) for dc in (-1, 0, 1) if (dr, dc) != (0, 0)]


def span(step, tile, half):
    return {-1: (0, half), 0: (half, tile), 1: (half + tile, half)}[step]


def landing(step, tile, half):
    return {-1: (tile - half, half), 0: (0, tile), 1: (0, half)}[step]


def column_peers(row, col, cols):
    depth = 4
    steps = [(0, 1), (1, 0), (0, 3), (3, 0), (1, 1), (3, 3), (1, 3), (3, 1), (2, 0), (0, 2), (2, 2), (1, 2), (3, 2), (2, 1), (2, 3)]
    x, z = col // depth, lax.rem(col, depth)
    return [(row, lax.rem(x + dx, cols // depth) * depth + lax.rem(z + dz, depth)) for dx, dz in steps]


LEAD = 16


def power_of(x):
    top = jnp.max(jnp.abs(x), axis=0, keepdims=True)
    return jnp.floor(jnp.log2(jnp.maximum(top, 1e-30)))


def code(out, x, power=None):
    power = power_of(x) if power is None else power
    out[:LEAD] = jnp.broadcast_to(power, (LEAD, x.shape[1])).astype(jnp.int32).astype(jnp.int16)
    x = jnp.clip(jnp.round(x * jnp.exp2(14.0 - power)), -32767.0, 32767.0)
    out[LEAD:] = x.astype(jnp.int32).astype(jnp.int16)


def decoded(ref):
    power = ref[:LEAD].astype(jnp.int32).astype(F32)[:1]
    return ref[LEAD:].astype(jnp.int32).astype(F32) * jnp.exp2(power - 14.0)


def code_pieces(out, ref):
    power = power_of(ref[...])
    size = ref.shape[0] // out.shape[0]
    for k in range(out.shape[0]):
        code(out.at[k], ref[k * size:(k + 1) * size], power)


class Sends:
    def __init__(self, send_sem, recv_sem):
        self.send_sem, self.recv_sem, self.at, self.all = send_sem, recv_sem, 0, []

    def __call__(self, src, dst, device):
        n = self.at
        self.at += 1
        copy = pltpu.make_async_remote_copy(
            src_ref=src, dst_ref=dst, send_sem=self.send_sem.at[n], recv_sem=self.recv_sem.at[n],
            device_id=device, device_id_type=MESH)
        copy.start()
        self.all.append(copy)
        return copy

    def finish(self):
        for copy in self.all:
            copy.wait_send()


def greet(devices):
    barrier = pltpu.get_barrier_semaphore()
    for device in devices:
        pl.semaphore_signal(barrier, inc=1, device_id=device, device_id_type=MESH)
    pl.semaphore_wait(barrier, len(devices))


def post_kernel(rows, cols, tile, half, scale, rows_ref, cols_ref, corners_ref, core_ref, obj_ref, grad_ref, out_ref, all16,
                wsum, rim_rows, rim_cols, rim_corners, mate, sum_a, sum_b, got_a, got_b, part_a, part_b, got_a2, got_b2,
                code_a, code_b, gsend, grecv):
    row, col = lax.axis_index("row"), lax.axis_index("col")
    core, y = lax.rem(row, 2), row // 2
    ys = rows // 2
    other = (row + 1 - 2 * core, col)
    y_peers = [(lax.rem(y + s, ys) * 2 + core, col) for s in range(1, ys)]
    c_peers = column_peers(row, col, cols)
    near = [around(row, col, dr, dc, rows, cols) for dr, dc in NEAR]
    greet([other] + y_peers + c_peers + near)
    send = Sends(gsend, grecv)
    n = grad_ref.shape[0] // 2
    na, nb = n // ys, n // cols
    fin = n // (ys * cols)
    theirs = pl.ds(pl.multiple_of((1 - core) * n, n), n)
    mine = pl.ds(pl.multiple_of(core * n, n), n)
    pair = send(grad_ref.at[theirs], mate, other)
    rim_copies = []

    def place(i, by_rows, by_cols, at_corners):
        dr, dc = NEAR[i]
        if dc == 0:
            return by_rows.at[(dr + 1) // 2]
        if dr == 0:
            return by_cols.at[(dc + 1) // 2]
        return at_corners.at[dr + 1 + (dc + 1) // 2]

    def landed(i):
        return place(i, rim_rows, rim_cols, rim_corners)

    def send_rims(which):
        for i in which:
            rim_copies.append(send(place(i, rows_ref, cols_ref, corners_ref), landed(i), near[i]))

    send_rims([1, 6, 3, 4])
    pair.wait_recv()
    sum_a[...] = grad_ref[mine, :128] + mate[:, :128]
    sum_b[...] = grad_ref[mine, 128:] + mate[:, 128:]
    code_pieces(code_a, sum_a)
    code_pieces(code_b, sum_b)
    y_at = [lax.rem(y + s, ys) for s in range(1, ys)]
    c_at = [peer[1] for peer in c_peers]

    def piece(k, size):
        return pl.ds(pl.multiple_of(k * size, size), size)

    a1 = [send(code_a.at[y_at[s]], got_a.at[s], y_peers[s]) for s in range(ys - 1)]
    b1 = [send(code_b.at[c_at[s]], got_b.at[s], c_peers[s]) for s in range(cols - 1)]
    for c in a1:
        c.wait_recv()
    tot = sum_a[piece(y, na), :]
    for s in range(ys - 1):
        tot += decoded(got_a.at[s])
    part_a[...] = tot
    a2 = [send(part_a.at[piece(c_at[s], fin)], got_a2.at[s], c_peers[s]) for s in range(cols - 1)]
    for c in b1:
        c.wait_recv()
    tot = sum_b[piece(col, nb), :]
    for s in range(cols - 1):
        tot += decoded(got_b.at[s])
    part_b[...] = tot
    b2 = [send(part_b.at[piece(y_at[s], fin)], got_b2.at[s], y_peers[s]) for s in range(ys - 1)]
    send_rims([0, 2, 5, 7])
    for c in a2:
        c.wait_recv()
    tot = part_a[piece(col, fin), :]
    for s in range(cols - 1):
        tot += got_a2[s]
    at_a = piece(y * cols + col, fin)
    all16[core, 0, at_a, :] = (tot * scale).astype(all16.dtype)
    a3 = [send(all16.at[core, 0, at_a], all16.at[core, 0, at_a], p) for p in c_peers]
    for c in b2:
        c.wait_recv()
    tot = part_b[piece(y, fin), :]
    for s in range(ys - 1):
        tot += got_b2[s]
    at_b = piece(col * ys + y, fin)
    all16[core, 1, at_b, :] = (tot * scale).astype(all16.dtype)
    b3 = [send(all16.at[core, 1, at_b], all16.at[core, 1, at_b], p) for p in y_peers]
    for c in a3:
        c.wait_recv()
    big_a = piece(y, na)
    a4 = [send(all16.at[core, 0, big_a], all16.at[core, 0, big_a], p) for p in y_peers]
    for c in b3:
        c.wait_recv()
    big_b = piece(col, nb)
    b4 = [send(all16.at[core, 1, big_b], all16.at[core, 1, big_b], p) for p in c_peers]
    for c in a4 + b4:
        c.wait_recv()
    last = send(all16.at[core], all16.at[core], other)
    for c in rim_copies:
        c.wait_recv()
    out_ref[...] = core_ref[0:2]
    wsum[...] = core_ref[2]
    for i, (dr, dc) in enumerate(NEAR):
        r0, rl = landing(dr, tile, half)
        c0, cl = landing(dc, tile, half)
        keep = (row != -1) & (col != -1)
        if dr:
            keep = keep & (row != (0 if dr == 1 else rows - 1))
        if dc:
            keep = keep & (col != (0 if dc == 1 else cols - 1))

        @pl.when(keep)
        def _(i=i, r0=r0, rl=rl, c0=c0, cl=cl):
            for q in range(2):
                out_ref[q, r0:r0 + rl, c0:c0 + cl] += landed(i)[q].astype(F32)
            wsum[r0:r0 + rl, c0:c0 + cl] += landed(i)[2].astype(F32)

    for q in range(2):
        out_ref[q] = obj_ref[q] + out_ref[q] / (wsum[...] + 1.0)
    last.wait_recv()
    send.finish()


def post_call(rims, core, obj, grad, rows, cols, scale):
    tile, half = obj.shape[1], rims[0].shape[2]
    total = grad.shape[0]
    ys, n = rows // 2, total // 2
    na, nb, fin = n // ys, n // cols, n // (ys * cols)
    copies = 1 + 8 + 2 * (ys - 1) + 2 * (cols - 1) + 2 * (ys - 1) + 2 * (cols - 1) + 1
    V = pl.BlockSpec(memory_space=pltpu.VMEM)
    return pl.pallas_call(
        functools.partial(post_kernel, rows, cols, tile, half, scale),
        out_shape=[jax.ShapeDtypeStruct(obj.shape, F32), jax.ShapeDtypeStruct((2, 2, n, 128), BF16)],
        in_specs=[V] * 6,
        out_specs=[V, V],
        scratch_shapes=[
            pltpu.VMEM((tile, tile), F32),
            pltpu.VMEM((2, 3, half, tile), BF16),
            pltpu.VMEM((2, 3, tile, half), BF16),
            pltpu.VMEM((4, 3, half, half), BF16),
            pltpu.VMEM((n, 256), F32),
            pltpu.VMEM((n, 128), F32),
            pltpu.VMEM((n, 128), F32),
            pltpu.VMEM((ys - 1, LEAD + na, 128), jnp.int16),
            pltpu.VMEM((cols - 1, LEAD + nb, 128), jnp.int16),
            pltpu.VMEM((na, 128), F32),
            pltpu.VMEM((nb, 128), F32),
            pltpu.VMEM((cols - 1, fin, 128), F32),
            pltpu.VMEM((ys - 1, fin, 128), F32),
            pltpu.VMEM((ys, LEAD + na, 128), jnp.int16),
            pltpu.VMEM((cols, LEAD + nb, 128), jnp.int16),
            pltpu.SemaphoreType.DMA((copies,)),
            pltpu.SemaphoreType.DMA((copies,)),
        ],
        compiler_params=pltpu.CompilerParams(collective_id=1, has_side_effects=True, vmem_limit_bytes=40 * 2**20),
        name="post",
    )(*rims, core, obj, grad)


def pre_kernel(rows, cols, tile, half, owner_ref, offsets_ref, obj_ref, ext_ref, meta_ref,
               mine, out_rows, out_cols, in_rows, in_cols, in_corners, gsend, grecv, lsem):
    row, col = lax.axis_index("row"), lax.axis_index("col")
    near = [around(row, col, dr, dc, rows, cols) for dr, dc in NEAR]
    c_peers = column_peers(row, col, cols)
    held = owner_ref.shape[0]
    core = pltpu.make_async_copy(obj_ref, ext_ref.at[:, half:half + tile, half:half + tile], lsem.at[0])
    core.start()
    lane = lax.broadcasted_iota(jnp.int32, (1, 128), 1)
    note = jnp.zeros((1, 128), jnp.int32)
    for h in range(held):
        note = jnp.where(lane == h, owner_ref[h], note)
        for k in range(2):
            note = jnp.where(lane == held + 2 * h + k, offsets_ref[h, k], note)
    mine[...] = note
    core.wait()
    end = half + tile
    for q in range(2):
        for k, at in enumerate((half, end - half)):
            code(out_rows.at[k, q], ext_ref[q, at:at + half, half:end])
            code(out_cols.at[k, q], ext_ref[q, half:end, at:at + half])
    greet(c_peers + near)
    send = Sends(gsend, grecv)
    got = []

    def edge(dr, dc):
        if dc == 0:
            return out_rows.at[(dr + 1) // 2]
        if dr == 0:
            return out_cols.at[(dc + 1) // 2]
        at = 0 if dc < 0 else tile - half
        return out_rows.at[(dr + 1) // 2, :, :, at:at + half]

    def landed(dr, dc):
        if dc == 0:
            return in_rows.at[(dr + 1) // 2]
        if dr == 0:
            return in_cols.at[(dc + 1) // 2]
        return in_corners.at[dr + 1 + (dc + 1) // 2]

    for i, (dr, dc) in enumerate(NEAR):
        got.append(send(edge(dr, dc), landed(dr, dc), near[i]))
    for s in range(cols - 1):
        got.append(send(mine, meta_ref.at[col], c_peers[s]))
    own = pltpu.make_async_copy(mine, meta_ref.at[col], lsem.at[1])
    own.start()
    for c in got:
        c.wait_recv()
    own.wait()
    for dr, dc in NEAR:
        tr, rl = span(-dr, tile, half)
        tc, cl = span(-dc, tile, half)
        ref = landed(dr, dc)
        for q in range(2):
            ext_ref[q, tr:tr + rl, tc:tc + cl] = decoded(ref.at[q])
    send.finish()
    big = tile + 2 * half

    @pl.when(row == 0)
    def _():
        ext_ref[:, :half, :] = jnp.zeros((2, half, big), F32)

    @pl.when(row == rows - 1)
    def _():
        ext_ref[:, big - half:, :] = jnp.zeros((2, half, big), F32)

    @pl.when(col == 0)
    def _():
        ext_ref[:, :, :half] = jnp.zeros((2, big, half), F32)

    @pl.when(col == cols - 1)
    def _():
        ext_ref[:, :, big - half:] = jnp.zeros((2, big, half), F32)


def pre_call(owner, offsets, obj, side, rows, cols):
    tile, half = obj.shape[1], side // 2
    big = tile + side
    copies = 8 + cols - 1
    V = pl.BlockSpec(memory_space=pltpu.VMEM)
    S = pl.BlockSpec(memory_space=pltpu.SMEM)
    return pl.pallas_call(
        functools.partial(pre_kernel, rows, cols, tile, half),
        out_shape=[jax.ShapeDtypeStruct((2, big, big), F32), jax.ShapeDtypeStruct((cols, 1, 128), jnp.int32)],
        in_specs=[S, S, pl.BlockSpec(memory_space=pltpu.HBM)],
        out_specs=[V, V],
        scratch_shapes=[
            pltpu.VMEM((1, 128), jnp.int32),
            pltpu.VMEM((2, 2, half + LEAD, tile), jnp.int16),
            pltpu.VMEM((2, 2, tile + LEAD, half), jnp.int16),
            pltpu.VMEM((2, 2, half + LEAD, tile), jnp.int16),
            pltpu.VMEM((2, 2, tile + LEAD, half), jnp.int16),
            pltpu.VMEM((4, 2, half + LEAD, half), jnp.int16),
            pltpu.SemaphoreType.DMA((copies,)),
            pltpu.SemaphoreType.DMA((copies,)),
            pltpu.SemaphoreType.DMA((2,)),
        ],
        compiler_params=pltpu.CompilerParams(collective_id=0, has_side_effects=True, vmem_limit_bytes=32 * 2**20),
        name="pre",
    )(owner, offsets, obj)


def cut_kernel(cols, half, held, meta_ref, ext, patch_hbm, list_ref, patch, osem):
    col = lax.axis_index("col")
    side = 2 * half
    tall, wide, most = side + 8, side + 128, list_ref.shape[0]

    def clear(p, carry):
        for k in range(8):
            list_ref[p, k] = 0
        return carry

    lax.fori_loop(0, most, clear, 0)

    def scan(s, count):
        live, r, c = jnp.int32(0), jnp.int32(0), jnp.int32(0)
        for h in range(held):
            hit = meta_ref[s, 0, h] == col
            live = jnp.where(hit, 1, live)
            r = jnp.where(hit, meta_ref[s, 0, held + 2 * h], r)
            c = jnp.where(hit, meta_ref[s, 0, held + 2 * h + 1], c)

        @pl.when((live == 1) & (count < most))
        def _():
            list_ref[count, 0] = 1
            list_ref[count, 1] = s
            list_ref[count, 2] = r // 8
            list_ref[count, 3] = lax.rem(r, 8)
            list_ref[count, 4] = c // 128
            list_ref[count, 5] = lax.rem(c, 128)
        return count + live

    lax.fori_loop(0, cols, scan, 0)

    def out(p):
        return pltpu.make_async_copy(patch.at[p], patch_hbm.at[p], osem.at[p])

    def visit(p, carry):
        @pl.when(list_ref[p, 0] == 1)
        def _():
            r0 = pl.multiple_of(list_ref[p, 2] * 8, 8)
            c0 = pl.multiple_of(list_ref[p, 4] * 128, 128)
            for q in range(2):
                w = ext[q, pl.ds(r0, tall), pl.ds(c0, wide)]
                patch[p, q] = moved_back(w, list_ref[p, 3], list_ref[p, 5])

        @pl.when(list_ref[p, 0] == 0)
        def _():
            patch[p] = jnp.zeros((2, side, side), F32)

        out(p).start()
        return carry

    lax.fori_loop(0, most, visit, 0)

    def drain(p, carry):
        out(p).wait()
        return carry

    lax.fori_loop(0, most, drain, 0)


def cut_call(meta, ext, tile, cols, held, most):
    big = ext.shape[1]
    side = big - tile
    A = pl.BlockSpec(memory_space=pltpu.HBM)
    S = pl.BlockSpec(memory_space=pltpu.SMEM)
    return pl.pallas_call(
        functools.partial(cut_kernel, cols, side // 2, held),
        out_shape=[jax.ShapeDtypeStruct((most, 2, side, side), F32), jax.ShapeDtypeStruct((most, 8), jnp.int32)],
        in_specs=[S, pl.BlockSpec(memory_space=pltpu.VMEM)],
        out_specs=[A, S],
        scratch_shapes=[
            pltpu.VMEM((most, 2, side, side), F32),
            pltpu.SemaphoreType.DMA((most,)),
        ],
        compiler_params=pltpu.CompilerParams(vmem_limit_bytes=47 * 2**20),
        name="cut",
    )(meta, ext)


def main_kernel(rows, cols, list_ref, owner_ref, amp_hbm, patch_hbm, probe_hbm, tab_hbm,
                placed_hbm, grad_ref, pow_ref,
                placed_ref, psem, slots, amps, amp, probe, tab, patch, far, total, ratio, ebuf, hbuf, ssum,
                gsend, grecv, lsem):
    row, col = lax.axis_index("row"), lax.axis_index("col")
    c_peers = column_peers(row, col, cols)
    held, side, modes, most = amp.shape[0], amp.shape[1], probe.shape[0], patch.shape[0]
    local = [
        pltpu.make_async_copy(amp_hbm, amp, lsem.at[0]),
        pltpu.make_async_copy(probe_hbm, probe, lsem.at[1]),
        pltpu.make_async_copy(tab_hbm, tab, lsem.at[2]),
        pltpu.make_async_copy(patch_hbm, patch, lsem.at[3]),
    ]
    for copy in local:
        copy.start()
    greet(c_peers)
    send = Sends(gsend, grecv)
    local[0].wait()
    amp_copies = []
    for s in range(cols):
        to = col if s == 0 else c_peers[s - 1][1]
        which = jnp.int32(0)
        for h in range(1, held):
            which = jnp.where(owner_ref[h] == to, h, which)
        if s == 0:
            amps[col] = amp[which]
        else:
            slots[s] = amp[which]
            amp_copies.append(send(slots.at[s], amps.at[col], c_peers[s - 1]))
    local[1].wait()
    power = jnp.zeros((side, side), F32)
    for m in range(modes):
        power += probe[m, 0] * probe[m, 0] + probe[m, 1] * probe[m, 1]
    pow_ref[...] = power
    grad_ref[...] = jnp.zeros_like(grad_ref)
    ssum[...] = jnp.zeros_like(ssum)
    local[2].wait()
    local[3].wait()

    chunk = hbuf.shape[2] // modes
    chunks = side // chunk

    def left_pass(k, fields, halves):
        for m in range(modes):
            for h in range(2):
                part = dot(tab[k, h * side:(h + 1) * side], fields[m])
                for c in range(chunks):
                    rows_c = slice(c * chunk, (c + 1) * chunk)
                    halves[c, m * chunk:(m + 1) * chunk, h * side:(h + 1) * side] = part[rows_c].astype(BF16)

    def there(p, fields, halves):
        ssum[...] += patch[p, 0] * patch[p, 0] + patch[p, 1] * patch[p, 1]
        for m in range(modes):
            pr, pi = probe[m, 0], probe[m, 1]
            xr, xi = patch[p, 0], patch[p, 1]
            fields[m, :side] = (pr * xr - pi * xi).astype(BF16)
            fields[m, side:] = (pr * xi + pi * xr).astype(BF16)
        left_pass(0, fields, halves)
        for c in range(chunks):
            rows_c = slice(c * chunk, (c + 1) * chunk)
            out = dot(halves[c], tab[1])
            tot = jnp.zeros((chunk, side), F32)
            for m in range(modes):
                one = out[m * chunk:(m + 1) * chunk]
                far[p, m, rows_c] = one
                tot += one[:, :side] * one[:, :side] + one[:, side:] * one[:, side:]
            total[p, rows_c] = lax.rsqrt(jnp.maximum(tot, 0.25))

    def there_two(k, carry):
        for u in range(2):
            there(2 * k + u, ebuf.at[u], hbuf.at[u])
        return carry

    lax.fori_loop(0, most // 2, there_two, 0)
    for p in range(most - most % 2, most):
        there(p, ebuf.at[0], hbuf.at[0])
    for copy in amp_copies:
        copy.wait_recv()

    def out(p):
        return pltpu.make_async_copy(placed_ref.at[p], placed_hbm.at[p], psem.at[p])

    def drain(p, carry):
        out(p).wait()
        return carry

    def back(p, carry):
        fields, halves = ebuf.at[0], hbuf.at[0]
        ratio[...] = amps[list_ref[p, 1]].astype(F32) * total[p]
        for m in range(modes):
            fields[m, :side] = (far[p, m, :, :side] * ratio[...]).astype(BF16)
            fields[m, side:] = (far[p, m, :, side:] * ratio[...]).astype(BF16)
        left_pass(2, fields, halves)
        for c in range(chunks):
            rows_c = slice(c * chunk, (c + 1) * chunk)
            ret = dot(halves[c], tab[3])
            xr, xi = patch[p, 0, rows_c], patch[p, 1, rows_c]
            nr, ni = -xr * pow_ref[rows_c], -xi * pow_ref[rows_c]
            for m in range(modes):
                one = ret[m * chunk:(m + 1) * chunk]
                rr, ri = one[:, :side], one[:, side:]
                pr, pi = probe[m, 0, rows_c], probe[m, 1, rows_c]
                nr += pr * rr + pi * ri
                ni += pr * ri - pi * rr
                at_r = 2 * m * side + c * chunk
                at_i = at_r + side
                grad_ref[at_r:at_r + chunk] += xr * rr + xi * ri
                grad_ref[at_i:at_i + chunk] += xr * ri - xi * rr
            placed_ref[p, 0, rows_c] = nr
            placed_ref[p, 1, rows_c] = ni
        out(p).start()
        return carry

    lax.fori_loop(0, most, back, 0)
    for m in range(modes):
        for q in range(2):
            grad_ref[(2 * m + q) * side:(2 * m + q + 1) * side] -= probe[m, q] * ssum[...]
    lax.fori_loop(0, most, drain, 0)
    send.finish()


def main_call(items, owner, amp, patch, probe, rows, cols):
    side, modes, most = amp.shape[1], probe.shape[0], patch.shape[0]
    copies = cols - 1
    tr, ti = tables(side)

    def left(a, b):
        return jnp.concatenate([jnp.concatenate([a, -b], 1), jnp.concatenate([b, a], 1)], 0)

    def right(a, b):
        return jnp.concatenate([jnp.concatenate([a, b], 1), jnp.concatenate([-b, a], 1)], 0)

    tab = jnp.stack([left(tr, ti), right(tr, ti), left(tr, -ti), right(tr, -ti)])
    V = pl.BlockSpec(memory_space=pltpu.VMEM)
    A = pl.BlockSpec(memory_space=pltpu.HBM)
    S = pl.BlockSpec(memory_space=pltpu.SMEM)
    return pl.pallas_call(
        functools.partial(main_kernel, rows, cols),
        out_shape=[
            jax.ShapeDtypeStruct((most, 2, side, side), F32),
            jax.ShapeDtypeStruct((modes * 2 * side, side), F32),
            jax.ShapeDtypeStruct((side, side), F32),
        ],
        in_specs=[S, S, A, A, A, A],
        out_specs=[A, V, V],
        scratch_shapes=[
            pltpu.VMEM((most, 2, side, side), F32),
            pltpu.SemaphoreType.DMA((most,)),
            pltpu.VMEM((cols, side, side), BF16),
            pltpu.VMEM((cols, side, side), BF16),
            pltpu.VMEM(amp.shape, BF16),
            pltpu.VMEM(probe.shape, F32),
            pltpu.VMEM(tab.shape, BF16),
            pltpu.VMEM((most, 2, side, side), F32),
            pltpu.VMEM((most, modes, side, 2 * side), F32),
            pltpu.VMEM((most, side, side), F32),
            pltpu.VMEM((side, side), F32),
            pltpu.VMEM((2, modes, 2 * side, side), BF16),
            pltpu.VMEM((2, 4, modes * side // 4, 2 * side), BF16),
            pltpu.VMEM((side, side), F32),
            pltpu.SemaphoreType.DMA((copies,)),
            pltpu.SemaphoreType.DMA((copies,)),
            pltpu.SemaphoreType.DMA((4,)),
        ],
        compiler_params=pltpu.CompilerParams(collective_id=2, has_side_effects=True, vmem_limit_bytes=62 * 2**20),
        name="main",
    )(items, owner, amp, patch, probe, tab)


def place_kernel(tile, half, list_ref, placed_hbm, pow_ref, rows_ref, cols_ref, corners_ref, core_ref, placed_ref, psem, num):
    side = 2 * half
    big, tall, wide = tile + side, side + 8, side + 128

    def fetch(p):
        return pltpu.make_async_copy(placed_hbm.at[p], placed_ref.at[p], psem.at[p])

    def start(p, carry):
        fetch(p).start()
        return carry

    lax.fori_loop(0, list_ref.shape[0], start, 0)
    num[...] = jnp.zeros_like(num)

    def visit(p, carry):
        fetch(p).wait()

        @pl.when(list_ref[p, 0] == 1)
        def _():
            r0 = pl.multiple_of(list_ref[p, 2] * 8, 8)
            c0 = pl.multiple_of(list_ref[p, 4] * 128, 128)
            for q in range(3):
                w = moved_on(placed_ref[p, q] if q < 2 else pow_ref[...], list_ref[p, 3], list_ref[p, 5])
                num[q, pl.ds(r0, tall), pl.ds(c0, wide)] += w
        return carry

    lax.fori_loop(0, list_ref.shape[0], visit, 0)
    for q in range(3):
        for dr, dc in NEAR:
            r0, rl = span(dr, tile, half)
            c0, cl = span(dc, tile, half)
            rim = num[q, r0:r0 + rl, c0:c0 + cl].astype(BF16)
            if dc == 0:
                rows_ref[(dr + 1) // 2, q] = rim
            elif dr == 0:
                cols_ref[(dc + 1) // 2, q] = rim
            else:
                corners_ref[dr + 1 + (dc + 1) // 2, q] = rim
        core_ref[q] = num[q, half:big - half, half:big - half]


def place_call(items, placed, power, tile):
    side = power.shape[0]
    half = side // 2
    big = tile + side
    V = pl.BlockSpec(memory_space=pltpu.VMEM)
    S = pl.BlockSpec(memory_space=pltpu.SMEM)
    return pl.pallas_call(
        functools.partial(place_kernel, tile, half),
        out_shape=[
            jax.ShapeDtypeStruct((2, 3, half, tile), BF16),
            jax.ShapeDtypeStruct((2, 3, tile, half), BF16),
            jax.ShapeDtypeStruct((4, 3, half, half), BF16),
            jax.ShapeDtypeStruct((3, tile, tile), F32)],
        in_specs=[S, pl.BlockSpec(memory_space=pltpu.HBM), V],
        out_specs=[V, V, V, V],
        scratch_shapes=[
            pltpu.VMEM(placed.shape, F32),
            pltpu.SemaphoreType.DMA((placed.shape[0],)),
            pltpu.VMEM((3, big, big), F32)],
        compiler_params=pltpu.CompilerParams(vmem_limit_bytes=46 * 2**20),
        name="place",
    )(items, placed, power)


def finish_kernel(obj_ref, got_ref, out_hbm, grad_hbm, wide, sem):
    n = got_ref.shape[2]
    whole = pltpu.make_async_copy(obj_ref, out_hbm, sem.at[4])
    whole.start()
    parts = []
    for k in range(4):
        c, at = k // 2, (k % 2) * (n // 2)
        rows_k = pl.ds(k * (n // 2), n // 2)
        for h in range(2):
            wide[rows_k, 128 * h:128 * (h + 1)] = got_ref[c, h, at:at + n // 2].astype(F32)
        part = pltpu.make_async_copy(wide.at[rows_k], grad_hbm.at[rows_k], sem.at[k])
        part.start()
        parts.append(part)
    for part in parts:
        part.wait()
    whole.wait()


def finish_call(obj, got):
    n = got.shape[2]
    V = pl.BlockSpec(memory_space=pltpu.VMEM)
    A = pl.BlockSpec(memory_space=pltpu.HBM)
    return pl.pallas_call(
        finish_kernel,
        out_shape=[jax.ShapeDtypeStruct(obj.shape, F32), jax.ShapeDtypeStruct((2 * n, 256), F32)],
        in_specs=[V, V],
        out_specs=[A, A],
        scratch_shapes=[pltpu.VMEM((2 * n, 256), F32), pltpu.SemaphoreType.DMA((5,))],
        compiler_params=pltpu.CompilerParams(vmem_limit_bytes=16 * 2**20),
        name="finish",
    )(obj, got)


def on_device(object_field, probe, amplitudes, owner, offsets):
    rows, cols = lax.axis_size("row"), lax.axis_size("col")
    held = amplitudes.shape[0]
    most = 4 * (held - 1)
    side, tile = probe.shape[-1], object_field.shape[1]
    ext, meta = pre_call(owner, offsets, object_field, side, rows, cols)
    patch, items = cut_call(meta, ext, tile, cols, held, most)
    placed, grad, power = main_call(items, owner, amplitudes, patch, probe, rows, cols)
    *rims, core = place_call(items, placed, power, tile)
    scale = 1.0 / math.sqrt(rows * cols * held)
    object_out, gradient = post_call(rims, core, object_field, grad, rows, cols, scale)
    object_out, gradient = finish_call(object_out, gradient)
    return (object_out, gradient.reshape(probe.shape))


def solution(mesh):
    return jax.shard_map(
        on_device,
        mesh=mesh,
        in_specs=(
            P(None, "row", "col"),
            P(),
            P(("row", "col"), None, None),
            P(("row", "col")),
            P(("row", "col"), None),
        ),
        out_specs=(P(None, "row", "col"), P()),
        check_vma=False,
    )
```

```python
import functools
import math

import jax
import jax.numpy as jnp
import numpy as np
from jax import lax
from jax.experimental import pallas as pl
from jax.experimental.pallas import tpu as pltpu
from jax.sharding import PartitionSpec as P

F32, BF16 = jnp.float32, jnp.bfloat16
MESH = pl.DeviceIdType.MESH

def tables(side):
    series = np.arange(side, dtype=np.int32)
    angles = (series[:, None] * series[None, :] % side).astype(np.float32) * np.float32(2.0 * math.pi / side)
    factor = np.float32(1.0 / math.sqrt(side))
    re = jnp.asarray(np.cos(angles) * factor).astype(BF16)
    im = jnp.asarray(-np.sin(angles) * factor).astype(BF16)
    return re, im

def dot(a, b):
    return jnp.dot(a, b, preferred_element_type=F32)

def moved_back(w, rows, lanes):
    tall, wide = w.shape
    t = pltpu.roll(w.reshape(tall // 8, 8, wide), lax.rem(8 - rows, 8), 1)
    sub = lax.broadcasted_iota(jnp.int32, (tall // 8 - 1, 8, wide), 1)
    w = jnp.where(sub < 8 - rows, t[:-1], t[1:]).reshape(tall - 8, wide)
    lane = lax.broadcasted_iota(jnp.int32, (tall - 8, 128), 1)
    parts = [pltpu.roll(w[:, k:k + 128], lax.rem(128 - lanes, 128), 1) for k in range(0, wide, 128)]
    return jnp.concatenate([jnp.where(lane < 128 - lanes, a, b) for a, b in zip(parts[:-1], parts[1:])], 1)


def moved_on(w, rows, lanes):
    tall, wide = w.shape
    lane = lax.broadcasted_iota(jnp.int32, (tall, 128), 1)
    none = jnp.zeros((tall, 128), F32)
    parts = [none] + [pltpu.roll(w[:, k:k + 128], lanes, 1) for k in range(0, wide, 128)] + [none]
    w = jnp.concatenate([jnp.where(lane < lanes, a, b) for a, b in zip(parts[:-1], parts[1:])], 1)
    wide += 128
    t = pltpu.roll(w.reshape(tall // 8, 8, wide), rows, 1)
    none = jnp.zeros((1, 8, wide), F32)
    sub = lax.broadcasted_iota(jnp.int32, (tall // 8 + 1, 8, wide), 1)
    both = jnp.where(sub < rows, jnp.concatenate([none, t], 0), jnp.concatenate([t, none], 0))
    return both.reshape(tall + 8, wide)


def around(row, col, dr, dc, rows, cols):
    return lax.rem(row + dr + rows, rows), lax.rem(col + dc + cols, cols)


NEAR = [(dr, dc) for dr in (-1, 0, 1) for dc in (-1, 0, 1) if (dr, dc) != (0, 0)]


def span(step, tile, half):
    return {-1: (0, half), 0: (half, tile), 1: (half + tile, half)}[step]


def landing(step, tile, half):
    return {-1: (tile - half, half), 0: (0, tile), 1: (0, half)}[step]


def column_peers(row, col, cols):
    depth = 4
    steps = [(2, 1), (1, 2), (2, 3), (3, 2), (2, 2), (1, 1), (3, 3), (1, 3), (3, 1), (2, 0), (0, 2), (0, 1), (1, 0), (0, 3), (3, 0)]
    x, z = col // depth, lax.rem(col, depth)
    return [(row, lax.rem(x + dx, cols // depth) * depth + lax.rem(z + dz, depth)) for dx, dz in steps]


LEAD = 16


def power_of(x):
    top = jnp.max(jnp.abs(x), axis=0, keepdims=True)
    return jnp.floor(jnp.log2(jnp.maximum(top, 1e-30)))


def code(out, x, power=None):
    power = power_of(x) if power is None else power
    out[:LEAD] = jnp.broadcast_to(power, (LEAD, x.shape[1])).astype(jnp.int32).astype(jnp.int16)
    x = jnp.clip(jnp.round(x * jnp.exp2(14.0 - power)), -32767.0, 32767.0)
    out[LEAD:] = x.astype(jnp.int32).astype(jnp.int16)


def decoded(ref):
    power = ref[:LEAD].astype(jnp.int32).astype(F32)[:1]
    return ref[LEAD:].astype(jnp.int32).astype(F32) * jnp.exp2(power - 14.0)


def code_pieces(out, ref):
    power = power_of(ref[...])
    size = ref.shape[0] // out.shape[0]
    for k in range(out.shape[0]):
        code(out.at[k], ref[k * size:(k + 1) * size], power)


def owned_by(to, owner_ref, held):
    which = jnp.int32(0)
    for h in range(1, held):
        which = jnp.where(owner_ref[h] == to, h, which)
    return which


class Sends:
    def __init__(self, send_sem, recv_sem):
        self.send_sem, self.recv_sem, self.at, self.all = send_sem, recv_sem, 0, []

    def __call__(self, src, dst, device):
        n = self.at
        self.at += 1
        copy = pltpu.make_async_remote_copy(
            src_ref=src, dst_ref=dst, send_sem=self.send_sem.at[n], recv_sem=self.recv_sem.at[n],
            device_id=device, device_id_type=MESH)
        copy.start()
        self.all.append(copy)
        return copy

    def finish(self):
        for copy in self.all:
            copy.wait_send()


def greet(devices):
    barrier = pltpu.get_barrier_semaphore()
    for device in devices:
        pl.semaphore_signal(barrier, inc=1, device_id=device, device_id_type=MESH)
    pl.semaphore_wait(barrier, len(devices))


def post_kernel(rows, cols, tile, half, scale, rows_ref, cols_ref, corners_ref, core_ref, obj_ref, grad_ref, out_ref, all16,
                wsum, rim_rows, rim_cols, rim_corners, mate, sum_a, sum_b, got_a, got_b, part_a, part_b, got_a2, got_b2,
                code_a, code_b, gsend, grecv):
    row, col = lax.axis_index("row"), lax.axis_index("col")
    core, y = lax.rem(row, 2), row // 2
    ys = rows // 2
    other = (row + 1 - 2 * core, col)
    y_peers = [(lax.rem(y + s, ys) * 2 + core, col) for s in range(1, ys)]
    c_peers = column_peers(row, col, cols)
    near = [around(row, col, dr, dc, rows, cols) for dr, dc in NEAR]
    greet([other] + y_peers + c_peers + near)
    send = Sends(gsend, grecv)
    n = grad_ref.shape[0] // 2
    na, nb = n // ys, n // cols
    fin = n // (ys * cols)
    theirs = pl.ds(pl.multiple_of((1 - core) * n, n), n)
    mine = pl.ds(pl.multiple_of(core * n, n), n)
    pair = [send(grad_ref.at[theirs, k:k + 128], mate.at[:, k:k + 128], other) for k in (0, 128)]
    rim_copies = []

    def place(i, by_rows, by_cols, at_corners):
        dr, dc = NEAR[i]
        if dc == 0:
            return by_rows.at[(dr + 1) // 2]
        if dr == 0:
            return by_cols.at[(dc + 1) // 2]
        return at_corners.at[dr + 1 + (dc + 1) // 2]

    def landed(i):
        return place(i, rim_rows, rim_cols, rim_corners)

    def send_rims(which):
        for i in which:
            rim_copies.append(send(place(i, rows_ref, cols_ref, corners_ref), landed(i), near[i]))

    send_rims([1, 6, 3, 4])
    y_at = [lax.rem(y + s, ys) for s in range(1, ys)]
    c_at = [peer[1] for peer in c_peers]
    pair[0].wait_recv()
    sum_a[...] = grad_ref[mine, :128] + mate[:, :128]
    code_pieces(code_a, sum_a)
    def piece(k, size):
        return pl.ds(pl.multiple_of(k * size, size), size)

    a1 = [send(code_a.at[y_at[s]], got_a.at[s], y_peers[s]) for s in range(ys - 1)]
    pair[1].wait_recv()
    sum_b[...] = grad_ref[mine, 128:] + mate[:, 128:]
    code_pieces(code_b, sum_b)
    b1 = [send(code_b.at[c_at[s]], got_b.at[s], c_peers[s]) for s in range(cols - 1)]
    for c in a1:
        c.wait_recv()
    tot = sum_a[piece(y, na), :]
    for s in range(ys - 1):
        tot += decoded(got_a.at[s])
    part_a[...] = tot
    a2 = [send(part_a.at[piece(c_at[s], fin)], got_a2.at[s], c_peers[s]) for s in range(cols - 1)]
    for c in b1:
        c.wait_recv()
    tot = sum_b[piece(col, nb), :]
    for s in range(cols - 1):
        tot += decoded(got_b.at[s])
    part_b[...] = tot
    b2 = [send(part_b.at[piece(y_at[s], fin)], got_b2.at[s], y_peers[s]) for s in range(ys - 1)]
    send_rims([0, 2, 5, 7])
    for c in a2:
        c.wait_recv()
    tot = part_a[piece(col, fin), :]
    for s in range(cols - 1):
        tot += got_a2[s]
    at_a = piece(y * cols + col, fin)
    all16[core, 0, at_a, :] = (tot * scale).astype(all16.dtype)
    a3 = [send(all16.at[core, 0, at_a], all16.at[core, 0, at_a], p) for p in c_peers]
    for c in b2:
        c.wait_recv()
    tot = part_b[piece(y, fin), :]
    for s in range(ys - 1):
        tot += got_b2[s]
    at_b = piece(col * ys + y, fin)
    all16[core, 1, at_b, :] = (tot * scale).astype(all16.dtype)
    b3 = [send(all16.at[core, 1, at_b], all16.at[core, 1, at_b], p) for p in y_peers]
    for c in a3:
        c.wait_recv()
    big_a = piece(y, na)
    a4 = [send(all16.at[core, 0, big_a], all16.at[core, 0, big_a], p) for p in y_peers]
    for c in b3:
        c.wait_recv()
    big_b = piece(col, nb)
    b4 = [send(all16.at[core, 1, big_b], all16.at[core, 1, big_b], p) for p in c_peers]
    last = []
    for k, copies in enumerate((a4, b4)):
        for c in copies:
            c.wait_recv()
        last.append(send(all16.at[core, k], all16.at[core, k], other))
    for c in rim_copies:
        c.wait_recv()
    out_ref[...] = core_ref[0:2]
    wsum[...] = core_ref[2]
    for i, (dr, dc) in enumerate(NEAR):
        r0, rl = landing(dr, tile, half)
        c0, cl = landing(dc, tile, half)
        keep = (row != -1) & (col != -1)
        if dr:
            keep = keep & (row != (0 if dr == 1 else rows - 1))
        if dc:
            keep = keep & (col != (0 if dc == 1 else cols - 1))

        @pl.when(keep)
        def _(i=i, r0=r0, rl=rl, c0=c0, cl=cl):
            for q in range(2):
                out_ref[q, r0:r0 + rl, c0:c0 + cl] += landed(i)[q].astype(F32)
            wsum[r0:r0 + rl, c0:c0 + cl] += landed(i)[2].astype(F32)

    for q in range(2):
        out_ref[q] = obj_ref[q] + out_ref[q] / (wsum[...] + 1.0)
    for c in last:
        c.wait_recv()
    send.finish()


def post_call(rims, core, obj, grad, rows, cols, scale):
    tile, half = obj.shape[1], rims[0].shape[2]
    total = grad.shape[0]
    ys, n = rows // 2, total // 2
    na, nb, fin = n // ys, n // cols, n // (ys * cols)
    copies = 2 + 8 + 4 * (ys - 1) + 4 * (cols - 1) + 2
    V = pl.BlockSpec(memory_space=pltpu.VMEM)
    return pl.pallas_call(
        functools.partial(post_kernel, rows, cols, tile, half, scale),
        out_shape=[jax.ShapeDtypeStruct(obj.shape, F32), jax.ShapeDtypeStruct((2, 2, n, 128), BF16)],
        in_specs=[V] * 6,
        out_specs=[V, V],
        scratch_shapes=[
            pltpu.VMEM((tile, tile), F32),
            pltpu.VMEM((2, 3, half, tile), BF16),
            pltpu.VMEM((2, 3, tile, half), BF16),
            pltpu.VMEM((4, 3, half, half), BF16),
            pltpu.VMEM((n, 256), F32),
            pltpu.VMEM((n, 128), F32),
            pltpu.VMEM((n, 128), F32),
            pltpu.VMEM((ys - 1, LEAD + na, 128), jnp.int16),
            pltpu.VMEM((cols - 1, LEAD + nb, 128), jnp.int16),
            pltpu.VMEM((na, 128), F32),
            pltpu.VMEM((nb, 128), F32),
            pltpu.VMEM((cols - 1, fin, 128), F32),
            pltpu.VMEM((ys - 1, fin, 128), F32),
            pltpu.VMEM((ys, LEAD + na, 128), jnp.int16),
            pltpu.VMEM((cols, LEAD + nb, 128), jnp.int16),
            pltpu.SemaphoreType.DMA((copies,)),
            pltpu.SemaphoreType.DMA((copies,)),
        ],
        compiler_params=pltpu.CompilerParams(collective_id=1, has_side_effects=True, vmem_limit_bytes=40 * 2**20),
        name="post",
    )(*rims, core, obj, grad)


def pre_kernel(rows, cols, tile, half, owner_ref, offsets_ref, obj_ref, ext_ref, meta_ref,
               mine, out_rows, out_cols, in_rows, in_cols, in_corners, gsend, grecv, lsem):
    row, col = lax.axis_index("row"), lax.axis_index("col")
    near = [around(row, col, dr, dc, rows, cols) for dr, dc in NEAR]
    c_peers = column_peers(row, col, cols)
    held = owner_ref.shape[0]
    core = pltpu.make_async_copy(obj_ref, ext_ref.at[:, half:half + tile, half:half + tile], lsem.at[0])
    core.start()
    lane = lax.broadcasted_iota(jnp.int32, (1, 128), 1)
    note = jnp.zeros((1, 128), jnp.int32)
    for h in range(held):
        note = jnp.where(lane == h, owner_ref[h], note)
        for k in range(2):
            note = jnp.where(lane == held + 2 * h + k, offsets_ref[k, h], note)
    mine[...] = note
    core.wait()
    end = half + tile
    for q in range(2):
        for k, at in enumerate((half, end - half)):
            code(out_rows.at[k, q], ext_ref[q, at:at + half, half:end])
            code(out_cols.at[k, q], ext_ref[q, half:end, at:at + half])
    greet(c_peers + near)
    send = Sends(gsend, grecv)
    got = []

    def edge(dr, dc):
        if dc == 0:
            return out_rows.at[(dr + 1) // 2]
        if dr == 0:
            return out_cols.at[(dc + 1) // 2]
        at = 0 if dc < 0 else tile - half
        return out_rows.at[(dr + 1) // 2, :, :, at:at + half]

    def landed(dr, dc):
        if dc == 0:
            return in_rows.at[(dr + 1) // 2]
        if dr == 0:
            return in_cols.at[(dc + 1) // 2]
        return in_corners.at[dr + 1 + (dc + 1) // 2]

    for i, (dr, dc) in enumerate(NEAR):
        got.append(send(edge(dr, dc), landed(dr, dc), near[i]))
    for s in range(cols - 1):
        got.append(send(mine, meta_ref.at[col], c_peers[s]))
    own = pltpu.make_async_copy(mine, meta_ref.at[col], lsem.at[1])
    own.start()
    for c in got:
        c.wait_recv()
    own.wait()
    for dr, dc in NEAR:
        tr, rl = span(-dr, tile, half)
        tc, cl = span(-dc, tile, half)
        ref = landed(dr, dc)
        for q in range(2):
            ext_ref[q, tr:tr + rl, tc:tc + cl] = decoded(ref.at[q])
    send.finish()
    big = tile + 2 * half

    @pl.when(row == 0)
    def _():
        ext_ref[:, :half, :] = jnp.zeros((2, half, big), F32)

    @pl.when(row == rows - 1)
    def _():
        ext_ref[:, big - half:, :] = jnp.zeros((2, half, big), F32)

    @pl.when(col == 0)
    def _():
        ext_ref[:, :, :half] = jnp.zeros((2, big, half), F32)

    @pl.when(col == cols - 1)
    def _():
        ext_ref[:, :, big - half:] = jnp.zeros((2, big, half), F32)


def pre_call(owner, offsets, obj, side, rows, cols):
    tile, half = obj.shape[1], side // 2
    big = tile + side
    copies = 8 + cols - 1
    V = pl.BlockSpec(memory_space=pltpu.VMEM)
    S = pl.BlockSpec(memory_space=pltpu.SMEM)
    return pl.pallas_call(
        functools.partial(pre_kernel, rows, cols, tile, half),
        out_shape=[jax.ShapeDtypeStruct((2, big, big), F32), jax.ShapeDtypeStruct((cols, 1, 128), jnp.int32)],
        in_specs=[S, S, pl.BlockSpec(memory_space=pltpu.HBM)],
        out_specs=[V, V],
        scratch_shapes=[
            pltpu.VMEM((1, 128), jnp.int32),
            pltpu.VMEM((2, 2, half + LEAD, tile), jnp.int16),
            pltpu.VMEM((2, 2, tile + LEAD, half), jnp.int16),
            pltpu.VMEM((2, 2, half + LEAD, tile), jnp.int16),
            pltpu.VMEM((2, 2, tile + LEAD, half), jnp.int16),
            pltpu.VMEM((4, 2, half + LEAD, half), jnp.int16),
            pltpu.SemaphoreType.DMA((copies,)),
            pltpu.SemaphoreType.DMA((copies,)),
            pltpu.SemaphoreType.DMA((2,)),
        ],
        compiler_params=pltpu.CompilerParams(collective_id=0, has_side_effects=True, vmem_limit_bytes=32 * 2**20),
        name="pre",
    )(owner, offsets, obj)


def cut_kernel(cols, half, held, meta_ref, ext, patch_hbm, list_ref, patch, osem):
    col = lax.axis_index("col")
    side = 2 * half
    tall, wide, most = side + 8, side + 128, list_ref.shape[0]

    def clear(p, carry):
        for k in range(8):
            list_ref[p, k] = 0
        return carry

    lax.fori_loop(0, most, clear, 0)

    def scan(s, count):
        live, r, c = jnp.int32(0), jnp.int32(0), jnp.int32(0)
        for h in range(held):
            hit = meta_ref[s, 0, h] == col
            live = jnp.where(hit, 1, live)
            r = jnp.where(hit, meta_ref[s, 0, held + 2 * h], r)
            c = jnp.where(hit, meta_ref[s, 0, held + 2 * h + 1], c)

        @pl.when((live == 1) & (count < most))
        def _():
            list_ref[count, 0] = 1
            list_ref[count, 1] = s
            list_ref[count, 2] = r // 8
            list_ref[count, 3] = lax.rem(r, 8)
            list_ref[count, 4] = c // 128
            list_ref[count, 5] = lax.rem(c, 128)
        return count + live

    lax.fori_loop(0, cols, scan, 0)

    def out(p):
        return pltpu.make_async_copy(patch.at[p], patch_hbm.at[p], osem.at[p])

    def visit(p, carry):
        @pl.when(list_ref[p, 0] == 1)
        def _():
            r0 = pl.multiple_of(list_ref[p, 2] * 8, 8)
            c0 = pl.multiple_of(list_ref[p, 4] * 128, 128)
            for q in range(2):
                w = ext[q, pl.ds(r0, tall), pl.ds(c0, wide)]
                patch[p, q] = moved_back(w, list_ref[p, 3], list_ref[p, 5])

        @pl.when(list_ref[p, 0] == 0)
        def _():
            patch[p] = jnp.zeros((2, side, side), F32)

        out(p).start()
        return carry

    lax.fori_loop(0, most, visit, 0)

    def drain(p, carry):
        out(p).wait()
        return carry

    lax.fori_loop(0, most, drain, 0)


def cut_call(meta, ext, tile, cols, held, most):
    big = ext.shape[1]
    side = big - tile
    A = pl.BlockSpec(memory_space=pltpu.HBM)
    S = pl.BlockSpec(memory_space=pltpu.SMEM)
    return pl.pallas_call(
        functools.partial(cut_kernel, cols, side // 2, held),
        out_shape=[jax.ShapeDtypeStruct((most, 2, side, side), F32), jax.ShapeDtypeStruct((most, 8), jnp.int32)],
        in_specs=[S, pl.BlockSpec(memory_space=pltpu.VMEM)],
        out_specs=[A, S],
        scratch_shapes=[
            pltpu.VMEM((most, 2, side, side), F32),
            pltpu.SemaphoreType.DMA((most,)),
        ],
        compiler_params=pltpu.CompilerParams(vmem_limit_bytes=47 * 2**20),
        name="cut",
    )(meta, ext)


def main_kernel(rows, cols, list_ref, owner_ref, amp_hbm, patch_hbm, probe_hbm, tab_hbm,
                placed_hbm, grad_ref,
                placed_ref, pow_ref, psem, slots, amps, amp, probe, tab, patch, far, total, ratio, ebuf, hbuf, ssum,
                gsend, grecv, lsem):
    row, col = lax.axis_index("row"), lax.axis_index("col")
    c_peers = column_peers(row, col, cols)
    held, side, modes, most = amp.shape[0], amp.shape[1], probe.shape[0], patch.shape[0]
    local = [
        pltpu.make_async_copy(amp_hbm, amp, lsem.at[0]),
        pltpu.make_async_copy(probe_hbm, probe, lsem.at[1]),
        pltpu.make_async_copy(tab_hbm, tab, lsem.at[2]),
        pltpu.make_async_copy(patch_hbm, patch, lsem.at[3]),
    ]
    for copy in local:
        copy.start()
    greet(c_peers)
    send = Sends(gsend, grecv)
    local[0].wait()
    amp_copies = []
    for h in range(2):
        part = pl.ds(h * (side // 2), side // 2)
        for k, peer in enumerate(c_peers):
            if h == 0:
                slots[k] = amp[owned_by(peer[1], owner_ref, held)]
            amp_copies.append(send(slots.at[k, part], amps.at[col, part], peer))
    amps[col] = amp[owned_by(col, owner_ref, held)]
    local[1].wait()
    power = jnp.zeros((side, side), F32)
    for m in range(modes):
        power += probe[m, 0] * probe[m, 0] + probe[m, 1] * probe[m, 1]
    pow_ref[...] = power
    weight = pltpu.make_async_copy(pow_ref, placed_hbm.at[most, 0], psem.at[most])
    weight.start()
    grad_ref[...] = jnp.zeros_like(grad_ref)
    ssum[...] = jnp.zeros_like(ssum)
    local[2].wait()
    local[3].wait()

    chunk = hbuf.shape[2] // modes
    chunks = side // chunk

    def left_pass(k, fields, halves):
        for m in range(modes):
            for h in range(2):
                part = dot(tab[k, h * side:(h + 1) * side], fields[m])
                for c in range(chunks):
                    rows_c = slice(c * chunk, (c + 1) * chunk)
                    halves[c, m * chunk:(m + 1) * chunk, h * side:(h + 1) * side] = part[rows_c].astype(BF16)

    def there(p, fields, halves):
        ssum[...] += patch[p, 0] * patch[p, 0] + patch[p, 1] * patch[p, 1]
        for m in range(modes):
            pr, pi = probe[m, 0], probe[m, 1]
            xr, xi = patch[p, 0], patch[p, 1]
            fields[m, :side] = (pr * xr - pi * xi).astype(BF16)
            fields[m, side:] = (pr * xi + pi * xr).astype(BF16)
        left_pass(0, fields, halves)
        for c in range(chunks):
            rows_c = slice(c * chunk, (c + 1) * chunk)
            out = dot(halves[c], tab[1])
            tot = jnp.zeros((chunk, side), F32)
            for m in range(modes):
                one = out[m * chunk:(m + 1) * chunk]
                far[p, m, rows_c] = one
                tot += one[:, :side] * one[:, :side] + one[:, side:] * one[:, side:]
            total[p, rows_c] = lax.rsqrt(jnp.maximum(tot, 0.25))

    def there_two(k, carry):
        for u in range(2):
            there(2 * k + u, ebuf.at[u], hbuf.at[u])
        return carry

    lax.fori_loop(0, most // 2, there_two, 0)
    for p in range(most - most % 2, most):
        there(p, ebuf.at[0], hbuf.at[0])
    for copy in amp_copies:
        copy.wait_recv()

    def out(p):
        return pltpu.make_async_copy(placed_ref.at[p], placed_hbm.at[p], psem.at[p])

    def drain(p, carry):
        out(p).wait()
        return carry

    def back(p, carry):
        fields, halves = ebuf.at[0], hbuf.at[0]
        ratio[...] = amps[list_ref[p, 1]].astype(F32) * total[p]
        for m in range(modes):
            fields[m, :side] = (far[p, m, :, :side] * ratio[...]).astype(BF16)
            fields[m, side:] = (far[p, m, :, side:] * ratio[...]).astype(BF16)
        left_pass(2, fields, halves)
        for c in range(chunks):
            rows_c = slice(c * chunk, (c + 1) * chunk)
            ret = dot(halves[c], tab[3])
            xr, xi = patch[p, 0, rows_c], patch[p, 1, rows_c]
            nr, ni = -xr * pow_ref[rows_c], -xi * pow_ref[rows_c]
            for m in range(modes):
                one = ret[m * chunk:(m + 1) * chunk]
                rr, ri = one[:, :side], one[:, side:]
                pr, pi = probe[m, 0, rows_c], probe[m, 1, rows_c]
                nr += pr * rr + pi * ri
                ni += pr * ri - pi * rr
                at_r = 2 * m * side + c * chunk
                at_i = at_r + side
                grad_ref[at_r:at_r + chunk] += xr * rr + xi * ri
                grad_ref[at_i:at_i + chunk] += xr * ri - xi * rr
            placed_ref[p, 0, rows_c] = nr
            placed_ref[p, 1, rows_c] = ni
        out(p).start()
        return carry

    lax.fori_loop(0, most, back, 0)
    for m in range(modes):
        for q in range(2):
            grad_ref[(2 * m + q) * side:(2 * m + q + 1) * side] -= probe[m, q] * ssum[...]
    lax.fori_loop(0, most, drain, 0)
    weight.wait()
    send.finish()


def main_call(items, owner, amp, patch, probe, rows, cols):
    side, modes, most = amp.shape[1], probe.shape[0], patch.shape[0]
    copies = 2 * (cols - 1)
    tr, ti = tables(side)

    def left(a, b):
        return jnp.concatenate([jnp.concatenate([a, -b], 1), jnp.concatenate([b, a], 1)], 0)

    def right(a, b):
        return jnp.concatenate([jnp.concatenate([a, b], 1), jnp.concatenate([-b, a], 1)], 0)

    tab = jnp.stack([left(tr, ti), right(tr, ti), left(tr, -ti), right(tr, -ti)])
    V = pl.BlockSpec(memory_space=pltpu.VMEM)
    A = pl.BlockSpec(memory_space=pltpu.HBM)
    S = pl.BlockSpec(memory_space=pltpu.SMEM)
    return pl.pallas_call(
        functools.partial(main_kernel, rows, cols),
        out_shape=[
            jax.ShapeDtypeStruct((most + 1, 2, side, side), F32),
            jax.ShapeDtypeStruct((modes * 2 * side, side), F32),
        ],
        in_specs=[S, S, A, A, A, A],
        out_specs=[A, V],
        scratch_shapes=[
            pltpu.VMEM((most, 2, side, side), F32),
            pltpu.VMEM((side, side), F32),
            pltpu.SemaphoreType.DMA((most + 1,)),
            pltpu.VMEM((cols - 1, side, side), BF16),
            pltpu.VMEM((cols, side, side), BF16),
            pltpu.VMEM(amp.shape, BF16),
            pltpu.VMEM(probe.shape, F32),
            pltpu.VMEM(tab.shape, BF16),
            pltpu.VMEM((most, 2, side, side), F32),
            pltpu.VMEM((most, modes, side, 2 * side), F32),
            pltpu.VMEM((most, side, side), F32),
            pltpu.VMEM((side, side), F32),
            pltpu.VMEM((2, modes, 2 * side, side), BF16),
            pltpu.VMEM((2, 4, modes * side // 4, 2 * side), BF16),
            pltpu.VMEM((side, side), F32),
            pltpu.SemaphoreType.DMA((copies,)),
            pltpu.SemaphoreType.DMA((copies,)),
            pltpu.SemaphoreType.DMA((4,)),
        ],
        compiler_params=pltpu.CompilerParams(collective_id=2, has_side_effects=True, vmem_limit_bytes=62 * 2**20),
        name="main",
    )(items, owner, amp, patch, probe, tab)


def place_kernel(tile, half, list_ref, placed_hbm, rows_ref, cols_ref, corners_ref, core_ref, placed_ref, pow_ref, psem, num):
    side = 2 * half
    big, tall, wide = tile + side, side + 8, side + 128

    def fetch(p):
        return pltpu.make_async_copy(placed_hbm.at[p], placed_ref.at[p], psem.at[p])

    def start(p, carry):
        fetch(p).start()
        return carry

    most = list_ref.shape[0]
    weight = pltpu.make_async_copy(placed_hbm.at[most, 0], pow_ref, psem.at[most])
    weight.start()
    lax.fori_loop(0, most, start, 0)
    num[...] = jnp.zeros_like(num)
    weight.wait()

    def visit(p, carry):
        fetch(p).wait()

        @pl.when(list_ref[p, 0] == 1)
        def _():
            r0 = pl.multiple_of(list_ref[p, 2] * 8, 8)
            c0 = pl.multiple_of(list_ref[p, 4] * 128, 128)
            for q in range(3):
                w = moved_on(placed_ref[p, q] if q < 2 else pow_ref[...], list_ref[p, 3], list_ref[p, 5])
                num[q, pl.ds(r0, tall), pl.ds(c0, wide)] += w
        return carry

    lax.fori_loop(0, list_ref.shape[0], visit, 0)
    for q in range(3):
        for dr, dc in NEAR:
            r0, rl = span(dr, tile, half)
            c0, cl = span(dc, tile, half)
            rim = num[q, r0:r0 + rl, c0:c0 + cl].astype(BF16)
            if dc == 0:
                rows_ref[(dr + 1) // 2, q] = rim
            elif dr == 0:
                cols_ref[(dc + 1) // 2, q] = rim
            else:
                corners_ref[dr + 1 + (dc + 1) // 2, q] = rim
        core_ref[q] = num[q, half:big - half, half:big - half]


def place_call(items, placed, tile):
    most, side = items.shape[0], placed.shape[-1]
    half = side // 2
    big = tile + side
    V = pl.BlockSpec(memory_space=pltpu.VMEM)
    S = pl.BlockSpec(memory_space=pltpu.SMEM)
    return pl.pallas_call(
        functools.partial(place_kernel, tile, half),
        out_shape=[
            jax.ShapeDtypeStruct((2, 3, half, tile), BF16),
            jax.ShapeDtypeStruct((2, 3, tile, half), BF16),
            jax.ShapeDtypeStruct((4, 3, half, half), BF16),
            jax.ShapeDtypeStruct((3, tile, tile), F32)],
        in_specs=[S, pl.BlockSpec(memory_space=pltpu.HBM)],
        out_specs=[V, V, V, V],
        scratch_shapes=[
            pltpu.VMEM((most, 2, side, side), F32),
            pltpu.VMEM((side, side), F32),
            pltpu.SemaphoreType.DMA((most + 1,)),
            pltpu.VMEM((3, big, big), F32)],
        compiler_params=pltpu.CompilerParams(vmem_limit_bytes=46 * 2**20),
        name="place",
    )(items, placed)


def finish_kernel(obj_ref, got_ref, out_hbm, grad_hbm, wide, sem):
    n = got_ref.shape[2]
    whole = pltpu.make_async_copy(obj_ref, out_hbm, sem.at[4])
    whole.start()
    parts = []
    for k in range(4):
        c, at = k // 2, (k % 2) * (n // 2)
        rows_k = pl.ds(k * (n // 2), n // 2)
        for h in range(2):
            wide[rows_k, 128 * h:128 * (h + 1)] = got_ref[c, h, at:at + n // 2].astype(F32)
        part = pltpu.make_async_copy(wide.at[rows_k], grad_hbm.at[rows_k], sem.at[k])
        part.start()
        parts.append(part)
    for part in parts:
        part.wait()
    whole.wait()


def finish_call(obj, got):
    n = got.shape[2]
    V = pl.BlockSpec(memory_space=pltpu.VMEM)
    A = pl.BlockSpec(memory_space=pltpu.HBM)
    return pl.pallas_call(
        finish_kernel,
        out_shape=[jax.ShapeDtypeStruct(obj.shape, F32), jax.ShapeDtypeStruct((2 * n, 256), F32)],
        in_specs=[V, V],
        out_specs=[A, A],
        scratch_shapes=[pltpu.VMEM((2 * n, 256), F32), pltpu.SemaphoreType.DMA((5,))],
        compiler_params=pltpu.CompilerParams(vmem_limit_bytes=16 * 2**20),
        name="finish",
    )(obj, got)


def on_device(object_field, probe, amplitudes, owner, offsets):
    rows, cols = lax.axis_size("row"), lax.axis_size("col")
    held = amplitudes.shape[0]
    most = 4 * (held - 1)
    side, tile = probe.shape[-1], object_field.shape[1]
    ext, meta = pre_call(owner, offsets.T, object_field, side, rows, cols)
    patch, items = cut_call(meta, ext, tile, cols, held, most)
    placed, grad = main_call(items, owner, amplitudes, patch, probe, rows, cols)
    *rims, core = place_call(items, placed, tile)
    scale = 1.0 / math.sqrt(rows * cols * held)
    object_out, gradient = post_call(rims, core, object_field, grad, rows, cols, scale)
    object_out, gradient = finish_call(object_out, gradient)
    return (object_out, gradient.reshape(probe.shape))


def solution(mesh):
    return jax.shard_map(
        on_device,
        mesh=mesh,
        in_specs=(
            P(None, "row", "col"),
            P(),
            P(("row", "col"), None, None),
            P(("row", "col")),
            P(("row", "col"), None),
        ),
        out_specs=(P(None, "row", "col"), P()),
        check_vma=False,
    )
```

```python
import functools
import math

import jax
import jax.numpy as jnp
import numpy as np
from jax import lax
from jax.experimental import pallas as pl
from jax.experimental.pallas import tpu as pltpu
from jax.sharding import PartitionSpec as P

F32, BF16 = jnp.float32, jnp.bfloat16
MESH = pl.DeviceIdType.MESH

def tables(side):
    series = np.arange(side, dtype=np.int32)
    angles = (series[:, None] * series[None, :] % side).astype(np.float32) * np.float32(2.0 * math.pi / side)
    factor = np.float32(1.0 / math.sqrt(side))
    re = jnp.asarray(np.cos(angles) * factor).astype(BF16)
    im = jnp.asarray(-np.sin(angles) * factor).astype(BF16)
    return re, im

def dot(a, b):
    return jnp.dot(a, b, preferred_element_type=F32)

def moved_back(w, rows, lanes):
    tall, wide = w.shape
    t = pltpu.roll(w.reshape(tall // 8, 8, wide), lax.rem(8 - rows, 8), 1)
    sub = lax.broadcasted_iota(jnp.int32, (tall // 8 - 1, 8, wide), 1)
    w = jnp.where(sub < 8 - rows, t[:-1], t[1:]).reshape(tall - 8, wide)
    lane = lax.broadcasted_iota(jnp.int32, (tall - 8, 128), 1)
    parts = [pltpu.roll(w[:, k:k + 128], lax.rem(128 - lanes, 128), 1) for k in range(0, wide, 128)]
    return jnp.concatenate([jnp.where(lane < 128 - lanes, a, b) for a, b in zip(parts[:-1], parts[1:])], 1)


def moved_on(w, rows, lanes):
    tall, wide = w.shape
    lane = lax.broadcasted_iota(jnp.int32, (tall, 128), 1)
    none = jnp.zeros((tall, 128), F32)
    parts = [none] + [pltpu.roll(w[:, k:k + 128], lanes, 1) for k in range(0, wide, 128)] + [none]
    w = jnp.concatenate([jnp.where(lane < lanes, a, b) for a, b in zip(parts[:-1], parts[1:])], 1)
    wide += 128
    t = pltpu.roll(w.reshape(tall // 8, 8, wide), rows, 1)
    none = jnp.zeros((1, 8, wide), F32)
    sub = lax.broadcasted_iota(jnp.int32, (tall // 8 + 1, 8, wide), 1)
    both = jnp.where(sub < rows, jnp.concatenate([none, t], 0), jnp.concatenate([t, none], 0))
    return both.reshape(tall + 8, wide)


def around(row, col, dr, dc, rows, cols):
    return lax.rem(row + dr + rows, rows), lax.rem(col + dc + cols, cols)


NEAR = [(dr, dc) for dr in (-1, 0, 1) for dc in (-1, 0, 1) if (dr, dc) != (0, 0)]


def span(step, tile, half):
    return {-1: (0, half), 0: (half, tile), 1: (half + tile, half)}[step]


def landing(step, tile, half):
    return {-1: (tile - half, half), 0: (0, tile), 1: (0, half)}[step]


def column_peers(row, col, cols):
    depth = 4
    steps = [(2, 1), (1, 2), (2, 3), (3, 2), (2, 2), (1, 1), (3, 3), (1, 3), (3, 1), (2, 0), (0, 2), (0, 1), (1, 0), (0, 3), (3, 0)]
    x, z = col // depth, lax.rem(col, depth)
    return [(row, lax.rem(x + dx, cols // depth) * depth + lax.rem(z + dz, depth)) for dx, dz in steps]


LEAD = 16


def power_of(x):
    top = jnp.max(jnp.abs(x), axis=0, keepdims=True)
    return jnp.floor(jnp.log2(jnp.maximum(top, 1e-30)))


def code(out, x, power=None):
    power = power_of(x) if power is None else power
    out[:LEAD] = jnp.broadcast_to(power, (LEAD, x.shape[1])).astype(jnp.int32).astype(jnp.int16)
    x = jnp.clip(jnp.round(x * jnp.exp2(14.0 - power)), -32767.0, 32767.0)
    out[LEAD:] = x.astype(jnp.int32).astype(jnp.int16)


def decoded(ref):
    power = ref[:LEAD].astype(jnp.int32).astype(F32)[:1]
    return ref[LEAD:].astype(jnp.int32).astype(F32) * jnp.exp2(power - 14.0)


def code_pieces(out, ref):
    power = power_of(ref[...])
    size = ref.shape[0] // out.shape[0]
    for k in range(out.shape[0]):
        code(out.at[k], ref[k * size:(k + 1) * size], power)


def owned_by(to, owner_ref, held):
    which = jnp.int32(0)
    for h in range(1, held):
        which = jnp.where(owner_ref[h] == to, h, which)
    return which


class Sends:
    def __init__(self, send_sem, recv_sem):
        self.send_sem, self.recv_sem, self.at, self.all = send_sem, recv_sem, 0, []

    def __call__(self, src, dst, device):
        n = self.at
        self.at += 1
        copy = pltpu.make_async_remote_copy(
            src_ref=src, dst_ref=dst, send_sem=self.send_sem.at[n], recv_sem=self.recv_sem.at[n],
            device_id=device, device_id_type=MESH)
        copy.start()
        self.all.append(copy)
        return copy

    def finish(self):
        for copy in self.all:
            copy.wait_send()


def arrive(devices):
    barrier = pltpu.get_barrier_semaphore()
    for device in devices:
        pl.semaphore_signal(barrier, inc=1, device_id=device, device_id_type=MESH)


def greeted(devices):
    pl.semaphore_wait(pltpu.get_barrier_semaphore(), len(devices))


def post_kernel(rows, cols, tile, half, scale, rows_ref, cols_ref, corners_ref, core_ref, obj_ref, grad_ref, out_ref, all16,
                wsum, rim_rows, rim_cols, rim_corners, mate, sum_a, sum_b, got_a, got_b, part_a, part_b, got_a2, got_b2,
                code_a, code_b, gsend, grecv):
    row, col = lax.axis_index("row"), lax.axis_index("col")
    core, y = lax.rem(row, 2), row // 2
    ys = rows // 2
    other = (row + 1 - 2 * core, col)
    y_peers = [(lax.rem(y + s, ys) * 2 + core, col) for s in range(1, ys)]
    c_peers = column_peers(row, col, cols)
    near = [around(row, col, dr, dc, rows, cols) for dr, dc in NEAR]
    peers = [other] + y_peers + c_peers + near
    arrive(peers)
    greeted(peers)
    send = Sends(gsend, grecv)
    n = grad_ref.shape[0] // 2
    na, nb = n // ys, n // cols
    fin = n // (ys * cols)
    theirs = pl.ds(pl.multiple_of((1 - core) * n, n), n)
    mine = pl.ds(pl.multiple_of(core * n, n), n)
    pair = [send(grad_ref.at[theirs, k:k + 128], mate.at[:, k:k + 128], other) for k in (0, 128)]
    rim_copies = []

    def place(i, by_rows, by_cols, at_corners):
        dr, dc = NEAR[i]
        if dc == 0:
            return by_rows.at[(dr + 1) // 2]
        if dr == 0:
            return by_cols.at[(dc + 1) // 2]
        return at_corners.at[dr + 1 + (dc + 1) // 2]

    def landed(i):
        return place(i, rim_rows, rim_cols, rim_corners)

    def send_rims(which):
        for i in which:
            rim_copies.append(send(place(i, rows_ref, cols_ref, corners_ref), landed(i), near[i]))

    send_rims([1, 6, 3, 4])
    y_at = [lax.rem(y + s, ys) for s in range(1, ys)]
    c_at = [peer[1] for peer in c_peers]
    pair[0].wait_recv()
    sum_a[...] = grad_ref[mine, :128] + mate[:, :128]
    code_pieces(code_a, sum_a)
    def piece(k, size):
        return pl.ds(pl.multiple_of(k * size, size), size)

    a1 = [send(code_a.at[y_at[s]], got_a.at[s], y_peers[s]) for s in range(ys - 1)]
    pair[1].wait_recv()
    sum_b[...] = grad_ref[mine, 128:] + mate[:, 128:]
    code_pieces(code_b, sum_b)
    b1 = [send(code_b.at[c_at[s]], got_b.at[s], c_peers[s]) for s in range(cols - 1)]
    for c in a1:
        c.wait_recv()
    tot = sum_a[piece(y, na), :]
    for s in range(ys - 1):
        tot += decoded(got_a.at[s])
    part_a[...] = tot
    a2 = [send(part_a.at[piece(c_at[s], fin)], got_a2.at[s], c_peers[s]) for s in range(cols - 1)]
    for c in b1:
        c.wait_recv()
    tot = sum_b[piece(col, nb), :]
    for s in range(cols - 1):
        tot += decoded(got_b.at[s])
    part_b[...] = tot
    b2 = [send(part_b.at[piece(y_at[s], fin)], got_b2.at[s], y_peers[s]) for s in range(ys - 1)]
    send_rims([0, 2, 5, 7])
    for c in a2:
        c.wait_recv()
    tot = part_a[piece(col, fin), :]
    for s in range(cols - 1):
        tot += got_a2[s]
    at_a = piece(y * cols + col, fin)
    all16[core, 0, at_a, :] = (tot * scale).astype(all16.dtype)
    a3 = [send(all16.at[core, 0, at_a], all16.at[core, 0, at_a], p) for p in c_peers]
    for c in b2:
        c.wait_recv()
    tot = part_b[piece(y, fin), :]
    for s in range(ys - 1):
        tot += got_b2[s]
    at_b = piece(col * ys + y, fin)
    all16[core, 1, at_b, :] = (tot * scale).astype(all16.dtype)
    b3 = [send(all16.at[core, 1, at_b], all16.at[core, 1, at_b], p) for p in y_peers]
    for c in a3:
        c.wait_recv()
    big_a = piece(y, na)
    a4 = [send(all16.at[core, 0, big_a], all16.at[core, 0, big_a], p) for p in y_peers]
    for c in b3:
        c.wait_recv()
    big_b = piece(col, nb)
    b4 = [send(all16.at[core, 1, big_b], all16.at[core, 1, big_b], p) for p in c_peers]
    last = []
    for k, copies in enumerate((a4, b4)):
        for c in copies:
            c.wait_recv()
        last.append(send(all16.at[core, k], all16.at[core, k], other))
    for c in rim_copies:
        c.wait_recv()
    out_ref[...] = core_ref[0:2]
    wsum[...] = core_ref[2]
    for i, (dr, dc) in enumerate(NEAR):
        r0, rl = landing(dr, tile, half)
        c0, cl = landing(dc, tile, half)
        keep = (row != -1) & (col != -1)
        if dr:
            keep = keep & (row != (0 if dr == 1 else rows - 1))
        if dc:
            keep = keep & (col != (0 if dc == 1 else cols - 1))

        @pl.when(keep)
        def _(i=i, r0=r0, rl=rl, c0=c0, cl=cl):
            for q in range(2):
                out_ref[q, r0:r0 + rl, c0:c0 + cl] += landed(i)[q].astype(F32)
            wsum[r0:r0 + rl, c0:c0 + cl] += landed(i)[2].astype(F32)

    for q in range(2):
        out_ref[q] = obj_ref[q] + out_ref[q] / (wsum[...] + 1.0)
    for c in last:
        c.wait_recv()
    send.finish()


def post_call(rims, core, obj, grad, rows, cols, scale):
    tile, half = obj.shape[1], rims[0].shape[2]
    total = grad.shape[0]
    ys, n = rows // 2, total // 2
    na, nb, fin = n // ys, n // cols, n // (ys * cols)
    copies = 2 + 8 + 4 * (ys - 1) + 4 * (cols - 1) + 2
    V = pl.BlockSpec(memory_space=pltpu.VMEM)
    return pl.pallas_call(
        functools.partial(post_kernel, rows, cols, tile, half, scale),
        out_shape=[jax.ShapeDtypeStruct(obj.shape, F32), jax.ShapeDtypeStruct((2, 2, n, 128), BF16)],
        in_specs=[V] * 6,
        out_specs=[V, V],
        scratch_shapes=[
            pltpu.VMEM((tile, tile), F32),
            pltpu.VMEM((2, 3, half, tile), BF16),
            pltpu.VMEM((2, 3, tile, half), BF16),
            pltpu.VMEM((4, 3, half, half), BF16),
            pltpu.VMEM((n, 256), F32),
            pltpu.VMEM((n, 128), F32),
            pltpu.VMEM((n, 128), F32),
            pltpu.VMEM((ys - 1, LEAD + na, 128), jnp.int16),
            pltpu.VMEM((cols - 1, LEAD + nb, 128), jnp.int16),
            pltpu.VMEM((na, 128), F32),
            pltpu.VMEM((nb, 128), F32),
            pltpu.VMEM((cols - 1, fin, 128), F32),
            pltpu.VMEM((ys - 1, fin, 128), F32),
            pltpu.VMEM((ys, LEAD + na, 128), jnp.int16),
            pltpu.VMEM((cols, LEAD + nb, 128), jnp.int16),
            pltpu.SemaphoreType.DMA((copies,)),
            pltpu.SemaphoreType.DMA((copies,)),
        ],
        compiler_params=pltpu.CompilerParams(collective_id=1, has_side_effects=True, vmem_limit_bytes=40 * 2**20),
        name="post",
    )(*rims, core, obj, grad)


def pre_kernel(rows, cols, tile, half, owner_ref, offsets_ref, obj_ref, ext_ref, meta_ref,
               mine, out_rows, out_cols, in_rows, in_cols, in_corners, gsend, grecv, lsem):
    row, col = lax.axis_index("row"), lax.axis_index("col")
    near = [around(row, col, dr, dc, rows, cols) for dr, dc in NEAR]
    c_peers = column_peers(row, col, cols)
    held = owner_ref.shape[0]
    core = pltpu.make_async_copy(obj_ref, ext_ref.at[:, half:half + tile, half:half + tile], lsem.at[0])
    core.start()
    arrive(c_peers + near)
    lane = lax.broadcasted_iota(jnp.int32, (1, 128), 1)
    note = jnp.zeros((1, 128), jnp.int32)
    for h in range(held):
        note = jnp.where(lane == h, owner_ref[h], note)
        for k in range(2):
            note = jnp.where(lane == held + 2 * h + k, offsets_ref[k, h], note)
    mine[...] = note
    core.wait()
    end = half + tile
    for q in range(2):
        for k, at in enumerate((half, end - half)):
            code(out_rows.at[k, q], ext_ref[q, at:at + half, half:end])
            code(out_cols.at[k, q], ext_ref[q, half:end, at:at + half])
    greeted(c_peers + near)
    send = Sends(gsend, grecv)
    got = []

    def edge(dr, dc):
        if dc == 0:
            return out_rows.at[(dr + 1) // 2]
        if dr == 0:
            return out_cols.at[(dc + 1) // 2]
        at = 0 if dc < 0 else tile - half
        return out_rows.at[(dr + 1) // 2, :, :, at:at + half]

    def landed(dr, dc):
        if dc == 0:
            return in_rows.at[(dr + 1) // 2]
        if dr == 0:
            return in_cols.at[(dc + 1) // 2]
        return in_corners.at[dr + 1 + (dc + 1) // 2]

    for i, (dr, dc) in enumerate(NEAR):
        got.append(send(edge(dr, dc), landed(dr, dc), near[i]))
    for s in range(cols - 1):
        got.append(send(mine, meta_ref.at[col], c_peers[s]))
    own = pltpu.make_async_copy(mine, meta_ref.at[col], lsem.at[1])
    own.start()
    for c in got:
        c.wait_recv()
    own.wait()
    for dr, dc in NEAR:
        tr, rl = span(-dr, tile, half)
        tc, cl = span(-dc, tile, half)
        ref = landed(dr, dc)
        for q in range(2):
            ext_ref[q, tr:tr + rl, tc:tc + cl] = decoded(ref.at[q])
    send.finish()
    big = tile + 2 * half

    @pl.when(row == 0)
    def _():
        ext_ref[:, :half, :] = jnp.zeros((2, half, big), F32)

    @pl.when(row == rows - 1)
    def _():
        ext_ref[:, big - half:, :] = jnp.zeros((2, half, big), F32)

    @pl.when(col == 0)
    def _():
        ext_ref[:, :, :half] = jnp.zeros((2, big, half), F32)

    @pl.when(col == cols - 1)
    def _():
        ext_ref[:, :, big - half:] = jnp.zeros((2, big, half), F32)


def pre_call(owner, offsets, obj, side, rows, cols):
    tile, half = obj.shape[1], side // 2
    big = tile + side
    copies = 8 + cols - 1
    V = pl.BlockSpec(memory_space=pltpu.VMEM)
    S = pl.BlockSpec(memory_space=pltpu.SMEM)
    return pl.pallas_call(
        functools.partial(pre_kernel, rows, cols, tile, half),
        out_shape=[jax.ShapeDtypeStruct((2, big, big), F32), jax.ShapeDtypeStruct((cols, 1, 128), jnp.int32)],
        in_specs=[S, S, pl.BlockSpec(memory_space=pltpu.HBM)],
        out_specs=[V, V],
        scratch_shapes=[
            pltpu.VMEM((1, 128), jnp.int32),
            pltpu.VMEM((2, 2, half + LEAD, tile), jnp.int16),
            pltpu.VMEM((2, 2, tile + LEAD, half), jnp.int16),
            pltpu.VMEM((2, 2, half + LEAD, tile), jnp.int16),
            pltpu.VMEM((2, 2, tile + LEAD, half), jnp.int16),
            pltpu.VMEM((4, 2, half + LEAD, half), jnp.int16),
            pltpu.SemaphoreType.DMA((copies,)),
            pltpu.SemaphoreType.DMA((copies,)),
            pltpu.SemaphoreType.DMA((2,)),
        ],
        compiler_params=pltpu.CompilerParams(collective_id=0, has_side_effects=True, vmem_limit_bytes=32 * 2**20),
        name="pre",
    )(owner, offsets, obj)


def cut_kernel(cols, half, held, meta_ref, ext, patch_hbm, list_ref, patch, osem):
    col = lax.axis_index("col")
    side = 2 * half
    tall, wide, most = side + 8, side + 128, list_ref.shape[0]

    def clear(p, carry):
        for k in range(8):
            list_ref[p, k] = 0
        return carry

    lax.fori_loop(0, most, clear, 0)

    def scan(s, count):
        live, r, c = jnp.int32(0), jnp.int32(0), jnp.int32(0)
        for h in range(held):
            hit = meta_ref[s, 0, h] == col
            live = jnp.where(hit, 1, live)
            r = jnp.where(hit, meta_ref[s, 0, held + 2 * h], r)
            c = jnp.where(hit, meta_ref[s, 0, held + 2 * h + 1], c)

        @pl.when((live == 1) & (count < most))
        def _():
            list_ref[count, 0] = 1
            list_ref[count, 1] = s
            list_ref[count, 2] = r // 8
            list_ref[count, 3] = lax.rem(r, 8)
            list_ref[count, 4] = c // 128
            list_ref[count, 5] = lax.rem(c, 128)
        return count + live

    lax.fori_loop(0, cols, scan, 0)

    def out(p):
        return pltpu.make_async_copy(patch.at[p], patch_hbm.at[p], osem.at[p])

    def visit(p, carry):
        @pl.when(list_ref[p, 0] == 1)
        def _():
            r0 = pl.multiple_of(list_ref[p, 2] * 8, 8)
            c0 = pl.multiple_of(list_ref[p, 4] * 128, 128)
            for q in range(2):
                w = ext[q, pl.ds(r0, tall), pl.ds(c0, wide)]
                patch[p, q] = moved_back(w, list_ref[p, 3], list_ref[p, 5])

        @pl.when(list_ref[p, 0] == 0)
        def _():
            patch[p] = jnp.zeros((2, side, side), F32)

        out(p).start()
        return carry

    lax.fori_loop(0, most, visit, 0)

    def drain(p, carry):
        out(p).wait()
        return carry

    lax.fori_loop(0, most, drain, 0)


def cut_call(meta, ext, tile, cols, held, most):
    big = ext.shape[1]
    side = big - tile
    A = pl.BlockSpec(memory_space=pltpu.HBM)
    S = pl.BlockSpec(memory_space=pltpu.SMEM)
    return pl.pallas_call(
        functools.partial(cut_kernel, cols, side // 2, held),
        out_shape=[jax.ShapeDtypeStruct((most, 2, side, side), F32), jax.ShapeDtypeStruct((most, 8), jnp.int32)],
        in_specs=[S, pl.BlockSpec(memory_space=pltpu.VMEM)],
        out_specs=[A, S],
        scratch_shapes=[
            pltpu.VMEM((most, 2, side, side), F32),
            pltpu.SemaphoreType.DMA((most,)),
        ],
        compiler_params=pltpu.CompilerParams(vmem_limit_bytes=47 * 2**20),
        name="cut",
    )(meta, ext)


def main_kernel(rows, cols, list_ref, owner_ref, amp_hbm, patch_hbm, probe_hbm, tab_hbm,
                placed_hbm, grad_ref,
                placed_ref, pow_ref, psem, slots, amps, amp, probe, tab, patch, far, total, ratio, ebuf, hbuf, ssum,
                gsend, grecv, lsem):
    row, col = lax.axis_index("row"), lax.axis_index("col")
    c_peers = column_peers(row, col, cols)
    held, side, modes, most = amp.shape[0], amp.shape[1], probe.shape[0], patch.shape[0]
    local = [
        pltpu.make_async_copy(amp_hbm, amp, lsem.at[0]),
        pltpu.make_async_copy(probe_hbm, probe, lsem.at[1]),
        pltpu.make_async_copy(tab_hbm, tab, lsem.at[2]),
        pltpu.make_async_copy(patch_hbm, patch, lsem.at[3]),
    ]
    for copy in local:
        copy.start()
    arrive(c_peers)
    send = Sends(gsend, grecv)
    local[0].wait()
    for k, peer in enumerate(c_peers):
        slots[k] = amp[owned_by(peer[1], owner_ref, held)]
    amps[col] = amp[owned_by(col, owner_ref, held)]
    greeted(c_peers)
    amp_copies = []
    for h in range(2):
        part = pl.ds(h * (side // 2), side // 2)
        for k, peer in enumerate(c_peers):
            amp_copies.append(send(slots.at[k, part], amps.at[col, part], peer))
    local[1].wait()
    power = jnp.zeros((side, side), F32)
    for m in range(modes):
        power += probe[m, 0] * probe[m, 0] + probe[m, 1] * probe[m, 1]
    pow_ref[...] = power
    weight = pltpu.make_async_copy(pow_ref, placed_hbm.at[most, 0], psem.at[most])
    weight.start()
    grad_ref[...] = jnp.zeros_like(grad_ref)
    ssum[...] = jnp.zeros_like(ssum)
    local[2].wait()
    local[3].wait()

    chunk = hbuf.shape[2] // modes
    chunks = side // chunk

    def left_pass(k, fields, halves):
        for m in range(modes):
            for h in range(2):
                part = dot(tab[k, h * side:(h + 1) * side], fields[m])
                for c in range(chunks):
                    rows_c = slice(c * chunk, (c + 1) * chunk)
                    halves[c, m * chunk:(m + 1) * chunk, h * side:(h + 1) * side] = part[rows_c].astype(BF16)

    def there(p, fields, halves):
        ssum[...] += patch[p, 0] * patch[p, 0] + patch[p, 1] * patch[p, 1]
        for m in range(modes):
            pr, pi = probe[m, 0], probe[m, 1]
            xr, xi = patch[p, 0], patch[p, 1]
            fields[m, :side] = (pr * xr - pi * xi).astype(BF16)
            fields[m, side:] = (pr * xi + pi * xr).astype(BF16)
        left_pass(0, fields, halves)
        for c in range(chunks):
            rows_c = slice(c * chunk, (c + 1) * chunk)
            out = dot(halves[c], tab[1])
            tot = jnp.zeros((chunk, side), F32)
            for m in range(modes):
                one = out[m * chunk:(m + 1) * chunk]
                far[p, m, rows_c] = one
                tot += one[:, :side] * one[:, :side] + one[:, side:] * one[:, side:]
            total[p, rows_c] = lax.rsqrt(jnp.maximum(tot, 0.25))

    def there_two(k, carry):
        for u in range(2):
            there(2 * k + u, ebuf.at[u], hbuf.at[u])
        return carry

    lax.fori_loop(0, most // 2, there_two, 0)
    for p in range(most - most % 2, most):
        there(p, ebuf.at[0], hbuf.at[0])
    for copy in amp_copies:
        copy.wait_recv()

    def out(p):
        return pltpu.make_async_copy(placed_ref.at[p], placed_hbm.at[p], psem.at[p])

    def drain(p, carry):
        out(p).wait()
        return carry

    def back(p, carry):
        fields, halves = ebuf.at[0], hbuf.at[0]
        ratio[...] = amps[list_ref[p, 1]].astype(F32) * total[p]
        for m in range(modes):
            fields[m, :side] = (far[p, m, :, :side] * ratio[...]).astype(BF16)
            fields[m, side:] = (far[p, m, :, side:] * ratio[...]).astype(BF16)
        left_pass(2, fields, halves)
        for c in range(chunks):
            rows_c = slice(c * chunk, (c + 1) * chunk)
            ret = dot(halves[c], tab[3])
            xr, xi = patch[p, 0, rows_c], patch[p, 1, rows_c]
            nr, ni = -xr * pow_ref[rows_c], -xi * pow_ref[rows_c]
            for m in range(modes):
                one = ret[m * chunk:(m + 1) * chunk]
                rr, ri = one[:, :side], one[:, side:]
                pr, pi = probe[m, 0, rows_c], probe[m, 1, rows_c]
                nr += pr * rr + pi * ri
                ni += pr * ri - pi * rr
                at_r = 2 * m * side + c * chunk
                at_i = at_r + side
                grad_ref[at_r:at_r + chunk] += xr * rr + xi * ri
                grad_ref[at_i:at_i + chunk] += xr * ri - xi * rr
            placed_ref[p, 0, rows_c] = nr
            placed_ref[p, 1, rows_c] = ni
        out(p).start()
        return carry

    lax.fori_loop(0, most, back, 0)
    for m in range(modes):
        for q in range(2):
            grad_ref[(2 * m + q) * side:(2 * m + q + 1) * side] -= probe[m, q] * ssum[...]
    lax.fori_loop(0, most, drain, 0)
    weight.wait()
    send.finish()


def main_call(items, owner, amp, patch, probe, rows, cols):
    side, modes, most = amp.shape[1], probe.shape[0], patch.shape[0]
    copies = 2 * (cols - 1)
    tr, ti = tables(side)

    def left(a, b):
        return jnp.concatenate([jnp.concatenate([a, -b], 1), jnp.concatenate([b, a], 1)], 0)

    def right(a, b):
        return jnp.concatenate([jnp.concatenate([a, b], 1), jnp.concatenate([-b, a], 1)], 0)

    tab = jnp.stack([left(tr, ti), right(tr, ti), left(tr, -ti), right(tr, -ti)])
    V = pl.BlockSpec(memory_space=pltpu.VMEM)
    A = pl.BlockSpec(memory_space=pltpu.HBM)
    S = pl.BlockSpec(memory_space=pltpu.SMEM)
    return pl.pallas_call(
        functools.partial(main_kernel, rows, cols),
        out_shape=[
            jax.ShapeDtypeStruct((most + 1, 2, side, side), F32),
            jax.ShapeDtypeStruct((modes * 2 * side, side), F32),
        ],
        in_specs=[S, S, A, A, A, A],
        out_specs=[A, V],
        scratch_shapes=[
            pltpu.VMEM((most, 2, side, side), F32),
            pltpu.VMEM((side, side), F32),
            pltpu.SemaphoreType.DMA((most + 1,)),
            pltpu.VMEM((cols - 1, side, side), BF16),
            pltpu.VMEM((cols, side, side), BF16),
            pltpu.VMEM(amp.shape, BF16),
            pltpu.VMEM(probe.shape, F32),
            pltpu.VMEM(tab.shape, BF16),
            pltpu.VMEM((most, 2, side, side), F32),
            pltpu.VMEM((most, modes, side, 2 * side), F32),
            pltpu.VMEM((most, side, side), F32),
            pltpu.VMEM((side, side), F32),
            pltpu.VMEM((2, modes, 2 * side, side), BF16),
            pltpu.VMEM((2, 4, modes * side // 4, 2 * side), BF16),
            pltpu.VMEM((side, side), F32),
            pltpu.SemaphoreType.DMA((copies,)),
            pltpu.SemaphoreType.DMA((copies,)),
            pltpu.SemaphoreType.DMA((4,)),
        ],
        compiler_params=pltpu.CompilerParams(collective_id=2, has_side_effects=True, vmem_limit_bytes=62 * 2**20),
        name="main",
    )(items, owner, amp, patch, probe, tab)


def place_kernel(tile, half, list_ref, placed_hbm, rows_ref, cols_ref, corners_ref, core_ref, placed_ref, pow_ref, psem, num):
    side = 2 * half
    big, tall, wide = tile + side, side + 8, side + 128

    def fetch(p):
        return pltpu.make_async_copy(placed_hbm.at[p], placed_ref.at[p], psem.at[p])

    def start(p, carry):
        fetch(p).start()
        return carry

    most = list_ref.shape[0]
    weight = pltpu.make_async_copy(placed_hbm.at[most, 0], pow_ref, psem.at[most])
    weight.start()
    lax.fori_loop(0, most, start, 0)
    num[...] = jnp.zeros_like(num)
    weight.wait()

    def visit(p, carry):
        fetch(p).wait()

        @pl.when(list_ref[p, 0] == 1)
        def _():
            r0 = pl.multiple_of(list_ref[p, 2] * 8, 8)
            c0 = pl.multiple_of(list_ref[p, 4] * 128, 128)
            for q in range(3):
                w = moved_on(placed_ref[p, q] if q < 2 else pow_ref[...], list_ref[p, 3], list_ref[p, 5])
                num[q, pl.ds(r0, tall), pl.ds(c0, wide)] += w
        return carry

    lax.fori_loop(0, list_ref.shape[0], visit, 0)
    for q in range(3):
        for dr, dc in NEAR:
            r0, rl = span(dr, tile, half)
            c0, cl = span(dc, tile, half)
            rim = num[q, r0:r0 + rl, c0:c0 + cl].astype(BF16)
            if dc == 0:
                rows_ref[(dr + 1) // 2, q] = rim
            elif dr == 0:
                cols_ref[(dc + 1) // 2, q] = rim
            else:
                corners_ref[dr + 1 + (dc + 1) // 2, q] = rim
        core_ref[q] = num[q, half:big - half, half:big - half]


def place_call(items, placed, tile):
    most, side = items.shape[0], placed.shape[-1]
    half = side // 2
    big = tile + side
    V = pl.BlockSpec(memory_space=pltpu.VMEM)
    S = pl.BlockSpec(memory_space=pltpu.SMEM)
    return pl.pallas_call(
        functools.partial(place_kernel, tile, half),
        out_shape=[
            jax.ShapeDtypeStruct((2, 3, half, tile), BF16),
            jax.ShapeDtypeStruct((2, 3, tile, half), BF16),
            jax.ShapeDtypeStruct((4, 3, half, half), BF16),
            jax.ShapeDtypeStruct((3, tile, tile), F32)],
        in_specs=[S, pl.BlockSpec(memory_space=pltpu.HBM)],
        out_specs=[V, V, V, V],
        scratch_shapes=[
            pltpu.VMEM((most, 2, side, side), F32),
            pltpu.VMEM((side, side), F32),
            pltpu.SemaphoreType.DMA((most + 1,)),
            pltpu.VMEM((3, big, big), F32)],
        compiler_params=pltpu.CompilerParams(vmem_limit_bytes=46 * 2**20),
        name="place",
    )(items, placed)


def finish_kernel(obj_ref, got_ref, out_hbm, grad_hbm, wide, sem):
    n = got_ref.shape[2]
    whole = pltpu.make_async_copy(obj_ref, out_hbm, sem.at[4])
    whole.start()
    parts = []
    for k in range(4):
        c, at = k // 2, (k % 2) * (n // 2)
        rows_k = pl.ds(k * (n // 2), n // 2)
        for h in range(2):
            wide[rows_k, 128 * h:128 * (h + 1)] = got_ref[c, h, at:at + n // 2].astype(F32)
        part = pltpu.make_async_copy(wide.at[rows_k], grad_hbm.at[rows_k], sem.at[k])
        part.start()
        parts.append(part)
    for part in parts:
        part.wait()
    whole.wait()


def finish_call(obj, got):
    n = got.shape[2]
    V = pl.BlockSpec(memory_space=pltpu.VMEM)
    A = pl.BlockSpec(memory_space=pltpu.HBM)
    return pl.pallas_call(
        finish_kernel,
        out_shape=[jax.ShapeDtypeStruct(obj.shape, F32), jax.ShapeDtypeStruct((2 * n, 256), F32)],
        in_specs=[V, V],
        out_specs=[A, A],
        scratch_shapes=[pltpu.VMEM((2 * n, 256), F32), pltpu.SemaphoreType.DMA((5,))],
        compiler_params=pltpu.CompilerParams(vmem_limit_bytes=16 * 2**20),
        name="finish",
    )(obj, got)


def on_device(object_field, probe, amplitudes, owner, offsets):
    rows, cols = lax.axis_size("row"), lax.axis_size("col")
    held = amplitudes.shape[0]
    most = 4 * (held - 1)
    side, tile = probe.shape[-1], object_field.shape[1]
    ext, meta = pre_call(owner, offsets.T, object_field, side, rows, cols)
    patch, items = cut_call(meta, ext, tile, cols, held, most)
    placed, grad = main_call(items, owner, amplitudes, patch, probe, rows, cols)
    *rims, core = place_call(items, placed, tile)
    scale = 1.0 / math.sqrt(rows * cols * held)
    object_out, gradient = post_call(rims, core, object_field, grad, rows, cols, scale)
    object_out, gradient = finish_call(object_out, gradient)
    return (object_out, gradient.reshape(probe.shape))


def solution(mesh):
    return jax.shard_map(
        on_device,
        mesh=mesh,
        in_specs=(
            P(None, "row", "col"),
            P(),
            P(("row", "col"), None, None),
            P(("row", "col")),
            P(("row", "col"), None),
        ),
        out_specs=(P(None, "row", "col"), P()),
        check_vma=False,
    )
```
